32 devices in a mesh: ia: 8 (over z, core), ka: 4 (over y, x).
Axes of the slice: x: 2, y: 2, z: 4, core: 2. Of those that a mesh axis runs over, the one named last changes fastest.
Arguments:
- amplitudes: float32 [8, 8, 1024, 1024], P('ia', 'ka'), may hold values from -3 to 3
- integrals: bfloat16 [8, 2, 8, 1024, 1024], P('ia', None, 'ka'), may hold values from -0.0625 to 0.0625
- tile_mask: int32 [8, 2, 8, 8, 8], P('ia', None, 'ka'), may hold values from 0 to 1, as said below
- pair_list: int32 [8, 2], replicated, may hold values from 0 to 7, as said below
Outputs:
- residual: float32 [8, 2, 1024, 1024], P('ia', None, 'ka')
The draws below stay inside these ranges and needn't reach their ends.
Inputs may be any that keep to these rules, and one draw needn't show every extreme that they name: `tile_mask`: 1 marks a filled 128 x 128 tile of an integral block, 0 an empty one. `pair_list`: row i names two different occupied indices, neither equal to i; j stands in row i exactly when i stands in row j.
All inputs are finite; a program needn't handle non-finite values.
Results may differ from the reference program's by a relative error of at most 0.0003.
Values sent between devices are 32-bit elements; how exact they have to be, the bound alone decides.
No kernel may reach another device: no remote copies, remote signals or barrier semaphores. Data moves between devices by JAX's collectives and lax.ppermute only.
A program may use at most 192 MiB of HBM per device.

```python
import jax
import jax.numpy as jnp
from jax import lax

V = 1024
VT = 128
NT = 8
NO = 8


def draw_tile_mask(key, part):
    level_key = jax.random.fold_in(key, 11)
    tile_key = jax.random.fold_in(key, 23)
    level = jax.random.randint(level_key, (NO, 2, NO, 1, 1), 4, 9)
    tiles = jax.random.randint(tile_key, (NO, 2, NO, NT, NT), 0, 8)
    return (tiles < level).astype(jnp.int32)


def draw_pair_list(key, part):
    order = jax.random.permutation(jax.random.fold_in(key, 5), NO).astype(jnp.int32)
    before = jnp.roll(order, 1)
    after = jnp.roll(order, -1)
    pairs = jnp.stack([before, after], axis=1)
    return jnp.zeros((NO, 2), jnp.int32).at[order].set(pairs)


def steps_of(stream_key, extent, shards, low, largest):
    loudness, own = 1.0, jax.random.fold_in(stream_key, 6)
    for dim, blocks in shards:
        draws = jnp.exp(jax.random.uniform(jax.random.fold_in(own, dim), (blocks,), jnp.float32, low / len(shards), largest / len(shards)))
        loudness = loudness * jnp.repeat(draws, extent[dim] // blocks).reshape([-1 if axis == dim else 1 for axis in range(len(extent))])
    return loudness


def gaussian(rng, shape, width, most, split=(), kind=jnp.bfloat16):
    values = width * jax.random.normal(rng, shape, jnp.float32)
    if split:
        values = values * steps_of(rng, shape, split, -0.22, 0.18)
    return jnp.clip(values, -most, most).astype(kind)


def setup_inputs(seed: int = 0) -> dict:
    keys = jax.random.split(jax.random.key(seed), 5)
    return {
        "amplitudes": gaussian(keys[0], (NO, NO, V, V), 0.5, 3.0, ((0, 8), (1, 4)), jnp.float32),
        "integrals": gaussian(keys[1], (NO, 2, NO, V, V), (NO * V) ** -0.5, 0.0625, ((0, 8), (2, 4))),
        "tile_mask": draw_tile_mask(jax.random.fold_in(keys[4], 71), 0),
        "pair_list": draw_pair_list(jax.random.fold_in(keys[4], 71), 0),
    }


def expand_mask(tile_mask, tile_side):
    grown = jnp.repeat(jnp.repeat(tile_mask, tile_side, axis=-2), tile_side, axis=-1)
    return grown.astype(jnp.float32)


def reference(amplitudes, integrals, tile_mask, pair_list):
    def one_row(index):
        mixed = 2.0 * amplitudes[index] - jnp.swapaxes(amplitudes[:, index], 1, 2)
        masked = integrals[index].astype(jnp.float32) * expand_mask(tile_mask[index], VT)
        return jnp.einsum("kxy,skyz->sxz", mixed, masked, precision=lax.Precision.HIGHEST)

    partial_value = lax.map(one_row, jnp.arange(NO, dtype=jnp.int32))
    owners = jnp.arange(NO, dtype=jnp.int32)
    partner_slot = jnp.where(pair_list[pair_list, 0] == owners[:, None], 0, 1).astype(jnp.int32)
    return partial_value + jnp.swapaxes(partial_value[pair_list, partner_slot], 2, 3)
```

```python
import functools

import jax
import jax.numpy as jnp
from jax import lax
from jax.experimental import pallas as pl
from jax.experimental.pallas import tpu as pltpu
from jax.sharding import PartitionSpec as P

CHUNKS = 4
VMEM_BYTES = 48 * 1024 * 1024


def flip_kernel(blocks_ref, *chunk_refs):
    flipped = blocks_ref[0, 0].T
    rows = chunk_refs[0].shape[2]
    for chunk, chunk_ref in enumerate(chunk_refs):
        chunk_ref[0, 0] = flipped[chunk * rows : (chunk + 1) * rows]


def flip_chunks(amplitudes, sections, chunks):
    pairs, virtuals = amplitudes.shape[1], amplitudes.shape[3]
    wide = virtuals // sections
    rows = wide // chunks
    piece = jax.ShapeDtypeStruct((sections, pairs, rows, virtuals), jnp.float32)
    return pl.pallas_call(
        flip_kernel,
        grid=(pairs, sections),
        in_specs=[pl.BlockSpec((1, 1, virtuals, wide), lambda d, q: (0, d, 0, q))],
        out_specs=[pl.BlockSpec((1, 1, rows, virtuals), lambda d, q: (q, d, 0, 0))] * chunks,
        out_shape=[piece] * chunks,
        compiler_params=pltpu.CompilerParams(vmem_limit_bytes=VMEM_BYTES),
        cost_estimate=pl.CostEstimate(
            flops=0, bytes_accessed=2 * amplitudes.size * 4, transcendentals=0
        ),
        name="flip",
    )(amplitudes)


def mask_kernel(tiles, mask_ref, integrals_ref, masked_ref):
    side = integrals_ref.shape[-1] // tiles
    slot, pair = pl.program_id(0), pl.program_id(1)
    for r in range(tiles):
        for c in range(tiles):
            keep = mask_ref[slot, pair, r, c] != 0
            spot = (pl.ds(r * side, side), pl.ds(c * side, side))
            tile = integrals_ref[0, 0, 0, spot[0], spot[1]]
            masked_ref[0, 0, spot[0], spot[1]] = jnp.where(keep, tile, jnp.zeros_like(tile))


def mask_blocks(integrals, tile_mask):
    _, slots, pairs, virtuals, _ = integrals.shape
    return pl.pallas_call(
        functools.partial(mask_kernel, tile_mask.shape[-1]),
        grid=(slots, pairs),
        in_specs=[
            pl.BlockSpec(memory_space=pltpu.SMEM),
            pl.BlockSpec((1, 1, 1, virtuals, virtuals), lambda s, k: (0, s, k, 0, 0)),
        ],
        out_specs=pl.BlockSpec((1, 1, virtuals, virtuals), lambda s, k: (s, k, 0, 0)),
        out_shape=jax.ShapeDtypeStruct((slots, pairs, virtuals, virtuals), jnp.bfloat16),
        compiler_params=pltpu.CompilerParams(vmem_limit_bytes=VMEM_BYTES),
        cost_estimate=pl.CostEstimate(
            flops=0, bytes_accessed=2 * integrals.size * 2, transcendentals=0
        ),
        name="mask",
    )(tile_mask[0], integrals)


def product_kernel(own_ref, mirrored_ref, masked_ref, out_ref, split_ref):
    sections, pairs, rows, virtuals = mirrored_ref.shape
    tall = sections * rows

    @pl.when((pl.program_id(0) == 0) & (pl.program_id(1) == 0))
    def _():
        for q in range(sections):
            for k in range(pairs):
                mixed = 2.0 * own_ref[0, k, q, 0] - mirrored_ref[q, k]
                high = mixed.astype(jnp.bfloat16)
                low = (mixed - high.astype(jnp.float32)).astype(jnp.bfloat16)
                split_ref[k, pl.ds(q * rows, rows)] = high
                split_ref[k, pl.ds(tall + q * rows, rows)] = low

    total = None
    for k in range(pairs):
        both = jnp.dot(split_ref[k], masked_ref[0, k], preferred_element_type=jnp.float32)
        both = both[:tall] + both[tall:]
        total = both if total is None else total + both
    out_ref[:, 0] = total.reshape(sections, rows, total.shape[-1])


def product(own, mirrored, masked, chunk):
    sections, pairs, rows, virtuals = mirrored.shape
    slots = masked.shape[0]
    wide = min(virtuals, 512)
    return pl.pallas_call(
        product_kernel,
        grid=(slots, virtuals // wide),
        in_specs=[
            pl.BlockSpec(
                (1, pairs, sections, 1, rows, virtuals), lambda s, n: (0, 0, 0, chunk, 0, 0)
            ),
            pl.BlockSpec((sections, pairs, rows, virtuals), lambda s, n: (0, 0, 0, 0)),
            pl.BlockSpec((1, pairs, virtuals, wide), lambda s, n: (s, 0, 0, n)),
        ],
        out_specs=pl.BlockSpec((sections, 1, rows, wide), lambda s, n: (0, s, 0, n)),
        out_shape=jax.ShapeDtypeStruct((sections, slots, rows, virtuals), jnp.float32),
        scratch_shapes=[pltpu.VMEM((pairs, 2 * sections * rows, virtuals), jnp.bfloat16)],
        compiler_params=pltpu.CompilerParams(vmem_limit_bytes=VMEM_BYTES),
        cost_estimate=pl.CostEstimate(
            flops=4 * sections * rows * pairs * virtuals * virtuals * slots,
            bytes_accessed=masked.size * 2 + 3 * mirrored.size * 4,
            transcendentals=0,
        ),
        name="product",
    )(own, mirrored, masked)


def finish_kernel(chunks, *refs):
    own_refs, delivered_refs = refs[:chunks], refs[chunks : 2 * chunks]
    out_ref, columns_ref = refs[2 * chunks :]
    rows = own_refs[0].shape[1]
    sections = columns_ref.shape[0] // (rows * chunks)
    pieces, _, short, _ = delivered_refs[0].shape
    parts = pieces // sections
    for chunk in range(chunks):
        for q in range(sections):
            for part in range(parts):
                start = (q * chunks + chunk) * rows + part * short
                columns_ref[pl.ds(start, short)] = delivered_refs[chunk][q * parts + part, 0]
    turned = columns_ref[...].T
    for chunk in range(chunks):
        spot = slice(chunk * rows, (chunk + 1) * rows)
        out_ref[0, 0, spot] = own_refs[chunk][0] + turned[spot]


def finish(own, delivered):
    chunks = len(own)
    slots, rows, virtuals = own[0].shape
    pieces, _, short, wide = delivered[0].shape
    return pl.pallas_call(
        functools.partial(finish_kernel, chunks),
        grid=(slots,),
        in_specs=[pl.BlockSpec((1, rows, virtuals), lambda s: (s, 0, 0))] * chunks
        + [pl.BlockSpec((pieces, 1, short, wide), lambda s: (0, s, 0, 0))] * chunks,
        out_specs=pl.BlockSpec((1, 1, wide, virtuals), lambda s: (0, s, 0, 0)),
        out_shape=jax.ShapeDtypeStruct((1, slots, wide, virtuals), jnp.float32),
        scratch_shapes=[pltpu.VMEM((virtuals, wide), jnp.float32)],
        compiler_params=pltpu.CompilerParams(vmem_limit_bytes=VMEM_BYTES),
        name="finish",
    )(*own, *delivered)


def swap(array, axis):
    return lax.all_to_all(array, axis, split_axis=0, concat_axis=0, tiled=True)


def body(sections, amplitudes, integrals, tile_mask, pair_list):
    _, pairs, virtuals, _ = amplitudes.shape
    occupied, slots = pair_list.shape
    wide = virtuals // sections
    chunks = CHUNKS
    rows = wide // chunks
    short = rows // pairs

    owners = jnp.arange(occupied, dtype=jnp.int32)
    partner_slot = jnp.where(pair_list[pair_list, 0] == owners[:, None], 0, 1).astype(jnp.int32)
    source_row = (pair_list * slots + partner_slot).reshape(-1)

    own_view = amplitudes.reshape(1, pairs, sections, chunks, rows, virtuals)
    flipped = flip_chunks(amplitudes, sections, chunks)
    masked = mask_blocks(integrals, tile_mask)

    own, delivered = [], []
    for chunk in range(chunks):
        across = swap(flipped[chunk], "ka").reshape(occupied, rows, virtuals)
        crossed = swap(across, "ia").reshape(sections, pairs, rows, virtuals)
        mirrored = swap(crossed, "ka")
        partial_rows = product(own_view, mirrored, masked, chunk)
        summed = lax.psum_scatter(partial_rows, "ka", scatter_dimension=0, tiled=False)
        own.append(summed)
        cut = summed.reshape(slots, pairs, short, sections, wide).transpose(3, 1, 0, 2, 4)
        columns = swap(cut, "ka").reshape(occupied, slots, short, wide)
        spread = swap(columns, "ia").reshape(occupied * slots, short, wide)
        routed = jnp.take(spread, source_row, axis=0).reshape(occupied, slots, short, wide)
        delivered.append(swap(routed, "ia"))
    return finish(own, delivered)


def solution(mesh):
    placed = (
        P("ia", "ka", None, None),
        P("ia", None, "ka", None, None),
        P("ia", None, "ka", None, None),
        P(),
    )
    return jax.shard_map(
        functools.partial(body, mesh.shape["ka"]),
        mesh=mesh,
        in_specs=placed,
        out_specs=P("ia", None, "ka", None),
        check_vma=False,
    )
```

```python
import functools

import jax
import jax.numpy as jnp
from jax import lax
from jax.experimental import pallas as pl
from jax.experimental.pallas import tpu as pltpu
from jax.sharding import PartitionSpec as P

ROUNDS = 4
VMEM_BYTES = 48 * 1024 * 1024


def call(kernel, name, scalars, operands, in_specs, out_specs, out_shape, grid, scratch=(), flops=0):
    moved = sum(x.size * x.dtype.itemsize for x in jax.tree.leaves(out_shape)) * 2
    return pl.pallas_call(
        kernel,
        grid_spec=pltpu.PrefetchScalarGridSpec(
            num_scalar_prefetch=1,
            grid=grid,
            in_specs=in_specs,
            out_specs=out_specs,
            scratch_shapes=list(scratch),
        ),
        out_shape=out_shape,
        compiler_params=pltpu.CompilerParams(vmem_limit_bytes=VMEM_BYTES),
        cost_estimate=pl.CostEstimate(flops=flops, bytes_accessed=moved, transcendentals=0),
        name=name,
    )(scalars, *operands)


def flip_kernel(pairs, place_ref, *refs):
    blocks, pieces = refs[:pairs], refs[pairs:]
    rounds = len(pieces) // pairs
    for e in range(pairs):
        flipped = blocks[e][0, 0].T
        rows = flipped.shape[0] // rounds
        for r in range(rounds):
            pieces[r * pairs + e][...] = flipped[r * rows : (r + 1) * rows]


def flip(place, amplitudes, section, sections, rounds):
    pairs, virtuals = amplitudes.shape[1], amplitudes.shape[3]
    wide = virtuals // sections
    rows = wide // rounds
    out = call(
        functools.partial(flip_kernel, pairs),
        "flip",
        place,
        [amplitudes] * pairs,
        [
            pl.BlockSpec((1, 1, virtuals, wide), lambda n, at, e=e: (0, at[1] ^ e, 0, section))
            for e in range(pairs)
        ],
        [pl.BlockSpec((rows, virtuals), lambda n, at: (0, 0))] * (rounds * pairs),
        [jax.ShapeDtypeStruct((rows, virtuals), jnp.float32)] * (rounds * pairs),
        (1,),
    )
    return [out[r * pairs : (r + 1) * pairs] for r in range(rounds)]


def mask_kernel(tiles, mask_ref, integrals_ref, masked_ref):
    side = integrals_ref.shape[-1] // tiles
    slot, pair = pl.program_id(0), pl.program_id(1)
    for r in range(tiles):
        for c in range(tiles):
            keep = mask_ref[slot, pair, r, c] != 0
            spot = (pl.ds(r * side, side), pl.ds(c * side, side))
            tile = integrals_ref[0, 0, 0, spot[0], spot[1]]
            masked_ref[0, 0, spot[0], spot[1]] = jnp.where(keep, tile, jnp.zeros_like(tile))


def mask_blocks(integrals, tile_mask):
    _, slots, pairs, virtuals, _ = integrals.shape
    out_shape = jax.ShapeDtypeStruct((slots, pairs, virtuals, virtuals), jnp.bfloat16)
    return call(
        functools.partial(mask_kernel, tile_mask.shape[-1]),
        "mask",
        tile_mask[0],
        [integrals],
        [pl.BlockSpec((1, 1, 1, virtuals, virtuals), lambda s, k, mask: (0, s, k, 0, 0))],
        pl.BlockSpec((1, 1, virtuals, virtuals), lambda s, k, mask: (s, k, 0, 0)),
        out_shape,
        (slots, pairs),
    )


def product_kernel(sections, pairs, place_ref, *refs):
    own_refs, refs = refs[:pairs], refs[pairs:]
    mirrored_refs, refs = refs[: sections * pairs], refs[sections * pairs :]
    masked_refs, refs = refs[:pairs], refs[pairs:]
    out_refs, split_ref = refs[:sections], refs[sections]
    rows = mirrored_refs[0].shape[0]
    tall = sections * rows
    here = place_ref[2]

    @pl.when((pl.program_id(0) == 0) & (pl.program_id(1) == 0))
    def _():
        for g in range(sections):
            start = pl.multiple_of((here ^ g) * rows, rows)
            for e in range(pairs):
                mixed = 2.0 * own_refs[e][0, 0, g, 0] - mirrored_refs[g * pairs + e][...]
                high = mixed.astype(jnp.bfloat16)
                low = (mixed - high.astype(jnp.float32)).astype(jnp.bfloat16)
                split_ref[e, pl.ds(start, rows)] = high
                split_ref[e, pl.ds(tall + start, rows)] = low

    total = None
    for e in range(pairs):
        both = jnp.dot(split_ref[e], masked_refs[e][0, 0], preferred_element_type=jnp.float32)
        both = both[:tall] + both[tall:]
        total = both if total is None else total + both
    for d in range(sections):
        out_refs[d][0] = total[d * rows : (d + 1) * rows]


def product(place, own, mirrored, masked, turn):
    sections, pairs = len(mirrored), len(mirrored[0])
    rows, virtuals = mirrored[0][0].shape
    slots = masked.shape[0]
    wide = min(virtuals, 512)
    flat = [piece for section in mirrored for piece in section]
    return call(
        functools.partial(product_kernel, sections, pairs),
        "product",
        place,
        [own] * pairs + flat + [masked] * pairs,
        [
            pl.BlockSpec(
                (1, 1, sections, 1, rows, virtuals),
                lambda s, n, at, e=e: (0, at[1] ^ e, 0, turn, 0, 0),
            )
            for e in range(pairs)
        ]
        + [pl.BlockSpec((rows, virtuals), lambda s, n, at: (0, 0))] * len(flat)
        + [
            pl.BlockSpec((1, 1, virtuals, wide), lambda s, n, at, e=e: (s, at[1] ^ e, 0, n))
            for e in range(pairs)
        ],
        [pl.BlockSpec((1, rows, wide), lambda s, n, at: (s, 0, n))] * sections,
        [jax.ShapeDtypeStruct((slots, rows, virtuals), jnp.float32)] * sections,
        (slots, virtuals // wide),
        scratch=[pltpu.VMEM((pairs, 2 * sections * rows, virtuals), jnp.bfloat16)],
        flops=4 * sections * rows * pairs * virtuals * virtuals * slots,
    )


def total_kernel(sections, place_ref, *refs):
    part_refs, total_ref, cut_refs = refs[:sections], refs[sections], refs[sections + 1 :]
    total_ref[...] = sum((part[...] for part in part_refs[1:]), part_refs[0][...])
    wide = cut_refs[0].shape[-1]
    for d in range(sections):
        start = pl.multiple_of((place_ref[2] ^ d) * wide, wide)
        cut_refs[d][...] = total_ref[:, :, pl.ds(start, wide)]


def total(place, parts):
    sections = len(parts)
    slots, rows, virtuals = parts[0].shape
    wide = virtuals // sections
    full = pl.BlockSpec((slots, rows, virtuals), lambda n, at: (0, 0, 0))
    out = call(
        functools.partial(total_kernel, sections),
        "total",
        place,
        parts,
        [full] * sections,
        [full] + [pl.BlockSpec((slots, rows, wide), lambda n, at: (0, 0, 0))] * sections,
        [jax.ShapeDtypeStruct((slots, rows, virtuals), jnp.float32)]
        + [jax.ShapeDtypeStruct((slots, rows, wide), jnp.float32)] * sections,
        (1,),
    )
    return out[0], out[1:]


def finish_kernel(rounds, place_ref, *refs):
    own_refs, delivered_refs = refs[:rounds], refs[rounds : 2 * rounds]
    out_ref, columns_ref = refs[2 * rounds :]
    rows = own_refs[0].shape[1]
    sections = columns_ref.shape[0] // (rows * rounds)
    pieces, _, short, _ = delivered_refs[0].shape
    parts = pieces // sections
    for r in range(rounds):
        for d in range(sections):
            base = pl.multiple_of(((place_ref[2] ^ d) * rounds + r) * rows, rows)
            for part in range(parts):
                columns_ref[pl.ds(base + part * short, short)] = delivered_refs[r][d * parts + part, 0]
    turned = columns_ref[...].T
    for r in range(rounds):
        spot = slice(r * rows, (r + 1) * rows)
        out_ref[0, 0, spot] = own_refs[r][0] + turned[spot]


def finish(place, own, delivered):
    rounds = len(own)
    slots, rows, virtuals = own[0].shape
    pieces, _, short, wide = delivered[0].shape
    return call(
        functools.partial(finish_kernel, rounds),
        "finish",
        place,
        list(own) + list(delivered),
        [pl.BlockSpec((1, rows, virtuals), lambda s, at: (s, 0, 0))] * rounds
        + [pl.BlockSpec((pieces, 1, short, wide), lambda s, at: (0, s, 0, 0))] * rounds,
        pl.BlockSpec((1, 1, wide, virtuals), lambda s, at: (0, s, 0, 0)),
        jax.ShapeDtypeStruct((1, slots, wide, virtuals), jnp.float32),
        (slots,),
        scratch=[pltpu.VMEM((virtuals, wide), jnp.float32)],
    )


def swap(array, axis):
    return lax.all_to_all(array, axis, split_axis=0, concat_axis=0, tiled=True)


def route(array, sections, pairs, move):
    moves = []
    for plane in range(sections):
        for core in range(pairs):
            for line in range(sections):
                to_plane, to_core, to_line = move(plane, core, line)
                source = (plane * pairs + core) * sections + line
                moves.append((source, (to_plane * pairs + to_core) * sections + to_line))
    return lax.ppermute(array, ("ia", "ka"), moves)


def body(sections, amplitudes, integrals, tile_mask, pair_list):
    _, pairs, virtuals, _ = amplitudes.shape
    occupied, slots = pair_list.shape
    wide = virtuals // sections
    rounds = ROUNDS
    rows = wide // rounds
    short = rows // pairs
    here, there = lax.axis_index("ka"), lax.axis_index("ia")
    place = jnp.stack([there // pairs, there % pairs, here]).astype(jnp.int32)

    owners = jnp.arange(occupied, dtype=jnp.int32)
    partner_slot = jnp.where(pair_list[pair_list, 0] == owners[:, None], 0, 1).astype(jnp.int32)
    source_row = (pair_list * slots + partner_slot).reshape(-1)

    own_view = amplitudes.reshape(1, pairs, sections, rounds, rows, virtuals)
    flipped = [flip(place, amplitudes, g, sections, rounds) for g in range(sections)]
    masked = mask_blocks(integrals, tile_mask)

    own, delivered = [], []
    for r in range(rounds):
        mirrored = []
        for g in range(sections):
            landed = []
            for e in range(pairs):
                piece = flipped[g][r][e]
                piece = route(piece, sections, pairs, lambda a, c, q: (a, c, a ^ q ^ g))
                piece = route(piece, sections, pairs, lambda a, c, l: (a ^ l ^ g, c ^ e, l))
                piece = route(piece, sections, pairs, lambda q, c, l: (q, c, q ^ l ^ g))
                landed.append(piece)
            mirrored.append(landed)
        parts = product(place, own_view, mirrored, masked, r)
        parts = [parts[0]] + [
            route(parts[d], sections, pairs, lambda a, c, q: (a, c, q ^ d))
            for d in range(1, sections)
        ]
        summed, cuts = total(place, parts)
        own.append(summed)
        columns = [cuts[0]] + [
            route(cuts[d], sections, pairs, lambda a, c, q: (a, c, q ^ d))
            for d in range(1, sections)
        ]
        columns = jnp.stack(columns).reshape(sections, slots, pairs, short, wide)
        columns = columns.swapaxes(1, 2).reshape(occupied, slots, short, wide)
        spread = swap(columns, "ia").reshape(occupied * slots, short, wide)
        routed = jnp.take(spread, source_row, axis=0).reshape(occupied, slots, short, wide)
        delivered.append(swap(routed, "ia"))
    return finish(place, own, delivered)


def solution(mesh):
    placed = (
        P("ia", "ka", None, None),
        P("ia", None, "ka", None, None),
        P("ia", None, "ka", None, None),
        P(),
    )
    return jax.shard_map(
        functools.partial(body, mesh.shape["ka"]),
        mesh=mesh,
        in_specs=placed,
        out_specs=P("ia", None, "ka", None),
        check_vma=False,
    )
```

```python
import functools

import jax
import jax.numpy as jnp
from jax import lax
from jax.experimental import pallas as pl
from jax.experimental.pallas import tpu as pltpu
from jax.sharding import PartitionSpec as P

CHUNKS = (2, 3, 2, 1)
LANES = 128
VMEM_BYTES = 48 * 1024 * 1024


def call(kernel, name, scalars, operands, in_specs, out_specs, out_shape, grid, scratch=(), flops=0):
    moved = sum(x.size * x.dtype.itemsize for x in jax.tree.leaves(out_shape)) * 2
    return pl.pallas_call(
        kernel,
        grid_spec=pltpu.PrefetchScalarGridSpec(
            num_scalar_prefetch=1,
            grid=grid,
            in_specs=in_specs,
            out_specs=out_specs,
            scratch_shapes=list(scratch),
        ),
        out_shape=out_shape,
        compiler_params=pltpu.CompilerParams(vmem_limit_bytes=VMEM_BYTES),
        cost_estimate=pl.CostEstimate(flops=flops, bytes_accessed=moved, transcendentals=0),
        name=name,
    )(scalars, *operands)


def whole(shape):
    return pl.BlockSpec(shape, lambda *_: (0,) * len(shape))


def first_flip_kernel(place_ref, blocks_ref, piece_ref):
    piece_ref[0, 0] = blocks_ref[0, 0].T[: piece_ref.shape[2]]


def first_flip(place, amplitudes, sections, rows):
    pairs, virtuals = amplitudes.shape[1], amplitudes.shape[3]
    steps = virtuals // sections // LANES
    return call(
        first_flip_kernel,
        "first_flip",
        place,
        [amplitudes],
        [pl.BlockSpec((1, 1, virtuals, LANES), lambda d, q, at: (0, d, 0, q * steps))],
        pl.BlockSpec((1, 1, rows, virtuals), lambda d, q, at: (q, d, 0, 0)),
        jax.ShapeDtypeStruct((sections, pairs, rows, virtuals), jnp.float32),
        (pairs, sections),
    )


def flip_kernel(spans, place_ref, blocks_ref, *pieces):
    flipped = blocks_ref[0, 0].T
    for (start, rows), piece in zip(spans, pieces):
        piece[0] = flipped[start : start + rows]


def flip(place, amplitudes, sections, e, spans):
    pairs, virtuals = amplitudes.shape[1], amplitudes.shape[3]
    wide = virtuals // sections
    return call(
        functools.partial(flip_kernel, spans),
        "flip",
        place,
        [amplitudes],
        [pl.BlockSpec((1, 1, virtuals, wide), lambda d, at: (0, d, 0, at[0] ^ e))],
        [pl.BlockSpec((1, rows, virtuals), lambda d, at: (d, 0, 0)) for _, rows in spans],
        [jax.ShapeDtypeStruct((pairs, rows, virtuals), jnp.float32) for _, rows in spans],
        (pairs,),
    )


def gather_kernel(place_ref, *refs):
    pieces, out_ref = refs[:-1], refs[-1]
    for e, piece in enumerate(pieces):
        out_ref[place_ref[0] ^ e] = piece[...]


def gather(place, pieces):
    shape = (len(pieces), *pieces[0].shape)
    return call(
        gather_kernel,
        "gather",
        place,
        pieces,
        [whole(pieces[0].shape)] * len(pieces),
        whole(shape),
        jax.ShapeDtypeStruct(shape, jnp.float32),
        (1,),
    )


def scatter_kernel(place_ref, stacked_ref, *pieces):
    for e, piece in enumerate(pieces):
        piece[...] = stacked_ref[place_ref[0] ^ e]


def scatter(place, stacked):
    count, shape = stacked.shape[0], stacked.shape[1:]
    return call(
        scatter_kernel,
        "scatter",
        place,
        [stacked],
        [whole(stacked.shape)],
        [whole(shape)] * count,
        [jax.ShapeDtypeStruct(shape, jnp.float32)] * count,
        (1,),
    )


def mask_kernel(tiles, mask_ref, integrals_ref, masked_ref):
    side = integrals_ref.shape[-1] // tiles
    slot, pair = pl.program_id(0), pl.program_id(1)
    for r in range(tiles):
        for c in range(tiles):
            keep = mask_ref[slot, pair, r, c] != 0
            spot = (pl.ds(r * side, side), pl.ds(c * side, side))
            tile = integrals_ref[0, 0, 0, spot[0], spot[1]]
            masked_ref[0, 0, spot[0], spot[1]] = jnp.where(keep, tile, jnp.zeros_like(tile))


def mask_blocks(integrals, tile_mask):
    _, slots, pairs, virtuals, _ = integrals.shape
    out_shape = jax.ShapeDtypeStruct((slots, pairs, virtuals, virtuals), jnp.bfloat16)
    return call(
        functools.partial(mask_kernel, tile_mask.shape[-1]),
        "mask",
        tile_mask[0],
        [integrals],
        [pl.BlockSpec((1, 1, 1, virtuals, virtuals), lambda s, k, mask: (0, s, k, 0, 0))],
        pl.BlockSpec((1, 1, virtuals, virtuals), lambda s, k, mask: (s, k, 0, 0)),
        out_shape,
        (slots, pairs),
    )


def product_kernel(sections, place_ref, *refs):
    own_refs, mirrored_refs, refs = refs[:sections], refs[sections : 2 * sections], refs[2 * sections :]
    masked_ref, out_ref, split_ref = refs
    pairs, rows, _ = mirrored_refs[0].shape
    tall = sections * rows

    @pl.when((pl.program_id(0) == 0) & (pl.program_id(1) == 0))
    def _():
        for e in range(sections):
            for k in range(pairs):
                mixed = 2.0 * own_refs[e][0, k] - mirrored_refs[e][k]
                high = mixed.astype(jnp.bfloat16)
                low = (mixed - high.astype(jnp.float32)).astype(jnp.bfloat16)
                split_ref[k, pl.ds(e * rows, rows)] = high
                split_ref[k, pl.ds(tall + e * rows, rows)] = low

    total = None
    for k in range(pairs):
        both = jnp.dot(split_ref[k], masked_ref[0, k], preferred_element_type=jnp.float32)
        both = both[:tall] + both[tall:]
        total = both if total is None else total + both
    for e in range(sections):
        out_ref[place_ref[0] ^ e, 0] = total[e * rows : (e + 1) * rows]


def product(place, own, mirrored, masked, start):
    sections = len(mirrored)
    pairs, rows, virtuals = mirrored[0].shape
    slots = masked.shape[0]
    deep = virtuals // sections
    wide = min(virtuals, 512)
    return call(
        functools.partial(product_kernel, sections),
        "product",
        place,
        [own] * sections + list(mirrored) + [masked],
        [
            pl.BlockSpec(
                tuple(pl.Element(size) for size in (1, pairs, rows, virtuals)),
                lambda s, n, at, e=e: (0, 0, pl.multiple_of((at[0] ^ e) * deep + start, 8), 0),
            )
            for e in range(sections)
        ]
        + [whole(mirrored[0].shape)] * sections
        + [pl.BlockSpec((1, pairs, virtuals, wide), lambda s, n, at: (s, 0, 0, n))],
        pl.BlockSpec((sections, 1, rows, wide), lambda s, n, at: (0, s, 0, n)),
        jax.ShapeDtypeStruct((sections, slots, rows, virtuals), jnp.float32),
        (slots, virtuals // wide),
        scratch=[pltpu.VMEM((pairs, 2 * sections * rows, virtuals), jnp.bfloat16)],
        flops=4 * sections * rows * pairs * virtuals * virtuals * slots,
    )


def cut_kernel(place_ref, total_ref, *cut_refs):
    parts, _, short, wide = cut_refs[0].shape
    for e, cut_ref in enumerate(cut_refs):
        start = pl.multiple_of((place_ref[0] ^ e) * wide, wide)
        for part in range(parts):
            cut_ref[part] = total_ref[:, part * short : (part + 1) * short, pl.ds(start, wide)]


def cut(place, total, sections, parts):
    slots, rows, virtuals = total.shape
    shape = (parts, slots, rows // parts, virtuals // sections)
    return call(
        cut_kernel,
        "cut",
        place,
        [total],
        [whole(total.shape)],
        [whole(shape)] * sections,
        [jax.ShapeDtypeStruct(shape, jnp.float32)] * sections,
        (1,),
    )


def finish_kernel(spans, place_ref, *refs):
    chunks = len(spans)
    own_refs, delivered_refs = refs[:chunks], refs[chunks : 2 * chunks]
    out_ref, columns_ref = refs[2 * chunks :]
    wide = out_ref.shape[2]
    sections = columns_ref.shape[0] // wide
    for (start, _), delivered_ref in zip(spans, delivered_refs):
        pieces, _, short, _ = delivered_ref.shape
        parts = pieces // sections
        for e in range(sections):
            base = (place_ref[0] ^ e) * wide + start
            for part in range(parts):
                spot = pl.multiple_of(base + part * short, 8)
                columns_ref[pl.ds(spot, short)] = delivered_ref[e * parts + part, 0]
    turned = columns_ref[...].T
    for (start, rows), own_ref in zip(spans, own_refs):
        out_ref[0, 0, start : start + rows] = own_ref[0] + turned[start : start + rows]


def finish(place, spans, own, delivered):
    slots, _, virtuals = own[0].shape
    wide = delivered[0].shape[-1]
    return call(
        functools.partial(finish_kernel, spans),
        "finish",
        place,
        list(own) + list(delivered),
        [pl.BlockSpec((1, *x.shape[1:]), lambda s, at: (s, 0, 0)) for x in own]
        + [
            pl.BlockSpec((x.shape[0], 1, *x.shape[2:]), lambda s, at: (0, s, 0, 0))
            for x in delivered
        ],
        pl.BlockSpec((1, 1, wide, virtuals), lambda s, at: (0, s, 0, 0)),
        jax.ShapeDtypeStruct((1, slots, wide, virtuals), jnp.float32),
        (slots,),
        scratch=[pltpu.VMEM((virtuals, wide), jnp.float32)],
    )


def swap(array, axis):
    return lax.all_to_all(array, axis, split_axis=0, concat_axis=0, tiled=True)


def spread(pieces):
    count = len(pieces)
    return [pieces[0]] + [
        lax.ppermute(pieces[e], "ka", [(q, q ^ e) for q in range(count)]) for e in range(1, count)
    ]


def body(sections, amplitudes, integrals, tile_mask, pair_list):
    _, pairs, virtuals, _ = amplitudes.shape
    occupied, slots = pair_list.shape
    wide = virtuals // sections
    sizes = [wide * part // sum(CHUNKS) for part in CHUNKS]
    spans = [(sum(sizes[:at]), size) for at, size in enumerate(sizes)]
    place = lax.axis_index("ka").astype(jnp.int32).reshape(1)

    owners = jnp.arange(occupied, dtype=jnp.int32)
    partner_slot = jnp.where(pair_list[pair_list, 0] == owners[:, None], 0, 1).astype(jnp.int32)
    source_row = (pair_list * slots + partner_slot).reshape(-1)

    first = first_flip(place, amplitudes, sections, sizes[0])
    flipped = [flip(place, amplitudes, sections, e, spans[1:]) for e in range(sections)]
    masked = mask_blocks(integrals, tile_mask)

    own, delivered = [], []
    for at, (start, rows) in enumerate(spans):
        short = rows // pairs
        if at == 0:
            across = swap(first, "ka")
        else:
            across = gather(place, spread([pieces[at - 1] for pieces in flipped]))
        crossed = swap(across.reshape(occupied, rows, virtuals), "ia")
        crossed = crossed.reshape(sections, pairs, rows, virtuals)
        mirrored = spread(scatter(place, crossed))
        partial_rows = product(place, amplitudes, mirrored, masked, start)
        summed = lax.psum_scatter(partial_rows, "ka", scatter_dimension=0, tiled=False)
        own.append(summed)
        columns = jnp.concatenate(spread(cut(place, summed, sections, pairs)))
        met = swap(columns, "ia").reshape(occupied * slots, short, wide)
        routed = jnp.take(met, source_row, axis=0).reshape(occupied, slots, short, wide)
        delivered.append(swap(routed, "ia"))
    return finish(place, spans, own, delivered)


def solution(mesh):
    placed = (
        P("ia", "ka", None, None),
        P("ia", None, "ka", None, None),
        P("ia", None, "ka", None, None),
        P(),
    )
    return jax.shard_map(
        functools.partial(body, mesh.shape["ka"]),
        mesh=mesh,
        in_specs=placed,
        out_specs=P("ia", None, "ka", None),
        check_vma=False,
    )
```

```python
import functools

import jax
import jax.numpy as jnp
from jax import lax
from jax.experimental import pallas as pl
from jax.experimental.pallas import tpu as pltpu
from jax.sharding import PartitionSpec as P

CHUNKS = (1, 2, 3, 2)
GROUPS = ((0, 1), (2,), (3,))
LANES = 128
VMEM_BYTES = 48 * 1024 * 1024


def call(kernel, name, scalars, operands, in_specs, out_specs, out_shape, grid, scratch=(), flops=0):
    moved = sum(x.size * x.dtype.itemsize for x in jax.tree.leaves(out_shape)) * 2
    return pl.pallas_call(
        kernel,
        grid_spec=pltpu.PrefetchScalarGridSpec(
            num_scalar_prefetch=1,
            grid=grid,
            in_specs=in_specs,
            out_specs=out_specs,
            scratch_shapes=list(scratch),
        ),
        out_shape=out_shape,
        compiler_params=pltpu.CompilerParams(vmem_limit_bytes=VMEM_BYTES),
        cost_estimate=pl.CostEstimate(flops=flops, bytes_accessed=moved, transcendentals=0),
        name=name,
    )(scalars, *operands)


def whole(shape):
    return pl.BlockSpec(shape, lambda *_: (0,) * len(shape))


def first_flip_kernel(place_ref, blocks_ref, piece_ref):
    piece_ref[0, 0] = blocks_ref[0, 0].T[: piece_ref.shape[2]]


def first_flip(place, amplitudes, sections, rows):
    pairs, virtuals = amplitudes.shape[1], amplitudes.shape[3]
    steps = virtuals // sections // LANES
    return call(
        first_flip_kernel,
        "first_flip",
        place,
        [amplitudes],
        [pl.BlockSpec((1, 1, virtuals, LANES), lambda d, q, at: (0, d, 0, q * steps))],
        pl.BlockSpec((1, 1, rows, virtuals), lambda d, q, at: (q, d, 0, 0)),
        jax.ShapeDtypeStruct((sections, pairs, rows, virtuals), jnp.float32),
        (pairs, sections),
    )


def flip_kernel(spans, low, place_ref, blocks_ref, after_ref, *pieces):
    flipped = blocks_ref[0, 0].T
    for (start, rows), piece in zip(spans, pieces):
        piece[0] = flipped[start - low : start - low + rows]


def flip(place, amplitudes, sections, e, spans, after):
    pairs, virtuals = amplitudes.shape[1], amplitudes.shape[3]
    wide = virtuals // sections
    low = spans[0][0] // LANES * LANES
    read = LANES if sum(spans[-1]) <= low + LANES else wide
    low = low if read == LANES else 0
    return call(
        functools.partial(flip_kernel, spans, low),
        "flip",
        place,
        [amplitudes, after],
        [
            pl.BlockSpec(
                (1, 1, virtuals, read),
                lambda d, at: (0, d, 0, (at[0] ^ e) * (wide // read) + low // read),
            ),
            pl.BlockSpec(memory_space=pl.ANY),
        ],
        [pl.BlockSpec((1, rows, virtuals), lambda d, at: (d, 0, 0)) for _, rows in spans],
        [jax.ShapeDtypeStruct((pairs, rows, virtuals), jnp.float32) for _, rows in spans],
        (pairs,),
    )


def gather_kernel(ordered, place_ref, *refs):
    pieces, out_ref = refs[:-2], refs[-1]
    for e, piece in enumerate(pieces):
        out_ref[place_ref[0] ^ e if ordered else e] = piece[...]


def gather(place, pieces, after, ordered=True):
    shape = (len(pieces), *pieces[0].shape)
    return call(
        functools.partial(gather_kernel, ordered),
        "gather",
        place,
        [*pieces, after],
        [whole(pieces[0].shape)] * len(pieces) + [pl.BlockSpec(memory_space=pl.ANY)],
        whole(shape),
        jax.ShapeDtypeStruct(shape, jnp.float32),
        (1,),
    )


def scatter_kernel(place_ref, stacked_ref, *pieces):
    for e, piece in enumerate(pieces):
        piece[...] = stacked_ref[place_ref[0] ^ e]


def scatter(place, stacked):
    count, shape = stacked.shape[0], stacked.shape[1:]
    return call(
        scatter_kernel,
        "scatter",
        place,
        [stacked],
        [whole(stacked.shape)],
        [whole(shape)] * count,
        [jax.ShapeDtypeStruct(shape, jnp.float32)] * count,
        (1,),
    )


def mask_kernel(tiles, mask_ref, integrals_ref, masked_ref):
    side = integrals_ref.shape[-1] // tiles
    slot, pair = pl.program_id(0), pl.program_id(1)
    for r in range(tiles):
        for c in range(tiles):
            keep = mask_ref[slot, pair, r, c] != 0
            spot = (pl.ds(r * side, side), pl.ds(c * side, side))
            tile = integrals_ref[0, 0, 0, spot[0], spot[1]]
            masked_ref[0, 0, spot[0], spot[1]] = jnp.where(keep, tile, jnp.zeros_like(tile))


def mask_blocks(integrals, tile_mask):
    _, slots, pairs, virtuals, _ = integrals.shape
    out_shape = jax.ShapeDtypeStruct((slots, pairs, virtuals, virtuals), jnp.bfloat16)
    return call(
        functools.partial(mask_kernel, tile_mask.shape[-1]),
        "mask",
        tile_mask[0],
        [integrals],
        [pl.BlockSpec((1, 1, 1, virtuals, virtuals), lambda s, k, mask: (0, s, k, 0, 0))],
        pl.BlockSpec((1, 1, virtuals, virtuals), lambda s, k, mask: (s, k, 0, 0)),
        out_shape,
        (slots, pairs),
    )


def product_kernel(sections, place_ref, *refs):
    own_refs, mirrored_refs, refs = refs[:sections], refs[sections : 2 * sections], refs[2 * sections :]
    masked_ref, out_ref, split_ref = refs
    pairs, rows, _ = mirrored_refs[0].shape
    tall = sections * rows

    @pl.when((pl.program_id(0) == 0) & (pl.program_id(1) == 0))
    def _():
        for e in range(sections):
            for k in range(pairs):
                mixed = 2.0 * own_refs[e][0, k] - mirrored_refs[e][k]
                high = mixed.astype(jnp.bfloat16)
                low = (mixed - high.astype(jnp.float32)).astype(jnp.bfloat16)
                split_ref[k, pl.ds(e * rows, rows)] = high
                split_ref[k, pl.ds(tall + e * rows, rows)] = low

    total = None
    for k in range(pairs):
        both = jnp.dot(split_ref[k], masked_ref[0, k], preferred_element_type=jnp.float32)
        both = both[:tall] + both[tall:]
        total = both if total is None else total + both
    for e in range(sections):
        out_ref[place_ref[0] ^ e, 0] = total[e * rows : (e + 1) * rows]


def product(place, own, mirrored, masked, start):
    sections = len(mirrored)
    pairs, rows, virtuals = mirrored[0].shape
    slots = masked.shape[0]
    deep = virtuals // sections
    wide = min(virtuals, 512)
    return call(
        functools.partial(product_kernel, sections),
        "product",
        place,
        [own] * sections + list(mirrored) + [masked],
        [
            pl.BlockSpec(
                tuple(pl.Element(size) for size in (1, pairs, rows, virtuals)),
                lambda s, n, at, e=e: (0, 0, pl.multiple_of((at[0] ^ e) * deep + start, 8), 0),
            )
            for e in range(sections)
        ]
        + [whole(mirrored[0].shape)] * sections
        + [pl.BlockSpec((1, pairs, virtuals, wide), lambda s, n, at: (s, 0, 0, n))],
        pl.BlockSpec((sections, 1, rows, wide), lambda s, n, at: (0, s, 0, n)),
        jax.ShapeDtypeStruct((sections, slots, rows, virtuals), jnp.float32),
        (slots, virtuals // wide),
        scratch=[pltpu.VMEM((pairs, 2 * sections * rows, virtuals), jnp.bfloat16)],
        flops=4 * sections * rows * pairs * virtuals * virtuals * slots,
    )


def cut_kernel(chunks, place_ref, *refs):
    total_refs, cut_refs = refs[:chunks], refs[chunks:]
    parts, _, _, wide = cut_refs[0].shape
    for e, cut_ref in enumerate(cut_refs):
        columns = pl.ds(pl.multiple_of((place_ref[0] ^ e) * wide, wide), wide)
        at = 0
        for total_ref in total_refs:
            short = total_ref.shape[1] // parts
            for part in range(parts):
                cut_ref[part, :, at : at + short] = total_ref[
                    :, part * short : (part + 1) * short, columns
                ]
            at += short


def cut(place, totals, sections, parts):
    slots, _, virtuals = totals[0].shape
    rows = sum(total.shape[1] for total in totals)
    shape = (parts, slots, rows // parts, virtuals // sections)
    return call(
        functools.partial(cut_kernel, len(totals)),
        "cut",
        place,
        totals,
        [whole(total.shape) for total in totals],
        [whole(shape)] * sections,
        [jax.ShapeDtypeStruct(shape, jnp.float32)] * sections,
        (1,),
    )


def finish_kernel(spans, groups, place_ref, *refs):
    chunks = len(spans)
    own_refs, delivered_refs = refs[:chunks], refs[chunks : chunks + len(groups)]
    out_ref, columns_ref = refs[chunks + len(groups) :]
    wide = out_ref.shape[2]
    sections = columns_ref.shape[0] // wide
    for group, delivered_ref in zip(groups, delivered_refs):
        parts = delivered_ref.shape[0] // sections
        for e in range(sections):
            base = (place_ref[0] ^ e) * wide
            for part in range(parts):
                at = 0
                for chunk in group:
                    start, rows = spans[chunk]
                    short = rows // parts
                    spot = pl.multiple_of(base + start + part * short, 8)
                    columns_ref[pl.ds(spot, short)] = delivered_ref[
                        e * parts + part, 0, at : at + short
                    ]
                    at += short
    turned = columns_ref[...].T
    for (start, rows), own_ref in zip(spans, own_refs):
        out_ref[0, 0, start : start + rows] = own_ref[0] + turned[start : start + rows]


def finish(place, spans, groups, own, delivered):
    slots, _, virtuals = own[0].shape
    wide = delivered[0].shape[-1]
    return call(
        functools.partial(finish_kernel, spans, groups),
        "finish",
        place,
        list(own) + list(delivered),
        [pl.BlockSpec((1, *x.shape[1:]), lambda s, at: (s, 0, 0)) for x in own]
        + [
            pl.BlockSpec((x.shape[0], 1, *x.shape[2:]), lambda s, at: (0, s, 0, 0))
            for x in delivered
        ],
        pl.BlockSpec((1, 1, wide, virtuals), lambda s, at: (0, s, 0, 0)),
        jax.ShapeDtypeStruct((1, slots, wide, virtuals), jnp.float32),
        (slots,),
        scratch=[pltpu.VMEM((virtuals, wide), jnp.float32)],
    )


def swap(array, axis):
    return lax.all_to_all(array, axis, split_axis=0, concat_axis=0, tiled=True)


def spread(pieces):
    count = len(pieces)
    return [pieces[0]] + [
        lax.ppermute(pieces[e], "ka", [(q, q ^ e) for q in range(count)]) for e in range(1, count)
    ]


def body(sections, amplitudes, integrals, tile_mask, pair_list):
    _, pairs, virtuals, _ = amplitudes.shape
    occupied, slots = pair_list.shape
    wide = virtuals // sections
    sizes = [wide * part // sum(CHUNKS) for part in CHUNKS]
    spans = [(sum(sizes[:at]), size) for at, size in enumerate(sizes)]
    place = lax.axis_index("ka").astype(jnp.int32).reshape(1)

    owners = jnp.arange(occupied, dtype=jnp.int32)
    partner_slot = jnp.where(pair_list[pair_list, 0] == owners[:, None], 0, 1).astype(jnp.int32)
    source_row = (pair_list * slots + partner_slot).reshape(-1)

    first = first_flip(place, amplitudes, sections, sizes[0])
    second = [flip(place, amplitudes, sections, e, spans[1:2], first) for e in range(sections)]
    across = [swap(first, "ka")]
    later = [flip(place, amplitudes, sections, e, spans[2:], across[0]) for e in range(sections)]
    flipped = [[*early, *late] for early, late in zip(second, later)]
    masked = mask_blocks(integrals, tile_mask)
    own = []
    for at, (start, rows) in enumerate(spans):
        if at > 0:
            met = spread([pieces[at - 1] for pieces in flipped])
            across.append(gather(place, met, mirrored[-1] if at > 1 else across[0]))
        if at > 0:
            mirrored = spread(returned)
            partial_rows = product(place, amplitudes, mirrored, masked, spans[at - 1][0])
            own.append(lax.psum_scatter(partial_rows, "ka", scatter_dimension=0, tiled=False))
        crossed = swap(across[at].reshape(occupied, rows, virtuals), "ia")
        returned = scatter(place, crossed.reshape(sections, pairs, rows, virtuals))
    partial_rows = product(place, amplitudes, spread(returned), masked, spans[-1][0])
    own.append(lax.psum_scatter(partial_rows, "ka", scatter_dimension=0, tiled=False))

    delivered = []
    for group in GROUPS:
        columns = spread(cut(place, [own[at] for at in group], sections, pairs))
        columns = gather(place, columns, returned[0], ordered=False)
        piece = columns.shape[-2:]
        met = swap(columns.reshape(occupied, slots, *piece), "ia")
        routed = jnp.take(met.reshape(occupied * slots, *piece), source_row, axis=0)
        delivered.append(swap(routed.reshape(occupied, slots, *piece), "ia"))
    return finish(place, spans, GROUPS, own, delivered)


def solution(mesh):
    placed = (
        P("ia", "ka", None, None),
        P("ia", None, "ka", None, None),
        P("ia", None, "ka", None, None),
        P(),
    )
    return jax.shard_map(
        functools.partial(body, mesh.shape["ka"]),
        mesh=mesh,
        in_specs=placed,
        out_specs=P("ia", None, "ka", None),
        check_vma=False,
    )
```

```python
import functools

import jax
import jax.numpy as jnp
from jax import lax
from jax.experimental import pallas as pl
from jax.experimental.pallas import tpu as pltpu
from jax.sharding import PartitionSpec as P

CHUNKS = (4, 2, 2)
GROUPS = ((0, 1), (2,))
LANES = 128
VMEM_BYTES = 48 * 1024 * 1024


def call(kernel, name, scalars, operands, in_specs, out_specs, out_shape, grid, scratch=(), flops=0):
    moved = sum(x.size * x.dtype.itemsize for x in jax.tree.leaves(out_shape)) * 2
    return pl.pallas_call(
        kernel,
        grid_spec=pltpu.PrefetchScalarGridSpec(
            num_scalar_prefetch=1,
            grid=grid,
            in_specs=in_specs,
            out_specs=out_specs,
            scratch_shapes=list(scratch),
        ),
        out_shape=out_shape,
        compiler_params=pltpu.CompilerParams(vmem_limit_bytes=VMEM_BYTES),
        cost_estimate=pl.CostEstimate(flops=flops, bytes_accessed=moved, transcendentals=0),
        name=name,
    )(scalars, *operands)


def whole(shape):
    return pl.BlockSpec(shape, lambda *_: (0,) * len(shape))


def flip_kernel(shift, place_ref, *refs):
    half = len(refs) // 2
    blocks, pieces = refs[:half], refs[half + 1 :]
    for block, piece in zip(blocks, pieces):
        piece[...] = block[0, 0].T[shift : shift + piece.shape[0]]


def flip(place, amplitudes, sections, t, span, after):
    pairs, virtuals = amplitudes.shape[1], amplitudes.shape[3]
    wide = virtuals // sections
    start, rows = span
    low = start // LANES * LANES
    read = LANES if start + rows <= low + LANES else wide
    low = low if read == LANES else 0
    return call(
        functools.partial(flip_kernel, start - low),
        "flip",
        place,
        [amplitudes] * pairs + [after],
        [
            pl.BlockSpec(
                (1, 1, virtuals, read),
                lambda n, at, e=e: (
                    0,
                    at[2] ^ e,
                    0,
                    (at[1] ^ t) * (wide // read) + low // read,
                ),
            )
            for e in range(pairs)
        ]
        + [pl.BlockSpec(memory_space=pl.ANY)],
        [whole((rows, virtuals))] * pairs,
        [jax.ShapeDtypeStruct((rows, virtuals), jnp.float32)] * pairs,
        (1,),
    )


def gather_kernel(ordered, place_ref, *refs):
    pieces, out_ref = refs[:-2], refs[-1]
    for e, piece in enumerate(pieces):
        out_ref[place_ref[0] ^ e if ordered else e] = piece[...]


def gather(place, pieces, after, ordered=True):
    shape = (len(pieces), *pieces[0].shape)
    return call(
        functools.partial(gather_kernel, ordered),
        "gather",
        place,
        [*pieces, after],
        [whole(pieces[0].shape)] * len(pieces) + [pl.BlockSpec(memory_space=pl.ANY)],
        whole(shape),
        jax.ShapeDtypeStruct(shape, jnp.float32),
        (1,),
    )


def mask_kernel(tiles, mask_ref, integrals_ref, masked_ref):
    side = integrals_ref.shape[-1] // tiles
    slot, pair = pl.program_id(0), pl.program_id(1)
    for r in range(tiles):
        for c in range(tiles):
            keep = mask_ref[slot, pair, r, c] != 0
            spot = (pl.ds(r * side, side), pl.ds(c * side, side))
            tile = integrals_ref[0, 0, 0, spot[0], spot[1]]
            masked_ref[0, 0, spot[0], spot[1]] = jnp.where(keep, tile, jnp.zeros_like(tile))


def mask_blocks(integrals, tile_mask):
    _, slots, pairs, virtuals, _ = integrals.shape
    out_shape = jax.ShapeDtypeStruct((slots, pairs, virtuals, virtuals), jnp.bfloat16)
    return call(
        functools.partial(mask_kernel, tile_mask.shape[-1]),
        "mask",
        tile_mask[0],
        [integrals],
        [pl.BlockSpec((1, 1, 1, virtuals, virtuals), lambda s, k, mask: (0, s, k, 0, 0))],
        pl.BlockSpec((1, 1, virtuals, virtuals), lambda s, k, mask: (s, k, 0, 0)),
        out_shape,
        (slots, pairs),
    )


def product_kernel(sections, pairs, place_ref, *refs):
    count = sections * pairs
    own_refs, mirrored_refs, refs = refs[:count], refs[count : 2 * count], refs[2 * count :]
    masked_refs, out_ref, split_ref = refs[:pairs], refs[pairs + 1], refs[pairs + 2]
    rows = mirrored_refs[0].shape[0]
    tall = sections * rows

    @pl.when((pl.program_id(0) == 0) & (pl.program_id(1) == 0))
    def _():
        for t in range(sections):
            for e in range(pairs):
                at = t * pairs + e
                mixed = 2.0 * own_refs[at][0, 0] - mirrored_refs[at][...]
                high = mixed.astype(jnp.bfloat16)
                low = (mixed - high.astype(jnp.float32)).astype(jnp.bfloat16)
                split_ref[e, pl.ds(t * rows, rows)] = high
                split_ref[e, pl.ds(tall + t * rows, rows)] = low

    total = None
    for e in range(pairs):
        both = jnp.dot(split_ref[e], masked_refs[e][0, 0], preferred_element_type=jnp.float32)
        both = both[:tall] + both[tall:]
        total = both if total is None else total + both
    for t in range(sections):
        out_ref[place_ref[0] ^ t, 0] = total[t * rows : (t + 1) * rows]


def product(place, own, mirrored, masked, start, after):
    sections, pairs = len(mirrored), len(mirrored[0])
    rows, virtuals = mirrored[0][0].shape
    slots = masked.shape[0]
    deep = virtuals // sections
    wide = min(virtuals, 512)
    return call(
        functools.partial(product_kernel, sections, pairs),
        "product",
        place,
        [own] * (sections * pairs) + sum(mirrored, []) + [masked] * pairs + [after],
        [
            pl.BlockSpec(
                tuple(pl.Element(size) for size in (1, 1, rows, virtuals)),
                lambda s, n, at, t=t, e=e: (
                    0,
                    at[2] ^ e,
                    pl.multiple_of((at[0] ^ t) * deep + start, 8),
                    0,
                ),
            )
            for t in range(sections)
            for e in range(pairs)
        ]
        + [whole((rows, virtuals))] * (sections * pairs)
        + [
            pl.BlockSpec((1, 1, virtuals, wide), lambda s, n, at, e=e: (s, at[2] ^ e, 0, n))
            for e in range(pairs)
        ]
        + [pl.BlockSpec(memory_space=pl.ANY)],
        pl.BlockSpec((sections, 1, rows, wide), lambda s, n, at: (0, s, 0, n)),
        jax.ShapeDtypeStruct((sections, slots, rows, virtuals), jnp.float32),
        (slots, virtuals // wide),
        scratch=[pltpu.VMEM((pairs, 2 * sections * rows, virtuals), jnp.bfloat16)],
        flops=4 * sections * rows * pairs * virtuals * virtuals * slots,
    )


def cut_kernel(chunks, place_ref, *refs):
    total_refs, cut_refs = refs[:chunks], refs[chunks:]
    parts, _, _, wide = cut_refs[0].shape
    for e, cut_ref in enumerate(cut_refs):
        columns = pl.ds(pl.multiple_of((place_ref[0] ^ e) * wide, wide), wide)
        at = 0
        for total_ref in total_refs:
            short = total_ref.shape[1] // parts
            for part in range(parts):
                cut_ref[part, :, at : at + short] = total_ref[
                    :, part * short : (part + 1) * short, columns
                ]
            at += short


def cut(place, totals, sections, parts):
    slots, _, virtuals = totals[0].shape
    rows = sum(total.shape[1] for total in totals)
    shape = (parts, slots, rows // parts, virtuals // sections)
    return call(
        functools.partial(cut_kernel, len(totals)),
        "cut",
        place,
        totals,
        [whole(total.shape) for total in totals],
        [whole(shape)] * sections,
        [jax.ShapeDtypeStruct(shape, jnp.float32)] * sections,
        (1,),
    )


def finish_kernel(spans, groups, place_ref, *refs):
    chunks = len(spans)
    own_refs, delivered_refs = refs[:chunks], refs[chunks : chunks + len(groups)]
    out_ref, columns_ref = refs[chunks + len(groups) :]
    wide = out_ref.shape[2]
    sections = columns_ref.shape[0] // wide
    for group, delivered_ref in zip(groups, delivered_refs):
        parts = delivered_ref.shape[0] // sections
        for e in range(sections):
            base = (place_ref[0] ^ e) * wide
            for part in range(parts):
                at = 0
                for chunk in group:
                    start, rows = spans[chunk]
                    short = rows // parts
                    spot = pl.multiple_of(base + start + part * short, 8)
                    columns_ref[pl.ds(spot, short)] = delivered_ref[
                        e * parts + part, 0, at : at + short
                    ]
                    at += short
    turned = columns_ref[...].T
    for (start, rows), own_ref in zip(spans, own_refs):
        out_ref[0, 0, start : start + rows] = own_ref[0] + turned[start : start + rows]


def finish(place, spans, groups, own, delivered):
    slots, _, virtuals = own[0].shape
    wide = delivered[0].shape[-1]
    return call(
        functools.partial(finish_kernel, spans, groups),
        "finish",
        place,
        list(own) + list(delivered),
        [pl.BlockSpec((1, *x.shape[1:]), lambda s, at: (s, 0, 0)) for x in own]
        + [
            pl.BlockSpec((x.shape[0], 1, *x.shape[2:]), lambda s, at: (0, s, 0, 0))
            for x in delivered
        ],
        pl.BlockSpec((1, 1, wide, virtuals), lambda s, at: (0, s, 0, 0)),
        jax.ShapeDtypeStruct((1, slots, wide, virtuals), jnp.float32),
        (slots,),
        scratch=[pltpu.VMEM((virtuals, wide), jnp.float32)],
    )


def swap(array, axis):
    return lax.all_to_all(array, axis, split_axis=0, concat_axis=0, tiled=True)


def route(array, sections, pairs, move):
    moves = []
    for plane in range(sections):
        for core in range(pairs):
            for line in range(sections):
                to_plane, to_core, to_line = move(plane, core, line)
                source = (plane * pairs + core) * sections + line
                moves.append((source, (to_plane * pairs + to_core) * sections + to_line))
    return lax.ppermute(array, ("ia", "ka"), moves)


def spread(pieces):
    count = len(pieces)
    return [pieces[0]] + [
        lax.ppermute(pieces[e], "ka", [(q, q ^ e) for q in range(count)]) for e in range(1, count)
    ]


def body(sections, amplitudes, integrals, tile_mask, pair_list):
    _, pairs, virtuals, _ = amplitudes.shape
    occupied, slots = pair_list.shape
    wide = virtuals // sections
    sizes = [wide * part // sum(CHUNKS) for part in CHUNKS]
    spans = [(sum(sizes[:at]), size) for at, size in enumerate(sizes)]
    here, there = lax.axis_index("ka"), lax.axis_index("ia")
    place = jnp.stack([here, there // pairs, there % pairs]).astype(jnp.int32)

    owners = jnp.arange(occupied, dtype=jnp.int32)
    partner_slot = jnp.where(pair_list[pair_list, 0] == owners[:, None], 0, 1).astype(jnp.int32)
    source_row = (pair_list * slots + partner_slot).reshape(-1)

    masked = mask_blocks(integrals, tile_mask)
    own, after, partial_rows = [], place, masked
    for start, rows in spans:
        mirrored = []
        for t in range(sections):
            landed = []
            pieces = flip(place, amplitudes, sections, t, (start, rows), after)
            after = pieces[0]
            for e, piece in enumerate(pieces):
                piece = route(piece, sections, pairs, lambda a, c, q: (q, c ^ e, a ^ t))
                landed.append(piece)
                if t > 0:
                    landed[-1] = route(piece, sections, pairs, lambda q, c, l: (q, c, l ^ t))
            mirrored.append(landed)
        partial_rows = product(place, amplitudes, mirrored, masked, start, partial_rows)
        own.append(lax.psum_scatter(partial_rows, "ka", scatter_dimension=0, tiled=False))

    delivered, after = [], partial_rows
    for group in GROUPS:
        columns = spread(cut(place, [own[at] for at in group], sections, pairs))
        columns = gather(place, columns, after, ordered=False)
        piece = columns.shape[-2:]
        met = after = swap(columns.reshape(occupied, slots, *piece), "ia")
        routed = jnp.take(met.reshape(occupied * slots, *piece), source_row, axis=0)
        delivered.append(swap(routed.reshape(occupied, slots, *piece), "ia"))
    return finish(place, spans, GROUPS, own, delivered)


def solution(mesh):
    placed = (
        P("ia", "ka", None, None),
        P("ia", None, "ka", None, None),
        P("ia", None, "ka", None, None),
        P(),
    )
    return jax.shard_map(
        functools.partial(body, mesh.shape["ka"]),
        mesh=mesh,
        in_specs=placed,
        out_specs=P("ia", None, "ka", None),
        check_vma=False,
    )
```

```python
import functools

import jax
import jax.numpy as jnp
from jax import lax
from jax.experimental import pallas as pl
from jax.experimental.pallas import tpu as pltpu
from jax.sharding import PartitionSpec as P

CHUNKS = (3, 2, 2, 1)
GROUPS = ((0,), (1,), (2, 3))
LANES = 128
VMEM_BYTES = 48 * 1024 * 1024


def call(kernel, name, scalars, operands, in_specs, out_specs, out_shape, grid, scratch=(), flops=0):
    moved = sum(x.size * x.dtype.itemsize for x in jax.tree.leaves(out_shape)) * 2
    return pl.pallas_call(
        kernel,
        grid_spec=pltpu.PrefetchScalarGridSpec(
            num_scalar_prefetch=1,
            grid=grid,
            in_specs=in_specs,
            out_specs=out_specs,
            scratch_shapes=list(scratch),
        ),
        out_shape=out_shape,
        compiler_params=pltpu.CompilerParams(vmem_limit_bytes=VMEM_BYTES),
        cost_estimate=pl.CostEstimate(flops=flops, bytes_accessed=moved, transcendentals=0),
        name=name,
    )(scalars, *operands)


def whole(shape):
    return pl.BlockSpec(shape, lambda *_: (0,) * len(shape))


def first_flip_kernel(place_ref, blocks_ref, piece_ref):
    piece_ref[0, 0] = blocks_ref[0, 0].T[: piece_ref.shape[2]]


def first_flip(place, amplitudes, sections, rows):
    pairs, virtuals = amplitudes.shape[1], amplitudes.shape[3]
    steps = virtuals // sections // LANES
    return call(
        first_flip_kernel,
        "first_flip",
        place,
        [amplitudes],
        [pl.BlockSpec((1, 1, virtuals, LANES), lambda d, q, at: (0, d, 0, q * steps))],
        pl.BlockSpec((1, 1, rows, virtuals), lambda d, q, at: (q, d, 0, 0)),
        jax.ShapeDtypeStruct((sections, pairs, rows, virtuals), jnp.float32),
        (pairs, sections),
    )


def flip_kernel(place_ref, blocks_ref, after_ref, piece_ref):
    wide = blocks_ref.shape[-1]
    piece_ref[0] = blocks_ref[0, 0].T[wide - piece_ref.shape[1] :]


def flip(place, amplitudes, sections, e, rows, after):
    pairs, virtuals = amplitudes.shape[1], amplitudes.shape[3]
    wide = virtuals // sections
    return call(
        flip_kernel,
        "flip",
        place,
        [amplitudes, after],
        [
            pl.BlockSpec((1, 1, virtuals, wide), lambda d, at: (0, d, 0, at[0] ^ e)),
            pl.BlockSpec(memory_space=pl.ANY),
        ],
        pl.BlockSpec((1, rows, virtuals), lambda d, at: (d, 0, 0)),
        jax.ShapeDtypeStruct((pairs, rows, virtuals), jnp.float32),
        (pairs,),
    )


def part_kernel(count, place_ref, *refs):
    pieces, out_refs = refs[:count], refs[count:]
    for e, piece in enumerate(pieces):
        at = 0
        for out_ref in out_refs:
            rows = out_ref.shape[2]
            out_ref[place_ref[0] ^ e, 0] = piece[0, at : at + rows]
            at += rows


def part(place, pieces, sizes):
    count, (pairs, rows, virtuals) = len(pieces), pieces[0].shape
    return call(
        functools.partial(part_kernel, count),
        "part",
        place,
        pieces,
        [pl.BlockSpec((1, rows, virtuals), lambda d, at: (d, 0, 0))] * count,
        [pl.BlockSpec((count, 1, size, virtuals), lambda d, at: (0, d, 0, 0)) for size in sizes],
        [jax.ShapeDtypeStruct((count, pairs, size, virtuals), jnp.float32) for size in sizes],
        (pairs,),
    )


def gather_kernel(place_ref, *refs):
    pieces, out_ref = refs[:-2], refs[-1]
    for e, piece in enumerate(pieces):
        out_ref[e] = piece[...]


def gather(place, pieces, after):
    shape = (len(pieces), *pieces[0].shape)
    return call(
        gather_kernel,
        "gather",
        place,
        [*pieces, after],
        [whole(pieces[0].shape)] * len(pieces) + [pl.BlockSpec(memory_space=pl.ANY)],
        whole(shape),
        jax.ShapeDtypeStruct(shape, jnp.float32),
        (1,),
    )


def scatter_kernel(place_ref, stacked_ref, after_ref, *pieces):
    for e, piece in enumerate(pieces):
        piece[...] = stacked_ref[place_ref[0] ^ e]


def scatter(place, stacked, after):
    count, shape = stacked.shape[0], stacked.shape[1:]
    return call(
        scatter_kernel,
        "scatter",
        place,
        [stacked, after],
        [whole(stacked.shape), pl.BlockSpec(memory_space=pl.ANY)],
        [whole(shape)] * count,
        [jax.ShapeDtypeStruct(shape, jnp.float32)] * count,
        (1,),
    )


def mask_kernel(tiles, mask_ref, integrals_ref, masked_ref):
    side = integrals_ref.shape[-1] // tiles
    slot, pair = pl.program_id(0), pl.program_id(1)
    for r in range(tiles):
        for c in range(tiles):
            keep = mask_ref[slot, pair, r, c] != 0
            spot = (pl.ds(r * side, side), pl.ds(c * side, side))
            tile = integrals_ref[0, 0, 0, spot[0], spot[1]]
            masked_ref[0, 0, spot[0], spot[1]] = jnp.where(keep, tile, jnp.zeros_like(tile))


def mask_blocks(integrals, tile_mask):
    _, slots, pairs, virtuals, _ = integrals.shape
    out_shape = jax.ShapeDtypeStruct((slots, pairs, virtuals, virtuals), jnp.bfloat16)
    return call(
        functools.partial(mask_kernel, tile_mask.shape[-1]),
        "mask",
        tile_mask[0],
        [integrals],
        [pl.BlockSpec((1, 1, 1, virtuals, virtuals), lambda s, k, mask: (0, s, k, 0, 0))],
        pl.BlockSpec((1, 1, virtuals, virtuals), lambda s, k, mask: (s, k, 0, 0)),
        out_shape,
        (slots, pairs),
    )


def product_kernel(sections, place_ref, *refs):
    own_refs, mirrored_refs, refs = refs[:sections], refs[sections : 2 * sections], refs[2 * sections :]
    masked_ref, _, out_ref, split_ref = refs
    pairs, rows, _ = mirrored_refs[0].shape
    tall = sections * rows

    @pl.when((pl.program_id(0) == 0) & (pl.program_id(1) == 0))
    def _():
        for e in range(sections):
            for k in range(pairs):
                mixed = 2.0 * own_refs[e][0, k] - mirrored_refs[e][k]
                high = mixed.astype(jnp.bfloat16)
                low = (mixed - high.astype(jnp.float32)).astype(jnp.bfloat16)
                split_ref[k, pl.ds(e * rows, rows)] = high
                split_ref[k, pl.ds(tall + e * rows, rows)] = low

    total = None
    for k in range(pairs):
        both = jnp.dot(split_ref[k], masked_ref[0, k], preferred_element_type=jnp.float32)
        both = both[:tall] + both[tall:]
        total = both if total is None else total + both
    for e in range(sections):
        out_ref[place_ref[0] ^ e, 0] = total[e * rows : (e + 1) * rows]


def product(place, own, mirrored, masked, start, after):
    sections = len(mirrored)
    pairs, rows, virtuals = mirrored[0].shape
    slots = masked.shape[0]
    deep = virtuals // sections
    wide = min(virtuals, 512)
    return call(
        functools.partial(product_kernel, sections),
        "product",
        place,
        [own] * sections + list(mirrored) + [masked, after],
        [
            pl.BlockSpec(
                tuple(pl.Element(size) for size in (1, pairs, rows, virtuals)),
                lambda s, n, at, e=e: (0, 0, pl.multiple_of((at[0] ^ e) * deep + start, 8), 0),
            )
            for e in range(sections)
        ]
        + [whole(mirrored[0].shape)] * sections
        + [
            pl.BlockSpec((1, pairs, virtuals, wide), lambda s, n, at: (s, 0, 0, n)),
            pl.BlockSpec(memory_space=pl.ANY),
        ],
        pl.BlockSpec((sections, 1, rows, wide), lambda s, n, at: (0, s, 0, n)),
        jax.ShapeDtypeStruct((sections, slots, rows, virtuals), jnp.float32),
        (slots, virtuals // wide),
        scratch=[pltpu.VMEM((pairs, 2 * sections * rows, virtuals), jnp.bfloat16)],
        flops=4 * sections * rows * pairs * virtuals * virtuals * slots,
    )


def cut_kernel(chunks, place_ref, *refs):
    total_refs, cut_refs = refs[:chunks], refs[chunks:]
    parts, _, _, wide = cut_refs[0].shape
    for e, cut_ref in enumerate(cut_refs):
        columns = pl.ds(pl.multiple_of((place_ref[0] ^ e) * wide, wide), wide)
        at = 0
        for total_ref in total_refs:
            short = total_ref.shape[1] // parts
            for part in range(parts):
                cut_ref[part, :, at : at + short] = total_ref[
                    :, part * short : (part + 1) * short, columns
                ]
            at += short


def cut(place, totals, sections, parts):
    slots, _, virtuals = totals[0].shape
    rows = sum(total.shape[1] for total in totals)
    shape = (parts, slots, rows // parts, virtuals // sections)
    return call(
        functools.partial(cut_kernel, len(totals)),
        "cut",
        place,
        totals,
        [whole(total.shape) for total in totals],
        [whole(shape)] * sections,
        [jax.ShapeDtypeStruct(shape, jnp.float32)] * sections,
        (1,),
    )


def finish_kernel(spans, groups, place_ref, *refs):
    chunks = len(spans)
    own_refs, delivered_refs = refs[:chunks], refs[chunks : chunks + len(groups)]
    out_ref, columns_ref = refs[chunks + len(groups) :]
    wide = out_ref.shape[2]
    sections = columns_ref.shape[0] // wide
    for group, delivered_ref in zip(groups, delivered_refs):
        parts = delivered_ref.shape[0] // sections
        for e in range(sections):
            base = (place_ref[0] ^ e) * wide
            for part in range(parts):
                at = 0
                for chunk in group:
                    start, rows = spans[chunk]
                    short = rows // parts
                    spot = pl.multiple_of(base + start + part * short, 8)
                    columns_ref[pl.ds(spot, short)] = delivered_ref[
                        e * parts + part, 0, at : at + short
                    ]
                    at += short
    turned = columns_ref[...].T
    for (start, rows), own_ref in zip(spans, own_refs):
        out_ref[0, 0, start : start + rows] = own_ref[0] + turned[start : start + rows]


def finish(place, spans, groups, own, delivered):
    slots, _, virtuals = own[0].shape
    wide = delivered[0].shape[-1]
    return call(
        functools.partial(finish_kernel, spans, groups),
        "finish",
        place,
        list(own) + list(delivered),
        [pl.BlockSpec((1, *x.shape[1:]), lambda s, at: (s, 0, 0)) for x in own]
        + [
            pl.BlockSpec((x.shape[0], 1, *x.shape[2:]), lambda s, at: (0, s, 0, 0))
            for x in delivered
        ],
        pl.BlockSpec((1, 1, wide, virtuals), lambda s, at: (0, s, 0, 0)),
        jax.ShapeDtypeStruct((1, slots, wide, virtuals), jnp.float32),
        (slots,),
        scratch=[pltpu.VMEM((virtuals, wide), jnp.float32)],
    )


def swap(array, axis):
    return lax.all_to_all(array, axis, split_axis=0, concat_axis=0, tiled=True)


def spread(pieces):
    count = len(pieces)
    return [pieces[0]] + [
        lax.ppermute(pieces[e], "ka", [(q, q ^ e) for q in range(count)]) for e in range(1, count)
    ]


def body(sections, amplitudes, integrals, tile_mask, pair_list):
    _, pairs, virtuals, _ = amplitudes.shape
    occupied, slots = pair_list.shape
    wide = virtuals // sections
    sizes = [wide * part // sum(CHUNKS) for part in CHUNKS]
    spans = [(sum(sizes[:at]), size) for at, size in enumerate(sizes)]
    place = lax.axis_index("ka").astype(jnp.int32).reshape(1)

    owners = jnp.arange(occupied, dtype=jnp.int32)
    partner_slot = jnp.where(pair_list[pair_list, 0] == owners[:, None], 0, 1).astype(jnp.int32)
    source_row = (pair_list * slots + partner_slot).reshape(-1)

    first = first_flip(place, amplitudes, sections, sizes[0])
    rest = [flip(place, amplitudes, sections, e, sum(sizes[1:]), first) for e in range(sections)]
    across = [swap(first, "ka"), *part(place, spread(rest), sizes[1:])]
    masked = mask_blocks(integrals, tile_mask)

    own, returned, partial_rows = [], [place], masked
    for (start, rows), sent in zip(spans, across):
        crossed = swap(sent.reshape(occupied, rows, virtuals), "ia")
        crossed = crossed.reshape(sections, pairs, rows, virtuals)
        returned = scatter(place, crossed, returned[0])
        mirrored = spread(returned)
        partial_rows = product(place, amplitudes, mirrored, masked, start, partial_rows)
        own.append(lax.psum_scatter(partial_rows, "ka", scatter_dimension=0, tiled=False))

    delivered, after = [], returned[0]
    for group in GROUPS:
        columns = spread(cut(place, [own[at] for at in group], sections, pairs))
        columns = gather(place, columns, after)
        piece = columns.shape[-2:]
        met = after = swap(columns.reshape(occupied, slots, *piece), "ia")
        routed = jnp.take(met.reshape(occupied * slots, *piece), source_row, axis=0)
        delivered.append(swap(routed.reshape(occupied, slots, *piece), "ia"))
    return finish(place, spans, GROUPS, own, delivered)


def solution(mesh):
    placed = (
        P("ia", "ka", None, None),
        P("ia", None, "ka", None, None),
        P("ia", None, "ka", None, None),
        P(),
    )
    return jax.shard_map(
        functools.partial(body, mesh.shape["ka"]),
        mesh=mesh,
        in_specs=placed,
        out_specs=P("ia", None, "ka", None),
        check_vma=False,
    )
```

```python
import functools

import jax
import jax.numpy as jnp
from jax import lax
from jax.experimental import pallas as pl
from jax.experimental.pallas import tpu as pltpu
from jax.sharding import PartitionSpec as P

CHUNKS = (3, 2, 2, 1)
GROUPS = ((0,), (1,), (2, 3))
LANES = 128
VMEM_BYTES = 48 * 1024 * 1024


def call(kernel, name, scalars, operands, in_specs, out_specs, out_shape, grid, scratch=(), flops=0):
    moved = sum(x.size * x.dtype.itemsize for x in jax.tree.leaves(out_shape)) * 2
    return pl.pallas_call(
        kernel,
        grid_spec=pltpu.PrefetchScalarGridSpec(
            num_scalar_prefetch=1,
            grid=grid,
            in_specs=in_specs,
            out_specs=out_specs,
            scratch_shapes=list(scratch),
        ),
        out_shape=out_shape,
        compiler_params=pltpu.CompilerParams(vmem_limit_bytes=VMEM_BYTES),
        cost_estimate=pl.CostEstimate(flops=flops, bytes_accessed=moved, transcendentals=0),
        name=name,
    )(scalars, *operands)


def whole(shape):
    return pl.BlockSpec(shape, lambda *_: (0,) * len(shape))


def first_flip_kernel(place_ref, blocks_ref, piece_ref):
    piece_ref[0, 0] = blocks_ref[0, 0].T[: piece_ref.shape[2]]


def first_flip(place, amplitudes, sections, rows):
    pairs, virtuals = amplitudes.shape[1], amplitudes.shape[3]
    steps = virtuals // sections // LANES
    return call(
        first_flip_kernel,
        "first_flip",
        place,
        [amplitudes],
        [pl.BlockSpec((1, 1, virtuals, LANES), lambda d, q, at: (0, d, 0, q * steps))],
        pl.BlockSpec((1, 1, rows, virtuals), lambda d, q, at: (q, d, 0, 0)),
        jax.ShapeDtypeStruct((sections, pairs, rows, virtuals), jnp.float32),
        (pairs, sections),
    )


def flip_kernel(place_ref, blocks_ref, after_ref, piece_ref):
    wide = blocks_ref.shape[-1]
    piece_ref[0] = blocks_ref[0, 0].T[wide - piece_ref.shape[1] :]


def flip(place, amplitudes, sections, e, rows, after):
    pairs, virtuals = amplitudes.shape[1], amplitudes.shape[3]
    wide = virtuals // sections
    return call(
        flip_kernel,
        "flip",
        place,
        [amplitudes, after],
        [
            pl.BlockSpec((1, 1, virtuals, wide), lambda d, at: (0, d, 0, at[0] ^ e)),
            pl.BlockSpec(memory_space=pl.ANY),
        ],
        pl.BlockSpec((1, rows, virtuals), lambda d, at: (d, 0, 0)),
        jax.ShapeDtypeStruct((pairs, rows, virtuals), jnp.float32),
        (pairs,),
    )


def part_kernel(count, place_ref, *refs):
    pieces, out_refs = refs[:count], refs[count:]
    for e, piece in enumerate(pieces):
        at = 0
        for out_ref in out_refs:
            rows = out_ref.shape[2]
            out_ref[place_ref[0] ^ e, 0] = piece[0, at : at + rows]
            at += rows


def part(place, pieces, sizes):
    count, (pairs, rows, virtuals) = len(pieces), pieces[0].shape
    return call(
        functools.partial(part_kernel, count),
        "part",
        place,
        pieces,
        [pl.BlockSpec((1, rows, virtuals), lambda d, at: (d, 0, 0))] * count,
        [pl.BlockSpec((count, 1, size, virtuals), lambda d, at: (0, d, 0, 0)) for size in sizes],
        [jax.ShapeDtypeStruct((count, pairs, size, virtuals), jnp.float32) for size in sizes],
        (pairs,),
    )


def gather_kernel(place_ref, *refs):
    pieces, out_ref = refs[:-2], refs[-1]
    for e, piece in enumerate(pieces):
        out_ref[e] = piece[...]


def gather(place, pieces, after):
    shape = (len(pieces), *pieces[0].shape)
    return call(
        gather_kernel,
        "gather",
        place,
        [*pieces, after],
        [whole(pieces[0].shape)] * len(pieces) + [pl.BlockSpec(memory_space=pl.ANY)],
        whole(shape),
        jax.ShapeDtypeStruct(shape, jnp.float32),
        (1,),
    )


def scatter_kernel(place_ref, stacked_ref, after_ref, *pieces):
    for e, piece in enumerate(pieces):
        piece[...] = stacked_ref[place_ref[0] ^ e]


def scatter(place, stacked, after):
    count, shape = stacked.shape[0], stacked.shape[1:]
    return call(
        scatter_kernel,
        "scatter",
        place,
        [stacked, after],
        [whole(stacked.shape), pl.BlockSpec(memory_space=pl.ANY)],
        [whole(shape)] * count,
        [jax.ShapeDtypeStruct(shape, jnp.float32)] * count,
        (1,),
    )


def mask_kernel(tiles, mask_ref, integrals_ref, after_ref, masked_ref):
    side = integrals_ref.shape[-1] // tiles
    slot, pair = pl.program_id(0), pl.program_id(1)
    for r in range(tiles):
        for c in range(tiles):
            keep = mask_ref[slot, pair, r, c] != 0
            spot = (pl.ds(r * side, side), pl.ds(c * side, side))
            tile = integrals_ref[0, 0, 0, spot[0], spot[1]]
            masked_ref[0, 0, spot[0], spot[1]] = jnp.where(keep, tile, jnp.zeros_like(tile))


def mask_blocks(integrals, tile_mask, after):
    _, slots, pairs, virtuals, _ = integrals.shape
    out_shape = jax.ShapeDtypeStruct((slots, pairs, virtuals, virtuals), jnp.bfloat16)
    return call(
        functools.partial(mask_kernel, tile_mask.shape[-1]),
        "mask",
        tile_mask[0],
        [integrals, after],
        [
            pl.BlockSpec((1, 1, 1, virtuals, virtuals), lambda s, k, mask: (0, s, k, 0, 0)),
            pl.BlockSpec(memory_space=pl.ANY),
        ],
        pl.BlockSpec((1, 1, virtuals, virtuals), lambda s, k, mask: (s, k, 0, 0)),
        out_shape,
        (slots, pairs),
    )


def product_kernel(sections, place_ref, *refs):
    own_refs, mirrored_refs, refs = refs[:sections], refs[sections : 2 * sections], refs[2 * sections :]
    masked_ref, _, out_ref, split_ref = refs
    pairs, rows, _ = mirrored_refs[0].shape
    tall = sections * rows

    @pl.when((pl.program_id(0) == 0) & (pl.program_id(1) == 0))
    def _():
        for e in range(sections):
            for k in range(pairs):
                mixed = 2.0 * own_refs[e][0, k] - mirrored_refs[e][k]
                high = mixed.astype(jnp.bfloat16)
                low = (mixed - high.astype(jnp.float32)).astype(jnp.bfloat16)
                split_ref[k, pl.ds(e * rows, rows)] = high
                split_ref[k, pl.ds(tall + e * rows, rows)] = low

    total = None
    for k in range(pairs):
        both = jnp.dot(split_ref[k], masked_ref[0, k], preferred_element_type=jnp.float32)
        both = both[:tall] + both[tall:]
        total = both if total is None else total + both
    for e in range(sections):
        out_ref[place_ref[0] ^ e, 0] = total[e * rows : (e + 1) * rows]


def product(place, own, mirrored, masked, start, after):
    sections = len(mirrored)
    pairs, rows, virtuals = mirrored[0].shape
    slots = masked.shape[0]
    deep = virtuals // sections
    wide = min(virtuals, 512)
    return call(
        functools.partial(product_kernel, sections),
        "product",
        place,
        [own] * sections + list(mirrored) + [masked, after],
        [
            pl.BlockSpec(
                tuple(pl.Element(size) for size in (1, pairs, rows, virtuals)),
                lambda s, n, at, e=e: (0, 0, pl.multiple_of((at[0] ^ e) * deep + start, 8), 0),
            )
            for e in range(sections)
        ]
        + [whole(mirrored[0].shape)] * sections
        + [
            pl.BlockSpec((1, pairs, virtuals, wide), lambda s, n, at: (s, 0, 0, n)),
            pl.BlockSpec(memory_space=pl.ANY),
        ],
        pl.BlockSpec((sections, 1, rows, wide), lambda s, n, at: (0, s, 0, n)),
        jax.ShapeDtypeStruct((sections, slots, rows, virtuals), jnp.float32),
        (slots, virtuals // wide),
        scratch=[pltpu.VMEM((pairs, 2 * sections * rows, virtuals), jnp.bfloat16)],
        flops=4 * sections * rows * pairs * virtuals * virtuals * slots,
    )


def cut_kernel(chunks, place_ref, *refs):
    total_refs, cut_refs = refs[:chunks], refs[chunks:]
    parts, _, _, wide = cut_refs[0].shape
    for e, cut_ref in enumerate(cut_refs):
        columns = pl.ds(pl.multiple_of((place_ref[0] ^ e) * wide, wide), wide)
        at = 0
        for total_ref in total_refs:
            short = total_ref.shape[1] // parts
            for part in range(parts):
                cut_ref[part, :, at : at + short] = total_ref[
                    :, part * short : (part + 1) * short, columns
                ]
            at += short


def cut(place, totals, sections, parts):
    slots, _, virtuals = totals[0].shape
    rows = sum(total.shape[1] for total in totals)
    shape = (parts, slots, rows // parts, virtuals // sections)
    return call(
        functools.partial(cut_kernel, len(totals)),
        "cut",
        place,
        totals,
        [whole(total.shape) for total in totals],
        [whole(shape)] * sections,
        [jax.ShapeDtypeStruct(shape, jnp.float32)] * sections,
        (1,),
    )


def finish_kernel(spans, groups, place_ref, *refs):
    chunks = len(spans)
    own_refs, delivered_refs = refs[:chunks], refs[chunks : chunks + len(groups)]
    out_ref, columns_ref = refs[chunks + len(groups) :]
    wide = out_ref.shape[2]
    sections = columns_ref.shape[0] // wide
    for group, delivered_ref in zip(groups, delivered_refs):
        parts = delivered_ref.shape[0] // sections
        for e in range(sections):
            base = (place_ref[0] ^ e) * wide
            for part in range(parts):
                at = 0
                for chunk in group:
                    start, rows = spans[chunk]
                    short = rows // parts
                    spot = pl.multiple_of(base + start + part * short, 8)
                    columns_ref[pl.ds(spot, short)] = delivered_ref[
                        e * parts + part, 0, at : at + short
                    ]
                    at += short
    turned = columns_ref[...].T
    for (start, rows), own_ref in zip(spans, own_refs):
        out_ref[0, 0, start : start + rows] = own_ref[0] + turned[start : start + rows]


def finish(place, spans, groups, own, delivered):
    slots, _, virtuals = own[0].shape
    wide = delivered[0].shape[-1]
    return call(
        functools.partial(finish_kernel, spans, groups),
        "finish",
        place,
        list(own) + list(delivered),
        [pl.BlockSpec((1, *x.shape[1:]), lambda s, at: (s, 0, 0)) for x in own]
        + [
            pl.BlockSpec((x.shape[0], 1, *x.shape[2:]), lambda s, at: (0, s, 0, 0))
            for x in delivered
        ],
        pl.BlockSpec((1, 1, wide, virtuals), lambda s, at: (0, s, 0, 0)),
        jax.ShapeDtypeStruct((1, slots, wide, virtuals), jnp.float32),
        (slots,),
        scratch=[pltpu.VMEM((virtuals, wide), jnp.float32)],
    )


def swap(array, axis):
    return lax.all_to_all(array, axis, split_axis=0, concat_axis=0, tiled=True)


def spread(pieces):
    count = len(pieces)
    return [pieces[0]] + [
        lax.ppermute(pieces[e], "ka", [(q, q ^ e) for q in range(count)]) for e in range(1, count)
    ]


def body(sections, amplitudes, integrals, tile_mask, pair_list):
    _, pairs, virtuals, _ = amplitudes.shape
    occupied, slots = pair_list.shape
    wide = virtuals // sections
    sizes = [wide * part // sum(CHUNKS) for part in CHUNKS]
    spans = [(sum(sizes[:at]), size) for at, size in enumerate(sizes)]
    place = lax.axis_index("ka").astype(jnp.int32).reshape(1)

    owners = jnp.arange(occupied, dtype=jnp.int32)
    partner_slot = jnp.where(pair_list[pair_list, 0] == owners[:, None], 0, 1).astype(jnp.int32)
    source_row = (pair_list * slots + partner_slot).reshape(-1)

    first = first_flip(place, amplitudes, sections, sizes[0])
    rest = [flip(place, amplitudes, sections, e, sum(sizes[1:]), first) for e in range(sections)]
    across = [swap(first, "ka"), *part(place, spread(rest), sizes[1:])]
    masked = mask_blocks(integrals, tile_mask, across[1])

    own, delivered, after, partial_rows = [], [], across[1], masked

    def send(group, after):
        columns = spread(cut(place, [own[at] for at in group], sections, pairs))
        return gather(place, columns, after)

    def deliver(columns):
        piece = columns.shape[-2:]
        met = swap(columns.reshape(occupied, slots, *piece), "ia")
        routed = jnp.take(met.reshape(occupied * slots, *piece), source_row, axis=0)
        return swap(routed.reshape(occupied, slots, *piece), "ia")

    for at, ((start, rows), sent) in enumerate(zip(spans, across)):
        crossed = swap(sent.reshape(occupied, rows, virtuals), "ia")
        if at == len(spans) - 1:
            after = leading = send(GROUPS[0], after)
        returned = scatter(place, crossed.reshape(sections, pairs, rows, virtuals), after)
        after = returned[0]
        mirrored = spread(returned)
        partial_rows = product(place, amplitudes, mirrored, masked, start, partial_rows)
        own.append(lax.psum_scatter(partial_rows, "ka", scatter_dimension=0, tiled=False))

    delivered.append(deliver(leading))
    for group in GROUPS[1:]:
        delivered.append(deliver(send(group, delivered[-1])))
    return finish(place, spans, GROUPS, own, delivered)


def solution(mesh):
    placed = (
        P("ia", "ka", None, None),
        P("ia", None, "ka", None, None),
        P("ia", None, "ka", None, None),
        P(),
    )
    return jax.shard_map(
        functools.partial(body, mesh.shape["ka"]),
        mesh=mesh,
        in_specs=placed,
        out_specs=P("ia", None, "ka", None),
        check_vma=False,
    )
```

```python
import functools

import jax
import jax.numpy as jnp
from jax import lax
from jax.experimental import pallas as pl
from jax.experimental.pallas import tpu as pltpu
from jax.sharding import PartitionSpec as P

CHUNKS = (2, 3, 2, 1)
SETS = ((0,), (1,), (2, 3))
GROUPS = ((0,), (1, 2, 3))
LANES = 128
VMEM_BYTES = 48 * 1024 * 1024


def call(kernel, name, scalars, operands, in_specs, out_specs, out_shape, grid, scratch=(), flops=0):
    moved = sum(x.size * x.dtype.itemsize for x in jax.tree.leaves(out_shape)) * 2
    return pl.pallas_call(
        kernel,
        grid_spec=pltpu.PrefetchScalarGridSpec(
            num_scalar_prefetch=1,
            grid=grid,
            in_specs=in_specs,
            out_specs=out_specs,
            scratch_shapes=list(scratch),
        ),
        out_shape=out_shape,
        compiler_params=pltpu.CompilerParams(vmem_limit_bytes=VMEM_BYTES),
        cost_estimate=pl.CostEstimate(flops=flops, bytes_accessed=moved, transcendentals=0),
        name=name,
    )(scalars, *operands)


def whole(shape):
    return pl.BlockSpec(shape, lambda *_: (0,) * len(shape))


def first_flip_kernel(place_ref, blocks_ref, piece_ref):
    piece_ref[0, 0] = blocks_ref[0, 0].T[: piece_ref.shape[2]]


def first_flip(place, amplitudes, sections, rows):
    pairs, virtuals = amplitudes.shape[1], amplitudes.shape[3]
    steps = virtuals // sections // LANES
    return call(
        first_flip_kernel,
        "first_flip",
        place,
        [amplitudes],
        [pl.BlockSpec((1, 1, virtuals, LANES), lambda d, q, at: (0, d, 0, q * steps))],
        pl.BlockSpec((1, 1, rows, virtuals), lambda d, q, at: (q, d, 0, 0)),
        jax.ShapeDtypeStruct((sections, pairs, rows, virtuals), jnp.float32),
        (pairs, sections),
    )


def flip_kernel(start, place_ref, blocks_ref, after_ref, piece_ref):
    piece_ref[0] = blocks_ref[0, 0].T[start : start + piece_ref.shape[1]]


def flip(place, amplitudes, sections, e, start, rows, after):
    pairs, virtuals = amplitudes.shape[1], amplitudes.shape[3]
    wide = virtuals // sections
    return call(
        functools.partial(flip_kernel, start),
        "flip",
        place,
        [amplitudes, after],
        [
            pl.BlockSpec((1, 1, virtuals, wide), lambda d, at: (0, d, 0, at[0] ^ e)),
            pl.BlockSpec(memory_space=pl.ANY),
        ],
        pl.BlockSpec((1, rows, virtuals), lambda d, at: (d, 0, 0)),
        jax.ShapeDtypeStruct((pairs, rows, virtuals), jnp.float32),
        (pairs,),
    )


def part_kernel(count, place_ref, *refs):
    pieces, out_refs = refs[:count], refs[count + 1 :]
    for e, piece in enumerate(pieces):
        at = 0
        for out_ref in out_refs:
            rows = out_ref.shape[2]
            out_ref[place_ref[0] ^ e, 0] = piece[0, at : at + rows]
            at += rows


def part(place, pieces, sizes, after):
    count, (pairs, rows, virtuals) = len(pieces), pieces[0].shape
    return call(
        functools.partial(part_kernel, count),
        "part",
        place,
        [*pieces, after],
        [pl.BlockSpec((1, rows, virtuals), lambda d, at: (d, 0, 0))] * count
        + [pl.BlockSpec(memory_space=pl.ANY)],
        [pl.BlockSpec((count, 1, size, virtuals), lambda d, at: (0, d, 0, 0)) for size in sizes],
        [jax.ShapeDtypeStruct((count, pairs, size, virtuals), jnp.float32) for size in sizes],
        (pairs,),
    )


def gather_kernel(place_ref, *refs):
    pieces, out_ref = refs[:-2], refs[-1]
    for e, piece in enumerate(pieces):
        out_ref[e] = piece[...]


def gather(place, pieces, after):
    shape = (len(pieces), *pieces[0].shape)
    return call(
        gather_kernel,
        "gather",
        place,
        [*pieces, after],
        [whole(pieces[0].shape)] * len(pieces) + [pl.BlockSpec(memory_space=pl.ANY)],
        whole(shape),
        jax.ShapeDtypeStruct(shape, jnp.float32),
        (1,),
    )


def scatter_kernel(place_ref, stacked_ref, after_ref, *pieces):
    for e, piece in enumerate(pieces):
        piece[...] = stacked_ref[place_ref[0] ^ e]


def scatter(place, stacked, after):
    count, shape = stacked.shape[0], stacked.shape[1:]
    return call(
        scatter_kernel,
        "scatter",
        place,
        [stacked, after],
        [whole(stacked.shape), pl.BlockSpec(memory_space=pl.ANY)],
        [whole(shape)] * count,
        [jax.ShapeDtypeStruct(shape, jnp.float32)] * count,
        (1,),
    )


def mask_kernel(tiles, mask_ref, integrals_ref, after_ref, masked_ref):
    side = integrals_ref.shape[-1] // tiles
    slot, pair = pl.program_id(0), pl.program_id(1)
    for r in range(tiles):
        for c in range(tiles):
            keep = mask_ref[slot, pair, r, c] != 0
            spot = (pl.ds(r * side, side), pl.ds(c * side, side))
            tile = integrals_ref[0, 0, 0, spot[0], spot[1]]
            masked_ref[0, 0, spot[0], spot[1]] = jnp.where(keep, tile, jnp.zeros_like(tile))


def mask_blocks(integrals, tile_mask, after):
    _, slots, pairs, virtuals, _ = integrals.shape
    out_shape = jax.ShapeDtypeStruct((slots, pairs, virtuals, virtuals), jnp.bfloat16)
    return call(
        functools.partial(mask_kernel, tile_mask.shape[-1]),
        "mask",
        tile_mask[0],
        [integrals, after],
        [
            pl.BlockSpec((1, 1, 1, virtuals, virtuals), lambda s, k, mask: (0, s, k, 0, 0)),
            pl.BlockSpec(memory_space=pl.ANY),
        ],
        pl.BlockSpec((1, 1, virtuals, virtuals), lambda s, k, mask: (s, k, 0, 0)),
        out_shape,
        (slots, pairs),
    )


def product_kernel(sections, place_ref, *refs):
    own_refs, mirrored_refs, refs = refs[:sections], refs[sections : 2 * sections], refs[2 * sections :]
    masked_ref, out_refs, split_ref = refs[0], refs[2:-1], refs[-1]
    pairs, rows, _ = mirrored_refs[0].shape
    tall = sections * rows

    @pl.when((pl.program_id(0) == 0) & (pl.program_id(1) == 0))
    def _():
        for e in range(sections):
            for k in range(pairs):
                mixed = 2.0 * own_refs[e][0, k] - mirrored_refs[e][k]
                high = mixed.astype(jnp.bfloat16)
                low = (mixed - high.astype(jnp.float32)).astype(jnp.bfloat16)
                split_ref[k, pl.ds(e * rows, rows)] = high
                split_ref[k, pl.ds(tall + e * rows, rows)] = low

    total = None
    for k in range(pairs):
        both = jnp.dot(split_ref[k], masked_ref[0, k], preferred_element_type=jnp.float32)
        both = both[:tall] + both[tall:]
        total = both if total is None else total + both
    for e, out_ref in enumerate(out_refs):
        out_ref[0] = total[e * rows : (e + 1) * rows]


def product(place, own, mirrored, masked, start, after):
    sections = len(mirrored)
    pairs, rows, virtuals = mirrored[0].shape
    slots = masked.shape[0]
    deep = virtuals // sections
    wide = min(virtuals, 512)
    return call(
        functools.partial(product_kernel, sections),
        "product",
        place,
        [own] * sections + list(mirrored) + [masked, after],
        [
            pl.BlockSpec(
                tuple(pl.Element(size) for size in (1, pairs, rows, virtuals)),
                lambda s, n, at, e=e: (0, 0, pl.multiple_of((at[0] ^ e) * deep + start, 8), 0),
            )
            for e in range(sections)
        ]
        + [whole(mirrored[0].shape)] * sections
        + [
            pl.BlockSpec((1, pairs, virtuals, wide), lambda s, n, at: (s, 0, 0, n)),
            pl.BlockSpec(memory_space=pl.ANY),
        ],
        [pl.BlockSpec((1, rows, wide), lambda s, n, at: (s, 0, n))] * sections,
        [jax.ShapeDtypeStruct((slots, rows, virtuals), jnp.float32)] * sections,
        (slots, virtuals // wide),
        scratch=[pltpu.VMEM((pairs, 2 * sections * rows, virtuals), jnp.bfloat16)],
        flops=4 * sections * rows * pairs * virtuals * virtuals * slots,
    )


def add_kernel(place_ref, *refs):
    refs[-1][...] = sum((part[...] for part in refs[1:-1]), refs[0][...])


def add(place, parts):
    slots, rows, virtuals = parts[0].shape
    block = pl.BlockSpec((1, rows, virtuals), lambda s, at: (s, 0, 0))
    return call(
        add_kernel,
        "add",
        place,
        parts,
        [block] * len(parts),
        block,
        jax.ShapeDtypeStruct(parts[0].shape, jnp.float32),
        (slots,),
    )


def cut_kernel(chunks, place_ref, *refs):
    total_refs, cut_refs = refs[:chunks], refs[chunks:]
    parts, _, _, wide = cut_refs[0].shape
    for e, cut_ref in enumerate(cut_refs):
        columns = pl.ds(pl.multiple_of((place_ref[0] ^ e) * wide, wide), wide)
        at = 0
        for total_ref in total_refs:
            short = total_ref.shape[1] // parts
            for part in range(parts):
                cut_ref[part, :, at : at + short] = total_ref[
                    :, part * short : (part + 1) * short, columns
                ]
            at += short


def cut(place, totals, sections, parts):
    slots, _, virtuals = totals[0].shape
    rows = sum(total.shape[1] for total in totals)
    shape = (parts, slots, rows // parts, virtuals // sections)
    return call(
        functools.partial(cut_kernel, len(totals)),
        "cut",
        place,
        totals,
        [whole(total.shape) for total in totals],
        [whole(shape)] * sections,
        [jax.ShapeDtypeStruct(shape, jnp.float32)] * sections,
        (1,),
    )


def finish_kernel(spans, groups, place_ref, *refs):
    chunks = len(spans)
    own_refs, delivered_refs = refs[:chunks], refs[chunks : chunks + len(groups)]
    out_ref, columns_ref = refs[chunks + len(groups) :]
    wide = out_ref.shape[2]
    sections = columns_ref.shape[0] // wide
    for group, delivered_ref in zip(groups, delivered_refs):
        parts = delivered_ref.shape[0] // sections
        for e in range(sections):
            base = (place_ref[0] ^ e) * wide
            for part in range(parts):
                at = 0
                for chunk in group:
                    start, rows = spans[chunk]
                    short = rows // parts
                    spot = pl.multiple_of(base + start + part * short, 8)
                    columns_ref[pl.ds(spot, short)] = delivered_ref[
                        e * parts + part, 0, at : at + short
                    ]
                    at += short
    turned = columns_ref[...].T
    for (start, rows), own_ref in zip(spans, own_refs):
        out_ref[0, 0, start : start + rows] = own_ref[0] + turned[start : start + rows]


def finish(place, spans, groups, own, delivered):
    slots, _, virtuals = own[0].shape
    wide = delivered[0].shape[-1]
    return call(
        functools.partial(finish_kernel, spans, groups),
        "finish",
        place,
        list(own) + list(delivered),
        [pl.BlockSpec((1, *x.shape[1:]), lambda s, at: (s, 0, 0)) for x in own]
        + [
            pl.BlockSpec((x.shape[0], 1, *x.shape[2:]), lambda s, at: (0, s, 0, 0))
            for x in delivered
        ],
        pl.BlockSpec((1, 1, wide, virtuals), lambda s, at: (0, s, 0, 0)),
        jax.ShapeDtypeStruct((1, slots, wide, virtuals), jnp.float32),
        (slots,),
        scratch=[pltpu.VMEM((virtuals, wide), jnp.float32)],
    )


def swap(array, axis):
    return lax.all_to_all(array, axis, split_axis=0, concat_axis=0, tiled=True)


def spread(pieces):
    count = len(pieces)
    return [pieces[0]] + [
        lax.ppermute(pieces[e], "ka", [(q, q ^ e) for q in range(count)]) for e in range(1, count)
    ]


def body(sections, amplitudes, integrals, tile_mask, pair_list):
    _, pairs, virtuals, _ = amplitudes.shape
    occupied, slots = pair_list.shape
    wide = virtuals // sections
    sizes = [wide * part // sum(CHUNKS) for part in CHUNKS]
    spans = [(sum(sizes[:at]), size) for at, size in enumerate(sizes)]
    place = lax.axis_index("ka").astype(jnp.int32).reshape(1)

    owners = jnp.arange(occupied, dtype=jnp.int32)
    partner_slot = jnp.where(pair_list[pair_list, 0] == owners[:, None], 0, 1).astype(jnp.int32)
    source_row = (pair_list * slots + partner_slot).reshape(-1)

    def send(group, after):
        columns = spread(cut(place, [own[at] for at in group], sections, pairs))
        return gather(place, columns, after)

    def deliver(columns):
        piece = columns.shape[-2:]
        met = swap(columns.reshape(occupied, slots, *piece), "ia")
        routed = jnp.take(met.reshape(occupied * slots, *piece), source_row, axis=0)
        return swap(routed.reshape(occupied, slots, *piece), "ia")

    first = first_flip(place, amplitudes, sections, sizes[0])
    masked = mask_blocks(integrals, tile_mask, first)
    across = [swap(first, "ka")]
    tokens = [first, *across]
    for chunks, after in zip(SETS[1:], tokens):
        rows = [sizes[at] for at in chunks]
        pieces = [
            flip(place, amplitudes, sections, e, spans[chunks[0]][0], sum(rows), after)
            for e in range(sections)
        ]
        across += part(place, spread(pieces), rows, masked)
    ready = [across[chunks[0]] for chunks in SETS[1:]]

    own, delivered, partial_rows = [], [], [masked]
    for at, ((start, rows), sent) in enumerate(zip(spans, across)):
        crossed = swap(sent.reshape(occupied, rows, virtuals), "ia")
        after = ready[at] if at < len(ready) else crossed
        if at == len(spans) - 1:
            after = leading = send(GROUPS[0], crossed)
        returned = scatter(place, crossed.reshape(sections, pairs, rows, virtuals), after)
        partial_rows = product(
            place, amplitudes, spread(returned), masked, start, partial_rows[0]
        )
        own.append(add(place, spread(partial_rows)))

    delivered.append(deliver(leading))
    for group in GROUPS[1:]:
        delivered.append(deliver(send(group, delivered[-1])))
    return finish(place, spans, GROUPS, own, delivered)


def solution(mesh):
    placed = (
        P("ia", "ka", None, None),
        P("ia", None, "ka", None, None),
        P("ia", None, "ka", None, None),
        P(),
    )
    return jax.shard_map(
        functools.partial(body, mesh.shape["ka"]),
        mesh=mesh,
        in_specs=placed,
        out_specs=P("ia", None, "ka", None),
        check_vma=False,
    )
```

```python
import functools

import jax
import jax.numpy as jnp
from jax import lax
from jax.experimental import pallas as pl
from jax.experimental.pallas import tpu as pltpu
from jax.sharding import PartitionSpec as P

CHUNKS = (2, 3, 2, 1)
SETS = ((0,), (1,), (2, 3))
GROUPS = ((0,), (1,), (2, 3))
LANES = 128
VMEM_BYTES = 48 * 1024 * 1024


def call(
    kernel, name, scalars, operands, in_specs, out_specs, out_shape, grid, scratch=(), flops=0, after=()
):
    moved = sum(x.size * x.dtype.itemsize for x in jax.tree.leaves(out_shape)) * 2
    reads = 1 + len(operands)

    def trimmed(*refs):
        kernel(*refs[:reads], *refs[reads + len(after) :])

    return pl.pallas_call(
        trimmed,
        grid_spec=pltpu.PrefetchScalarGridSpec(
            num_scalar_prefetch=1,
            grid=grid,
            in_specs=list(in_specs) + [pl.BlockSpec(memory_space=pl.ANY)] * len(after),
            out_specs=out_specs,
            scratch_shapes=list(scratch),
        ),
        out_shape=out_shape,
        compiler_params=pltpu.CompilerParams(vmem_limit_bytes=VMEM_BYTES),
        cost_estimate=pl.CostEstimate(flops=flops, bytes_accessed=moved, transcendentals=0),
        name=name,
    )(scalars, *operands, *after)


def whole(shape):
    return pl.BlockSpec(shape, lambda *_: (0,) * len(shape))


def first_flip_kernel(place_ref, blocks_ref, piece_ref):
    piece_ref[0, 0] = blocks_ref[0, 0].T[: piece_ref.shape[2]]


def first_flip(place, amplitudes, sections, rows):
    pairs, virtuals = amplitudes.shape[1], amplitudes.shape[3]
    steps = virtuals // sections // LANES
    return call(
        first_flip_kernel,
        "first_flip",
        place,
        [amplitudes],
        [pl.BlockSpec((1, 1, virtuals, LANES), lambda d, q, at: (0, d, 0, q * steps))],
        pl.BlockSpec((1, 1, rows, virtuals), lambda d, q, at: (q, d, 0, 0)),
        jax.ShapeDtypeStruct((sections, pairs, rows, virtuals), jnp.float32),
        (pairs, sections),
    )


def flip_kernel(start, place_ref, blocks_ref, piece_ref):
    piece_ref[0] = blocks_ref[0, 0].T[start : start + piece_ref.shape[1]]


def flip(place, amplitudes, sections, e, start, rows, after):
    pairs, virtuals = amplitudes.shape[1], amplitudes.shape[3]
    wide = virtuals // sections
    return call(
        functools.partial(flip_kernel, start),
        "flip",
        place,
        [amplitudes],
        [pl.BlockSpec((1, 1, virtuals, wide), lambda d, at: (0, d, 0, at[0] ^ e))],
        pl.BlockSpec((1, rows, virtuals), lambda d, at: (d, 0, 0)),
        jax.ShapeDtypeStruct((pairs, rows, virtuals), jnp.float32),
        (pairs,),
        after=after,
    )


def part_kernel(start, place_ref, *refs):
    pieces, out_ref = refs[:-1], refs[-1]
    for e, piece in enumerate(pieces):
        out_ref[place_ref[0] ^ e, 0] = piece[0, start : start + out_ref.shape[2]]


def part(place, pieces, start, size, after):
    count, (pairs, rows, virtuals) = len(pieces), pieces[0].shape
    return call(
        functools.partial(part_kernel, start),
        "part",
        place,
        pieces,
        [pl.BlockSpec((1, rows, virtuals), lambda d, at: (d, 0, 0))] * count,
        pl.BlockSpec((count, 1, size, virtuals), lambda d, at: (0, d, 0, 0)),
        jax.ShapeDtypeStruct((count, pairs, size, virtuals), jnp.float32),
        (pairs,),
        after=after,
    )


def gather_kernel(place_ref, *refs):
    pieces, out_ref = refs[:-1], refs[-1]
    for e, piece in enumerate(pieces):
        out_ref[e] = piece[...]


def gather(place, pieces, after):
    shape = (len(pieces), *pieces[0].shape)
    return call(
        gather_kernel,
        "gather",
        place,
        pieces,
        [whole(pieces[0].shape)] * len(pieces),
        whole(shape),
        jax.ShapeDtypeStruct(shape, jnp.float32),
        (1,),
        after=after,
    )


def scatter_kernel(place_ref, stacked_ref, *pieces):
    for e, piece in enumerate(pieces):
        piece[...] = stacked_ref[place_ref[0] ^ e]


def scatter(place, stacked, after):
    count, shape = stacked.shape[0], stacked.shape[1:]
    return call(
        scatter_kernel,
        "scatter",
        place,
        [stacked],
        [whole(stacked.shape)],
        [whole(shape)] * count,
        [jax.ShapeDtypeStruct(shape, jnp.float32)] * count,
        (1,),
        after=after,
    )


def mask_kernel(tiles, mask_ref, integrals_ref, masked_ref):
    side = integrals_ref.shape[-1] // tiles
    slot, pair = pl.program_id(0), pl.program_id(1)
    for r in range(tiles):
        for c in range(tiles):
            keep = mask_ref[slot, pair, r, c] != 0
            spot = (pl.ds(r * side, side), pl.ds(c * side, side))
            tile = integrals_ref[0, 0, 0, spot[0], spot[1]]
            masked_ref[0, 0, spot[0], spot[1]] = jnp.where(keep, tile, jnp.zeros_like(tile))


def mask_blocks(integrals, tile_mask, after):
    _, slots, pairs, virtuals, _ = integrals.shape
    out_shape = jax.ShapeDtypeStruct((slots, pairs, virtuals, virtuals), jnp.bfloat16)
    return call(
        functools.partial(mask_kernel, tile_mask.shape[-1]),
        "mask",
        tile_mask[0],
        [integrals],
        [pl.BlockSpec((1, 1, 1, virtuals, virtuals), lambda s, k, mask: (0, s, k, 0, 0))],
        pl.BlockSpec((1, 1, virtuals, virtuals), lambda s, k, mask: (s, k, 0, 0)),
        out_shape,
        (slots, pairs),
        after=after,
    )


def product_kernel(sections, place_ref, *refs):
    own_refs, mirrored_refs, refs = refs[:sections], refs[sections : 2 * sections], refs[2 * sections :]
    masked_ref, out_refs, split_ref = refs[0], refs[1:-1], refs[-1]
    pairs, rows, _ = mirrored_refs[0].shape
    tall = sections * rows

    @pl.when((pl.program_id(0) == 0) & (pl.program_id(1) == 0))
    def _():
        for e in range(sections):
            for k in range(pairs):
                mixed = 2.0 * own_refs[e][0, k] - mirrored_refs[e][k]
                high = mixed.astype(jnp.bfloat16)
                low = (mixed - high.astype(jnp.float32)).astype(jnp.bfloat16)
                split_ref[k, pl.ds(e * rows, rows)] = high
                split_ref[k, pl.ds(tall + e * rows, rows)] = low

    total = None
    for k in range(pairs):
        both = jnp.dot(split_ref[k], masked_ref[0, k], preferred_element_type=jnp.float32)
        both = both[:tall] + both[tall:]
        total = both if total is None else total + both
    for e, out_ref in enumerate(out_refs):
        out_ref[0] = total[e * rows : (e + 1) * rows]


def product(place, own, mirrored, masked, start, after):
    sections = len(mirrored)
    pairs, rows, virtuals = mirrored[0].shape
    slots = masked.shape[0]
    deep = virtuals // sections
    wide = min(virtuals, 512)
    return call(
        functools.partial(product_kernel, sections),
        "product",
        place,
        [own] * sections + list(mirrored) + [masked],
        [
            pl.BlockSpec(
                tuple(pl.Element(size) for size in (1, pairs, rows, virtuals)),
                lambda s, n, at, e=e: (0, 0, pl.multiple_of((at[0] ^ e) * deep + start, 8), 0),
            )
            for e in range(sections)
        ]
        + [whole(mirrored[0].shape)] * sections
        + [pl.BlockSpec((1, pairs, virtuals, wide), lambda s, n, at: (s, 0, 0, n))],
        [pl.BlockSpec((1, rows, wide), lambda s, n, at: (s, 0, n))] * sections,
        [jax.ShapeDtypeStruct((slots, rows, virtuals), jnp.float32)] * sections,
        (slots, virtuals // wide),
        scratch=[pltpu.VMEM((pairs, 2 * sections * rows, virtuals), jnp.bfloat16)],
        flops=4 * sections * rows * pairs * virtuals * virtuals * slots,
        after=after,
    )


def add_kernel(place_ref, *refs):
    refs[-1][...] = sum((part[...] for part in refs[1:-1]), refs[0][...])


def add(place, parts):
    slots, rows, virtuals = parts[0].shape
    block = pl.BlockSpec((1, rows, virtuals), lambda s, at: (s, 0, 0))
    return call(
        add_kernel,
        "add",
        place,
        parts,
        [block] * len(parts),
        block,
        jax.ShapeDtypeStruct(parts[0].shape, jnp.float32),
        (slots,),
    )


def cut_kernel(chunks, place_ref, *refs):
    total_refs, cut_refs = refs[:chunks], refs[chunks:]
    parts, _, _, wide = cut_refs[0].shape
    for e, cut_ref in enumerate(cut_refs):
        columns = pl.ds(pl.multiple_of((place_ref[0] ^ e) * wide, wide), wide)
        at = 0
        for total_ref in total_refs:
            short = total_ref.shape[1] // parts
            for part in range(parts):
                cut_ref[part, :, at : at + short] = total_ref[
                    :, part * short : (part + 1) * short, columns
                ]
            at += short


def cut(place, totals, sections, parts):
    slots, _, virtuals = totals[0].shape
    rows = sum(total.shape[1] for total in totals)
    shape = (parts, slots, rows // parts, virtuals // sections)
    return call(
        functools.partial(cut_kernel, len(totals)),
        "cut",
        place,
        totals,
        [whole(total.shape) for total in totals],
        [whole(shape)] * sections,
        [jax.ShapeDtypeStruct(shape, jnp.float32)] * sections,
        (1,),
    )


def finish_kernel(spans, groups, place_ref, *refs):
    chunks = len(spans)
    own_refs, delivered_refs = refs[:chunks], refs[chunks : chunks + len(groups)]
    out_ref, columns_ref = refs[chunks + len(groups) :]
    wide = out_ref.shape[2]
    sections = columns_ref.shape[0] // wide
    for group, delivered_ref in zip(groups, delivered_refs):
        parts = delivered_ref.shape[0] // sections
        for e in range(sections):
            base = (place_ref[0] ^ e) * wide
            for part in range(parts):
                at = 0
                for chunk in group:
                    start, rows = spans[chunk]
                    short = rows // parts
                    spot = pl.multiple_of(base + start + part * short, 8)
                    columns_ref[pl.ds(spot, short)] = delivered_ref[
                        e * parts + part, 0, at : at + short
                    ]
                    at += short
    turned = columns_ref[...].T
    for (start, rows), own_ref in zip(spans, own_refs):
        out_ref[0, 0, start : start + rows] = own_ref[0] + turned[start : start + rows]


def finish(place, spans, groups, own, delivered):
    slots, _, virtuals = own[0].shape
    wide = delivered[0].shape[-1]
    return call(
        functools.partial(finish_kernel, spans, groups),
        "finish",
        place,
        list(own) + list(delivered),
        [pl.BlockSpec((1, *x.shape[1:]), lambda s, at: (s, 0, 0)) for x in own]
        + [
            pl.BlockSpec((x.shape[0], 1, *x.shape[2:]), lambda s, at: (0, s, 0, 0))
            for x in delivered
        ],
        pl.BlockSpec((1, 1, wide, virtuals), lambda s, at: (0, s, 0, 0)),
        jax.ShapeDtypeStruct((1, slots, wide, virtuals), jnp.float32),
        (slots,),
        scratch=[pltpu.VMEM((virtuals, wide), jnp.float32)],
    )


def swap(array, axis):
    return lax.all_to_all(array, axis, split_axis=0, concat_axis=0, tiled=True)


def spread(pieces):
    count = len(pieces)
    return [pieces[0]] + [
        lax.ppermute(pieces[e], "ka", [(q, q ^ e) for q in range(count)]) for e in range(1, count)
    ]


def body(sections, amplitudes, integrals, tile_mask, pair_list):
    _, pairs, virtuals, _ = amplitudes.shape
    occupied, slots = pair_list.shape
    wide = virtuals // sections
    sizes = [wide * part // sum(CHUNKS) for part in CHUNKS]
    spans = [(sum(sizes[:at]), size) for at, size in enumerate(sizes)]
    place = lax.axis_index("ka").astype(jnp.int32).reshape(1)

    owners = jnp.arange(occupied, dtype=jnp.int32)
    partner_slot = jnp.where(pair_list[pair_list, 0] == owners[:, None], 0, 1).astype(jnp.int32)
    source_row = (pair_list * slots + partner_slot).reshape(-1)

    def fetch(chunks, after):
        start, rows = spans[chunks[0]][0], sum(sizes[at] for at in chunks)
        pieces = [flip(place, amplitudes, sections, e, start, rows, after) for e in range(sections)]
        pieces = spread(pieces)
        return [
            functools.partial(part, place, pieces, spans[at][0] - start, sizes[at]) for at in chunks
        ]

    def hop(at):
        crossed = swap(across[at].reshape(occupied, sizes[at], virtuals), "ia")
        return crossed.reshape(sections, pairs, sizes[at], virtuals)

    def multiply(at, returned, after):
        start = spans[at][0]
        return product(place, amplitudes, spread(returned), masked, start, after)

    def send(group):
        columns = cut(place, [own[at] for at in group], sections, pairs)
        return columns[0], lambda after: gather(place, spread(columns), after)

    def deliver(columns):
        piece = columns.shape[-2:]
        met = swap(columns.reshape(occupied, slots, *piece), "ia")
        routed = jnp.take(met.reshape(occupied * slots, *piece), source_row, axis=0)
        return swap(routed.reshape(occupied, slots, *piece), "ia")

    first = first_flip(place, amplitudes, sections, sizes[0])
    masked = mask_blocks(integrals, tile_mask, [first])
    across = [swap(first, "ka")]
    (second,) = fetch(SETS[1], [first])
    across.append(second([masked]))
    waiting = fetch(SETS[2], [across[1]])
    own, delivered = [], []
    after = [across[1]]
    for at in range(len(spans)):
        crossed = hop(at)
        if at == len(spans) - 1:
            leading = columns([crossed])
            after = [*after, leading]
        returned = scatter(place, crossed, after)
        begun = []
        if at == 1:
            token, columns = send(GROUPS[0])
            begun = [token]
        partial_rows = multiply(at, returned, begun)
        after = [partial_rows[0]]
        if waiting:
            across.append(waiting.pop(0)(after))
            after = [across[-1]]
        own.append(add(place, spread(partial_rows)))

    delivered.append(deliver(leading))
    for group in GROUPS[1:]:
        _, columns = send(group)
        delivered.append(deliver(columns([delivered[-1]])))
    return finish(place, spans, GROUPS, own, delivered)


def solution(mesh):
    placed = (
        P("ia", "ka", None, None),
        P("ia", None, "ka", None, None),
        P("ia", None, "ka", None, None),
        P(),
    )
    return jax.shard_map(
        functools.partial(body, mesh.shape["ka"]),
        mesh=mesh,
        in_specs=placed,
        out_specs=P("ia", None, "ka", None),
        check_vma=False,
    )
```

```python
import functools

import jax
import jax.numpy as jnp
from jax import lax
from jax.experimental import pallas as pl
from jax.experimental.pallas import tpu as pltpu
from jax.sharding import PartitionSpec as P

CHUNKS = (2, 3, 2, 1)
SETS = ((0,), (1,), (2, 3))
GROUPS = ((0,), (1,), (2, 3))
LANES = 128
VMEM_BYTES = 48 * 1024 * 1024


def call(
    kernel, name, scalars, operands, in_specs, out_specs, out_shape, grid, scratch=(), flops=0, after=()
):
    moved = sum(x.size * x.dtype.itemsize for x in jax.tree.leaves(out_shape)) * 2
    reads = 1 + len(operands)

    def trimmed(*refs):
        kernel(*refs[:reads], *refs[reads + len(after) :])

    return pl.pallas_call(
        trimmed,
        grid_spec=pltpu.PrefetchScalarGridSpec(
            num_scalar_prefetch=1,
            grid=grid,
            in_specs=list(in_specs) + [pl.BlockSpec(memory_space=pl.ANY)] * len(after),
            out_specs=out_specs,
            scratch_shapes=list(scratch),
        ),
        out_shape=out_shape,
        compiler_params=pltpu.CompilerParams(vmem_limit_bytes=VMEM_BYTES),
        cost_estimate=pl.CostEstimate(flops=flops, bytes_accessed=moved, transcendentals=0),
        name=name,
    )(scalars, *operands, *after)


def whole(shape):
    return pl.BlockSpec(shape, lambda *_: (0,) * len(shape))


def first_flip_kernel(place_ref, blocks_ref, piece_ref):
    piece_ref[0, 0] = blocks_ref[0, 0].T[: piece_ref.shape[2]]


def first_flip(place, amplitudes, sections, rows):
    pairs, virtuals = amplitudes.shape[1], amplitudes.shape[3]
    steps = virtuals // sections // LANES
    return call(
        first_flip_kernel,
        "first_flip",
        place,
        [amplitudes],
        [pl.BlockSpec((1, 1, virtuals, LANES), lambda d, q, at: (0, d, 0, q * steps))],
        pl.BlockSpec((1, 1, rows, virtuals), lambda d, q, at: (q, d, 0, 0)),
        jax.ShapeDtypeStruct((sections, pairs, rows, virtuals), jnp.float32),
        (pairs, sections),
    )


def flip_kernel(start, place_ref, blocks_ref, piece_ref):
    piece_ref[0] = blocks_ref[0, 0].T[start : start + piece_ref.shape[1]]


def flip(place, amplitudes, sections, e, start, rows, after):
    pairs, virtuals = amplitudes.shape[1], amplitudes.shape[3]
    wide = virtuals // sections
    return call(
        functools.partial(flip_kernel, start),
        "flip",
        place,
        [amplitudes],
        [pl.BlockSpec((1, 1, virtuals, wide), lambda d, at: (0, d, 0, at[0] ^ e))],
        pl.BlockSpec((1, rows, virtuals), lambda d, at: (d, 0, 0)),
        jax.ShapeDtypeStruct((pairs, rows, virtuals), jnp.float32),
        (pairs,),
        after=after,
    )


def part_kernel(start, place_ref, *refs):
    pieces, out_ref = refs[:-1], refs[-1]
    for e, piece in enumerate(pieces):
        out_ref[place_ref[0] ^ e, 0] = piece[0, start : start + out_ref.shape[2]]


def part(place, pieces, start, size, after):
    count, (pairs, rows, virtuals) = len(pieces), pieces[0].shape
    return call(
        functools.partial(part_kernel, start),
        "part",
        place,
        pieces,
        [pl.BlockSpec((1, rows, virtuals), lambda d, at: (d, 0, 0))] * count,
        pl.BlockSpec((count, 1, size, virtuals), lambda d, at: (0, d, 0, 0)),
        jax.ShapeDtypeStruct((count, pairs, size, virtuals), jnp.float32),
        (pairs,),
        after=after,
    )


def gather_kernel(place_ref, *refs):
    pieces, out_ref = refs[:-1], refs[-1]
    for e, piece in enumerate(pieces):
        out_ref[e] = piece[...]


def gather(place, pieces, after):
    shape = (len(pieces), *pieces[0].shape)
    return call(
        gather_kernel,
        "gather",
        place,
        pieces,
        [whole(pieces[0].shape)] * len(pieces),
        whole(shape),
        jax.ShapeDtypeStruct(shape, jnp.float32),
        (1,),
        after=after,
    )


def scatter_kernel(place_ref, stacked_ref, *pieces):
    for e, piece in enumerate(pieces):
        piece[...] = stacked_ref[place_ref[0] ^ e]


def scatter(place, stacked, after):
    count, shape = stacked.shape[0], stacked.shape[1:]
    return call(
        scatter_kernel,
        "scatter",
        place,
        [stacked],
        [whole(stacked.shape)],
        [whole(shape)] * count,
        [jax.ShapeDtypeStruct(shape, jnp.float32)] * count,
        (1,),
        after=after,
    )


def mask_kernel(tiles, mask_ref, integrals_ref, masked_ref):
    side = integrals_ref.shape[-1] // tiles
    slot, pair = pl.program_id(0), pl.program_id(1)
    for r in range(tiles):
        for c in range(tiles):
            keep = mask_ref[slot, pair, r, c] != 0
            spot = (pl.ds(r * side, side), pl.ds(c * side, side))
            tile = integrals_ref[0, 0, 0, spot[0], spot[1]]
            masked_ref[0, 0, spot[0], spot[1]] = jnp.where(keep, tile, jnp.zeros_like(tile))


def mask_blocks(integrals, tile_mask, after):
    _, slots, pairs, virtuals, _ = integrals.shape
    out_shape = jax.ShapeDtypeStruct((slots, pairs, virtuals, virtuals), jnp.bfloat16)
    return call(
        functools.partial(mask_kernel, tile_mask.shape[-1]),
        "mask",
        tile_mask[0],
        [integrals],
        [pl.BlockSpec((1, 1, 1, virtuals, virtuals), lambda s, k, mask: (0, s, k, 0, 0))],
        pl.BlockSpec((1, 1, virtuals, virtuals), lambda s, k, mask: (s, k, 0, 0)),
        out_shape,
        (slots, pairs),
        after=after,
    )


def product_kernel(sections, place_ref, *refs):
    own_refs, mirrored_refs, refs = refs[:sections], refs[sections : 2 * sections], refs[2 * sections :]
    masked_ref, out_refs, split_ref = refs[0], refs[1:-1], refs[-1]
    pairs, rows, _ = mirrored_refs[0].shape
    tall = sections * rows

    @pl.when((pl.program_id(0) == 0) & (pl.program_id(1) == 0))
    def _():
        for e in range(sections):
            for k in range(pairs):
                mixed = 2.0 * own_refs[e][0, k] - mirrored_refs[e][k]
                high = mixed.astype(jnp.bfloat16)
                low = (mixed - high.astype(jnp.float32)).astype(jnp.bfloat16)
                split_ref[k, pl.ds(e * rows, rows)] = high
                split_ref[k, pl.ds(tall + e * rows, rows)] = low

    total = None
    for k in range(pairs):
        both = jnp.dot(split_ref[k], masked_ref[0, k], preferred_element_type=jnp.float32)
        both = both[:tall] + both[tall:]
        total = both if total is None else total + both
    for e, out_ref in enumerate(out_refs):
        out_ref[0] = total[e * rows : (e + 1) * rows]


def product(place, own, mirrored, masked, start, after):
    sections = len(mirrored)
    pairs, rows, virtuals = mirrored[0].shape
    slots = masked.shape[0]
    deep = virtuals // sections
    wide = min(virtuals, 512)
    return call(
        functools.partial(product_kernel, sections),
        "product",
        place,
        [own] * sections + list(mirrored) + [masked],
        [
            pl.BlockSpec(
                tuple(pl.Element(size) for size in (1, pairs, rows, virtuals)),
                lambda s, n, at, e=e: (0, 0, pl.multiple_of((at[0] ^ e) * deep + start, 8), 0),
            )
            for e in range(sections)
        ]
        + [whole(mirrored[0].shape)] * sections
        + [pl.BlockSpec((1, pairs, virtuals, wide), lambda s, n, at: (s, 0, 0, n))],
        [pl.BlockSpec((1, rows, wide), lambda s, n, at: (s, 0, n))] * sections,
        [jax.ShapeDtypeStruct((slots, rows, virtuals), jnp.float32)] * sections,
        (slots, virtuals // wide),
        scratch=[pltpu.VMEM((pairs, 2 * sections * rows, virtuals), jnp.bfloat16)],
        flops=4 * sections * rows * pairs * virtuals * virtuals * slots,
        after=after,
    )


def add_kernel(place_ref, *refs):
    refs[-1][...] = sum((part[...] for part in refs[1:-1]), refs[0][...])


def add(place, parts, after):
    slots, rows, virtuals = parts[0].shape
    block = pl.BlockSpec((1, rows, virtuals), lambda s, at: (s, 0, 0))
    return call(
        add_kernel,
        "add",
        place,
        parts,
        [block] * len(parts),
        block,
        jax.ShapeDtypeStruct(parts[0].shape, jnp.float32),
        (slots,),
        after=after,
    )


def cut_kernel(chunks, place_ref, *refs):
    total_refs, cut_refs = refs[:chunks], refs[chunks:]
    parts, _, _, wide = cut_refs[0].shape
    for e, cut_ref in enumerate(cut_refs):
        columns = pl.ds(pl.multiple_of((place_ref[0] ^ e) * wide, wide), wide)
        at = 0
        for total_ref in total_refs:
            short = total_ref.shape[1] // parts
            for part in range(parts):
                cut_ref[part, :, at : at + short] = total_ref[
                    :, part * short : (part + 1) * short, columns
                ]
            at += short


def cut(place, totals, sections, parts):
    slots, _, virtuals = totals[0].shape
    rows = sum(total.shape[1] for total in totals)
    shape = (parts, slots, rows // parts, virtuals // sections)
    return call(
        functools.partial(cut_kernel, len(totals)),
        "cut",
        place,
        totals,
        [whole(total.shape) for total in totals],
        [whole(shape)] * sections,
        [jax.ShapeDtypeStruct(shape, jnp.float32)] * sections,
        (1,),
    )


def finish_kernel(spans, groups, place_ref, *refs):
    chunks = len(spans)
    own_refs, delivered_refs = refs[:chunks], refs[chunks : chunks + len(groups)]
    out_ref, columns_ref = refs[chunks + len(groups) :]
    wide = out_ref.shape[2]
    sections = columns_ref.shape[0] // wide
    for group, delivered_ref in zip(groups, delivered_refs):
        parts = delivered_ref.shape[0] // sections
        for e in range(sections):
            base = (place_ref[0] ^ e) * wide
            for part in range(parts):
                at = 0
                for chunk in group:
                    start, rows = spans[chunk]
                    short = rows // parts
                    spot = pl.multiple_of(base + start + part * short, 8)
                    columns_ref[pl.ds(spot, short)] = delivered_ref[
                        e * parts + part, 0, at : at + short
                    ]
                    at += short
    turned = columns_ref[...].T
    for (start, rows), own_ref in zip(spans, own_refs):
        out_ref[0, 0, start : start + rows] = own_ref[0] + turned[start : start + rows]


def finish(place, spans, groups, own, delivered):
    slots, _, virtuals = own[0].shape
    wide = delivered[0].shape[-1]
    return call(
        functools.partial(finish_kernel, spans, groups),
        "finish",
        place,
        list(own) + list(delivered),
        [pl.BlockSpec((1, *x.shape[1:]), lambda s, at: (s, 0, 0)) for x in own]
        + [
            pl.BlockSpec((x.shape[0], 1, *x.shape[2:]), lambda s, at: (0, s, 0, 0))
            for x in delivered
        ],
        pl.BlockSpec((1, 1, wide, virtuals), lambda s, at: (0, s, 0, 0)),
        jax.ShapeDtypeStruct((1, slots, wide, virtuals), jnp.float32),
        (slots,),
        scratch=[pltpu.VMEM((virtuals, wide), jnp.float32)],
    )


def swap(array, axis):
    return lax.all_to_all(array, axis, split_axis=0, concat_axis=0, tiled=True)


def spread(pieces):
    count = len(pieces)
    return [pieces[0]] + [
        lax.ppermute(pieces[e], "ka", [(q, q ^ e) for q in range(count)]) for e in range(1, count)
    ]


def body(sections, amplitudes, integrals, tile_mask, pair_list):
    _, pairs, virtuals, _ = amplitudes.shape
    occupied, slots = pair_list.shape
    wide = virtuals // sections
    sizes = [wide * part // sum(CHUNKS) for part in CHUNKS]
    spans = [(sum(sizes[:at]), size) for at, size in enumerate(sizes)]
    place = lax.axis_index("ka").astype(jnp.int32).reshape(1)

    owners = jnp.arange(occupied, dtype=jnp.int32)
    partner_slot = jnp.where(pair_list[pair_list, 0] == owners[:, None], 0, 1).astype(jnp.int32)
    source_row = (pair_list * slots + partner_slot).reshape(-1)

    def fetch(chunks, after):
        start, rows = spans[chunks[0]][0], sum(sizes[at] for at in chunks)
        pieces = [flip(place, amplitudes, sections, e, start, rows, after) for e in range(sections)]
        pieces = spread(pieces)
        return [
            functools.partial(part, place, pieces, spans[at][0] - start, sizes[at]) for at in chunks
        ]

    def hop(at):
        crossed = swap(across[at].reshape(occupied, sizes[at], virtuals), "ia")
        return crossed.reshape(sections, pairs, sizes[at], virtuals)

    def turn(at, crossed, after):
        pieces = scatter(place, crossed, after)
        return pieces[0], spread(pieces)

    def multiply(at, mirrored, after):
        parts = product(place, amplitudes, mirrored, masked, spans[at][0], after)
        return parts[0], spread(parts)

    def send(group):
        return spread(cut(place, [own[at] for at in group], sections, pairs))

    def meet(columns):
        return swap(columns.reshape(occupied, slots, *columns.shape[-2:]), "ia")

    def deliver(met):
        piece = met.shape[-2:]
        routed = jnp.take(met.reshape(occupied * slots, *piece), source_row, axis=0)
        return swap(routed.reshape(occupied, slots, *piece), "ia")

    first = first_flip(place, amplitudes, sections, sizes[0])
    masked = mask_blocks(integrals, tile_mask, [first])
    across = [swap(first, "ka")]
    (second,) = fetch(SETS[1], [first])
    across.append(second([masked]))
    waiting = fetch(SETS[2], [across[1]])
    turned, mirrored = turn(0, hop(0), [across[1]])
    begun, parts = multiply(0, mirrored, [])
    across.append(waiting[0]([begun]))
    turned, mirrored = turn(1, hop(1), [across[2]])
    turned, later = turn(2, hop(2), [turned])
    across.append(waiting[1]([turned]))
    own = [add(place, parts, [turned])]
    begun, parts = multiply(1, mirrored, [turned])
    crossed = hop(3)
    leading = gather(place, send(GROUPS[0]), [crossed])
    turned, mirrored = turn(3, crossed, [begun, leading])
    own.append(add(place, parts, []))
    met = meet(leading)
    begun, parts = multiply(2, later, [turned, met])
    own.append(add(place, parts, []))
    _, parts = multiply(3, mirrored, [begun])
    own.append(add(place, parts, []))

    delivered = [deliver(met)]
    for group in GROUPS[1:]:
        delivered.append(deliver(meet(gather(place, send(group), [delivered[-1]]))))
    return finish(place, spans, GROUPS, own, delivered)


def solution(mesh):
    placed = (
        P("ia", "ka", None, None),
        P("ia", None, "ka", None, None),
        P("ia", None, "ka", None, None),
        P(),
    )
    return jax.shard_map(
        functools.partial(body, mesh.shape["ka"]),
        mesh=mesh,
        in_specs=placed,
        out_specs=P("ia", None, "ka", None),
        check_vma=False,
    )
```

```python
import functools

import jax
import jax.numpy as jnp
from jax import lax
from jax.experimental import pallas as pl
from jax.experimental.pallas import tpu as pltpu
from jax.sharding import PartitionSpec as P

CHUNKS = (2, 3, 2, 1)
SETS = ((0,), (1,), (2, 3))
GROUPS = ((0,), (1,), (2, 3))
LANES = 128
VMEM_BYTES = 48 * 1024 * 1024


def call(
    kernel, name, scalars, operands, in_specs, out_specs, out_shape, grid, scratch=(), flops=0, after=()
):
    moved = sum(x.size * x.dtype.itemsize for x in jax.tree.leaves(out_shape)) * 2
    reads = 1 + len(operands)

    def trimmed(*refs):
        kernel(*refs[:reads], *refs[reads + len(after) :])

    return pl.pallas_call(
        trimmed,
        grid_spec=pltpu.PrefetchScalarGridSpec(
            num_scalar_prefetch=1,
            grid=grid,
            in_specs=list(in_specs) + [pl.BlockSpec(memory_space=pl.ANY)] * len(after),
            out_specs=out_specs,
            scratch_shapes=list(scratch),
        ),
        out_shape=out_shape,
        compiler_params=pltpu.CompilerParams(vmem_limit_bytes=VMEM_BYTES),
        cost_estimate=pl.CostEstimate(flops=flops, bytes_accessed=moved, transcendentals=0),
        name=name,
    )(scalars, *operands, *after)


def whole(shape):
    return pl.BlockSpec(shape, lambda *_: (0,) * len(shape))


def first_flip_kernel(place_ref, blocks_ref, piece_ref):
    piece_ref[0, 0] = blocks_ref[0, 0].T[: piece_ref.shape[2]]


def first_flip(place, amplitudes, sections, rows):
    pairs, virtuals = amplitudes.shape[1], amplitudes.shape[3]
    steps = virtuals // sections // LANES
    return call(
        first_flip_kernel,
        "first_flip",
        place,
        [amplitudes],
        [pl.BlockSpec((1, 1, virtuals, LANES), lambda d, q, at: (0, d, 0, q * steps))],
        pl.BlockSpec((1, 1, rows, virtuals), lambda d, q, at: (q, d, 0, 0)),
        jax.ShapeDtypeStruct((sections, pairs, rows, virtuals), jnp.float32),
        (pairs, sections),
    )


def flip_kernel(start, place_ref, blocks_ref, piece_ref):
    piece_ref[0] = blocks_ref[0, 0].T[start : start + piece_ref.shape[1]]


def flip(place, amplitudes, sections, e, start, rows, after):
    pairs, virtuals = amplitudes.shape[1], amplitudes.shape[3]
    wide = virtuals // sections
    return call(
        functools.partial(flip_kernel, start),
        "flip",
        place,
        [amplitudes],
        [pl.BlockSpec((1, 1, virtuals, wide), lambda d, at: (0, d, 0, at[0] ^ e))],
        pl.BlockSpec((1, rows, virtuals), lambda d, at: (d, 0, 0)),
        jax.ShapeDtypeStruct((pairs, rows, virtuals), jnp.float32),
        (pairs,),
        after=after,
    )


def part_kernel(start, place_ref, *refs):
    pieces, out_ref = refs[:-1], refs[-1]
    for e, piece in enumerate(pieces):
        out_ref[place_ref[0] ^ e, 0] = piece[0, start : start + out_ref.shape[2]]


def part(place, pieces, start, size, after):
    count, (pairs, rows, virtuals) = len(pieces), pieces[0].shape
    return call(
        functools.partial(part_kernel, start),
        "part",
        place,
        pieces,
        [pl.BlockSpec((1, rows, virtuals), lambda d, at: (d, 0, 0))] * count,
        pl.BlockSpec((count, 1, size, virtuals), lambda d, at: (0, d, 0, 0)),
        jax.ShapeDtypeStruct((count, pairs, size, virtuals), jnp.float32),
        (pairs,),
        after=after,
    )


def gather_kernel(place_ref, *refs):
    pieces, out_ref = refs[:-1], refs[-1]
    for e, piece in enumerate(pieces):
        out_ref[e] = piece[...]


def gather(place, pieces, after):
    shape = (len(pieces), *pieces[0].shape)
    return call(
        gather_kernel,
        "gather",
        place,
        pieces,
        [whole(pieces[0].shape)] * len(pieces),
        whole(shape),
        jax.ShapeDtypeStruct(shape, jnp.float32),
        (1,),
        after=after,
    )


def scatter_kernel(place_ref, stacked_ref, *pieces):
    for e, piece in enumerate(pieces):
        piece[...] = stacked_ref[place_ref[0] ^ e]


def scatter(place, stacked, after):
    count, shape = stacked.shape[0], stacked.shape[1:]
    return call(
        scatter_kernel,
        "scatter",
        place,
        [stacked],
        [whole(stacked.shape)],
        [whole(shape)] * count,
        [jax.ShapeDtypeStruct(shape, jnp.float32)] * count,
        (1,),
        after=after,
    )


def mask_kernel(tiles, mask_ref, integrals_ref, masked_ref):
    side = integrals_ref.shape[-1] // tiles
    slot, pair = pl.program_id(0), pl.program_id(1)
    for r in range(tiles):
        for c in range(tiles):
            keep = mask_ref[slot, pair, r, c] != 0
            spot = (pl.ds(r * side, side), pl.ds(c * side, side))
            tile = integrals_ref[0, 0, 0, spot[0], spot[1]]
            masked_ref[0, 0, spot[0], spot[1]] = jnp.where(keep, tile, jnp.zeros_like(tile))


def mask_blocks(integrals, tile_mask, after):
    _, slots, pairs, virtuals, _ = integrals.shape
    out_shape = jax.ShapeDtypeStruct((slots, pairs, virtuals, virtuals), jnp.bfloat16)
    return call(
        functools.partial(mask_kernel, tile_mask.shape[-1]),
        "mask",
        tile_mask[0],
        [integrals],
        [pl.BlockSpec((1, 1, 1, virtuals, virtuals), lambda s, k, mask: (0, s, k, 0, 0))],
        pl.BlockSpec((1, 1, virtuals, virtuals), lambda s, k, mask: (s, k, 0, 0)),
        out_shape,
        (slots, pairs),
        after=after,
    )


def product_kernel(sections, place_ref, *refs):
    own_refs, mirrored_refs, refs = refs[:sections], refs[sections : 2 * sections], refs[2 * sections :]
    masked_ref, out_refs, split_ref = refs[0], refs[1:-1], refs[-1]
    pairs, rows, _ = mirrored_refs[0].shape
    tall = sections * rows

    @pl.when((pl.program_id(0) == 0) & (pl.program_id(1) == 0))
    def _():
        for e in range(sections):
            for k in range(pairs):
                mixed = 2.0 * own_refs[e][0, k] - mirrored_refs[e][k]
                high = mixed.astype(jnp.bfloat16)
                low = (mixed - high.astype(jnp.float32)).astype(jnp.bfloat16)
                split_ref[k, pl.ds(e * rows, rows)] = high
                split_ref[k, pl.ds(tall + e * rows, rows)] = low

    total = None
    for k in range(pairs):
        both = jnp.dot(split_ref[k], masked_ref[0, k], preferred_element_type=jnp.float32)
        both = both[:tall] + both[tall:]
        total = both if total is None else total + both
    for e, out_ref in enumerate(out_refs):
        out_ref[0] = total[e * rows : (e + 1) * rows]


def product(place, own, mirrored, masked, start, after):
    sections = len(mirrored)
    pairs, rows, virtuals = mirrored[0].shape
    slots = masked.shape[0]
    deep = virtuals // sections
    wide = min(virtuals, 512)
    return call(
        functools.partial(product_kernel, sections),
        "product",
        place,
        [own] * sections + list(mirrored) + [masked],
        [
            pl.BlockSpec(
                tuple(pl.Element(size) for size in (1, pairs, rows, virtuals)),
                lambda s, n, at, e=e: (0, 0, pl.multiple_of((at[0] ^ e) * deep + start, 8), 0),
            )
            for e in range(sections)
        ]
        + [whole(mirrored[0].shape)] * sections
        + [pl.BlockSpec((1, pairs, virtuals, wide), lambda s, n, at: (s, 0, 0, n))],
        [pl.BlockSpec((1, rows, wide), lambda s, n, at: (s, 0, n))] * sections,
        [jax.ShapeDtypeStruct((slots, rows, virtuals), jnp.float32)] * sections,
        (slots, virtuals // wide),
        scratch=[pltpu.VMEM((pairs, 2 * sections * rows, virtuals), jnp.bfloat16)],
        flops=4 * sections * rows * pairs * virtuals * virtuals * slots,
        after=after,
    )


def add_kernel(place_ref, *refs):
    refs[-1][...] = sum((part[...] for part in refs[1:-1]), refs[0][...])


def add(place, parts, after):
    slots, rows, virtuals = parts[0].shape
    block = pl.BlockSpec((1, rows, virtuals), lambda s, at: (s, 0, 0))
    return call(
        add_kernel,
        "add",
        place,
        parts,
        [block] * len(parts),
        block,
        jax.ShapeDtypeStruct(parts[0].shape, jnp.float32),
        (slots,),
        after=after,
    )


def cut_kernel(chunks, place_ref, *refs):
    total_refs, cut_refs = refs[:chunks], refs[chunks:]
    parts, _, _, wide = cut_refs[0].shape
    for e, cut_ref in enumerate(cut_refs):
        columns = pl.ds(pl.multiple_of((place_ref[0] ^ e) * wide, wide), wide)
        at = 0
        for total_ref in total_refs:
            short = total_ref.shape[1] // parts
            for part in range(parts):
                cut_ref[part, :, at : at + short] = total_ref[
                    :, part * short : (part + 1) * short, columns
                ]
            at += short


def cut(place, totals, sections, parts):
    slots, _, virtuals = totals[0].shape
    rows = sum(total.shape[1] for total in totals)
    shape = (parts, slots, rows // parts, virtuals // sections)
    return call(
        functools.partial(cut_kernel, len(totals)),
        "cut",
        place,
        totals,
        [whole(total.shape) for total in totals],
        [whole(shape)] * sections,
        [jax.ShapeDtypeStruct(shape, jnp.float32)] * sections,
        (1,),
    )


def hold_kernel(index_ref, out_ref):
    for at in range(out_ref.shape[0]):
        out_ref[at] = index_ref[at]


def hold(index, after):
    return call(
        hold_kernel,
        "hold",
        index,
        [],
        [],
        pl.BlockSpec(memory_space=pltpu.SMEM),
        jax.ShapeDtypeStruct(index.shape, index.dtype),
        (1,),
        after=after,
    )


def finish_kernel(spans, groups, place_ref, *refs):
    chunks = len(spans)
    own_refs, delivered_refs = refs[:chunks], refs[chunks : chunks + len(groups)]
    out_ref, columns_ref = refs[chunks + len(groups) :]
    wide = out_ref.shape[2]
    sections = columns_ref.shape[0] // wide
    for group, delivered_ref in zip(groups, delivered_refs):
        parts = delivered_ref.shape[0] // sections
        for e in range(sections):
            base = (place_ref[0] ^ e) * wide
            for part in range(parts):
                at = 0
                for chunk in group:
                    start, rows = spans[chunk]
                    short = rows // parts
                    spot = pl.multiple_of(base + start + part * short, 8)
                    columns_ref[pl.ds(spot, short)] = delivered_ref[
                        e * parts + part, 0, at : at + short
                    ]
                    at += short
    turned = columns_ref[...].T
    for (start, rows), own_ref in zip(spans, own_refs):
        out_ref[0, 0, start : start + rows] = own_ref[0] + turned[start : start + rows]


def finish(place, spans, groups, own, delivered):
    slots, _, virtuals = own[0].shape
    wide = delivered[0].shape[-1]
    return call(
        functools.partial(finish_kernel, spans, groups),
        "finish",
        place,
        list(own) + list(delivered),
        [pl.BlockSpec((1, *x.shape[1:]), lambda s, at: (s, 0, 0)) for x in own]
        + [
            pl.BlockSpec((x.shape[0], 1, *x.shape[2:]), lambda s, at: (0, s, 0, 0))
            for x in delivered
        ],
        pl.BlockSpec((1, 1, wide, virtuals), lambda s, at: (0, s, 0, 0)),
        jax.ShapeDtypeStruct((1, slots, wide, virtuals), jnp.float32),
        (slots,),
        scratch=[pltpu.VMEM((virtuals, wide), jnp.float32)],
    )


def swap(array, axis):
    return lax.all_to_all(array, axis, split_axis=0, concat_axis=0, tiled=True)


def spread(pieces):
    count = len(pieces)
    return [pieces[0]] + [
        lax.ppermute(pieces[e], "ka", [(q, q ^ e) for q in range(count)]) for e in range(1, count)
    ]


def body(sections, amplitudes, integrals, tile_mask, pair_list):
    _, pairs, virtuals, _ = amplitudes.shape
    occupied, slots = pair_list.shape
    wide = virtuals // sections
    sizes = [wide * part // sum(CHUNKS) for part in CHUNKS]
    spans = [(sum(sizes[:at]), size) for at, size in enumerate(sizes)]
    place = lax.axis_index("ka").astype(jnp.int32).reshape(1)

    owners = jnp.arange(occupied, dtype=jnp.int32)
    partner_slot = jnp.where(pair_list[pair_list, 0] == owners[:, None], 0, 1).astype(jnp.int32)
    source_row = (pair_list * slots + partner_slot).reshape(-1)

    def fetch(chunks, after):
        start, rows = spans[chunks[0]][0], sum(sizes[at] for at in chunks)
        pieces = [flip(place, amplitudes, sections, e, start, rows, after) for e in range(sections)]
        pieces = spread(pieces)
        return [
            functools.partial(part, place, pieces, spans[at][0] - start, sizes[at]) for at in chunks
        ]

    def hop(at):
        crossed = swap(across[at].reshape(occupied, sizes[at], virtuals), "ia")
        return crossed.reshape(sections, pairs, sizes[at], virtuals)

    def turn(at, crossed, after):
        pieces = scatter(place, crossed, after)
        return pieces[0], spread(pieces)

    def multiply(at, mirrored, after):
        parts = product(place, amplitudes, mirrored, masked, spans[at][0], after)
        return parts[0], spread(parts)

    def send(group):
        return spread(cut(place, [own[at] for at in group], sections, pairs))

    def meet(columns):
        return swap(columns.reshape(occupied, slots, *columns.shape[-2:]), "ia")

    def deliver(met, after):
        piece = met.shape[-2:]
        rows = hold(source_row, after)
        routed = jnp.take(met.reshape(occupied * slots, *piece), rows, axis=0)
        return swap(routed.reshape(occupied, slots, *piece), "ia")

    first = first_flip(place, amplitudes, sections, sizes[0])
    masked = mask_blocks(integrals, tile_mask, [first])
    across = [swap(first, "ka")]
    (second,) = fetch(SETS[1], [first])
    across.append(second([masked]))
    waiting = fetch(SETS[2], [across[1]])
    turned, mirrored = turn(0, hop(0), [across[1]])
    begun, parts = multiply(0, mirrored, [])
    across.append(waiting[0]([begun]))
    own = [add(place, parts, [])]
    turned, mirrored = turn(1, hop(1), [across[2]])
    turned, later = turn(2, hop(2), [turned])
    across.append(waiting[1]([turned, own[0]]))
    begun, parts = multiply(1, mirrored, [])
    own.append(add(place, parts, []))
    crossed = hop(3)
    leading = gather(place, send(GROUPS[0]), [crossed, begun])
    turned, mirrored = turn(3, crossed, [leading])
    begun, parts = multiply(2, later, [turned])
    own.append(add(place, parts, []))
    delivered = [deliver(meet(leading), [begun])]
    begun, parts = multiply(3, mirrored, delivered)
    own.append(add(place, parts, []))
    after = [begun]
    for group in GROUPS[1:]:
        met = meet(gather(place, send(group), [delivered[-1], *after]))
        delivered.append(deliver(met, []))
        after = []
    return finish(place, spans, GROUPS, own, delivered)


def solution(mesh):
    placed = (
        P("ia", "ka", None, None),
        P("ia", None, "ka", None, None),
        P("ia", None, "ka", None, None),
        P(),
    )
    return jax.shard_map(
        functools.partial(body, mesh.shape["ka"]),
        mesh=mesh,
        in_specs=placed,
        out_specs=P("ia", None, "ka", None),
        check_vma=False,
    )
```

```python
import functools

import jax
import jax.numpy as jnp
from jax import lax
from jax.experimental import pallas as pl
from jax.experimental.pallas import tpu as pltpu
from jax.sharding import PartitionSpec as P

CHUNKS = (2, 3, 2, 1)
SETS = ((0,), (1,), (2, 3))
GROUPS = ((0,), (1,), (2, 3))
SCATTERED = (0, 1)
LANES = 128
VMEM_BYTES = 48 * 1024 * 1024


def call(
    kernel, name, scalars, operands, in_specs, out_specs, out_shape, grid, scratch=(), flops=0, after=()
):
    moved = sum(x.size * x.dtype.itemsize for x in jax.tree.leaves(out_shape)) * 2
    reads = 1 + len(operands)

    def trimmed(*refs):
        kernel(*refs[:reads], *refs[reads + len(after) :])

    return pl.pallas_call(
        trimmed,
        grid_spec=pltpu.PrefetchScalarGridSpec(
            num_scalar_prefetch=1,
            grid=grid,
            in_specs=list(in_specs) + [pl.BlockSpec(memory_space=pl.ANY)] * len(after),
            out_specs=out_specs,
            scratch_shapes=list(scratch),
        ),
        out_shape=out_shape,
        compiler_params=pltpu.CompilerParams(vmem_limit_bytes=VMEM_BYTES),
        cost_estimate=pl.CostEstimate(flops=flops, bytes_accessed=moved, transcendentals=0),
        name=name,
    )(scalars, *operands, *after)


def whole(shape):
    return pl.BlockSpec(shape, lambda *_: (0,) * len(shape))


def first_flip_kernel(place_ref, blocks_ref, piece_ref):
    piece_ref[0, 0] = blocks_ref[0, 0].T[: piece_ref.shape[2]]


def first_flip(place, amplitudes, sections, rows):
    pairs, virtuals = amplitudes.shape[1], amplitudes.shape[3]
    steps = virtuals // sections // LANES
    return call(
        first_flip_kernel,
        "first_flip",
        place,
        [amplitudes],
        [pl.BlockSpec((1, 1, virtuals, LANES), lambda d, q, at: (0, d, 0, q * steps))],
        pl.BlockSpec((1, 1, rows, virtuals), lambda d, q, at: (q, d, 0, 0)),
        jax.ShapeDtypeStruct((sections, pairs, rows, virtuals), jnp.float32),
        (pairs, sections),
    )


def flip_kernel(start, place_ref, blocks_ref, piece_ref):
    piece_ref[0] = blocks_ref[0, 0].T[start : start + piece_ref.shape[1]]


def flip(place, amplitudes, sections, e, start, rows, after):
    pairs, virtuals = amplitudes.shape[1], amplitudes.shape[3]
    wide = virtuals // sections
    return call(
        functools.partial(flip_kernel, start),
        "flip",
        place,
        [amplitudes],
        [pl.BlockSpec((1, 1, virtuals, wide), lambda d, at: (0, d, 0, at[0] ^ e))],
        pl.BlockSpec((1, rows, virtuals), lambda d, at: (d, 0, 0)),
        jax.ShapeDtypeStruct((pairs, rows, virtuals), jnp.float32),
        (pairs,),
        after=after,
    )


def part_kernel(start, place_ref, *refs):
    pieces, out_ref = refs[:-1], refs[-1]
    for e, piece in enumerate(pieces):
        out_ref[place_ref[0] ^ e, 0] = piece[0, start : start + out_ref.shape[2]]


def part(place, pieces, start, size, after):
    count, (pairs, rows, virtuals) = len(pieces), pieces[0].shape
    return call(
        functools.partial(part_kernel, start),
        "part",
        place,
        pieces,
        [pl.BlockSpec((1, rows, virtuals), lambda d, at: (d, 0, 0))] * count,
        pl.BlockSpec((count, 1, size, virtuals), lambda d, at: (0, d, 0, 0)),
        jax.ShapeDtypeStruct((count, pairs, size, virtuals), jnp.float32),
        (pairs,),
        after=after,
    )


def gather_kernel(place_ref, *refs):
    pieces, out_ref = refs[:-1], refs[-1]
    for e, piece in enumerate(pieces):
        out_ref[e] = piece[...]


def gather(place, pieces, after):
    shape = (len(pieces), *pieces[0].shape)
    return call(
        gather_kernel,
        "gather",
        place,
        pieces,
        [whole(pieces[0].shape)] * len(pieces),
        whole(shape),
        jax.ShapeDtypeStruct(shape, jnp.float32),
        (1,),
        after=after,
    )


def scatter_kernel(place_ref, stacked_ref, *pieces):
    for e, piece in enumerate(pieces):
        piece[...] = stacked_ref[place_ref[0] ^ e]


def scatter(place, stacked, after):
    count, shape = stacked.shape[0], stacked.shape[1:]
    return call(
        scatter_kernel,
        "scatter",
        place,
        [stacked],
        [whole(stacked.shape)],
        [whole(shape)] * count,
        [jax.ShapeDtypeStruct(shape, jnp.float32)] * count,
        (1,),
        after=after,
    )


def mask_kernel(tiles, mask_ref, integrals_ref, masked_ref):
    side = integrals_ref.shape[-1] // tiles
    slot, pair = pl.program_id(0), pl.program_id(1)
    for r in range(tiles):
        for c in range(tiles):
            keep = mask_ref[slot, pair, r, c] != 0
            spot = (pl.ds(r * side, side), pl.ds(c * side, side))
            tile = integrals_ref[0, 0, 0, spot[0], spot[1]]
            masked_ref[0, 0, spot[0], spot[1]] = jnp.where(keep, tile, jnp.zeros_like(tile))


def mask_blocks(integrals, tile_mask, after):
    _, slots, pairs, virtuals, _ = integrals.shape
    out_shape = jax.ShapeDtypeStruct((slots, pairs, virtuals, virtuals), jnp.bfloat16)
    return call(
        functools.partial(mask_kernel, tile_mask.shape[-1]),
        "mask",
        tile_mask[0],
        [integrals],
        [pl.BlockSpec((1, 1, 1, virtuals, virtuals), lambda s, k, mask: (0, s, k, 0, 0))],
        pl.BlockSpec((1, 1, virtuals, virtuals), lambda s, k, mask: (s, k, 0, 0)),
        out_shape,
        (slots, pairs),
        after=after,
    )


def product_kernel(sections, place_ref, *refs):
    own_refs, mirrored_refs, refs = refs[:sections], refs[sections : 2 * sections], refs[2 * sections :]
    masked_ref, out_refs, split_ref = refs[0], refs[1:-1], refs[-1]
    pairs, rows, _ = mirrored_refs[0].shape
    tall = sections * rows

    @pl.when((pl.program_id(0) == 0) & (pl.program_id(1) == 0))
    def _():
        for e in range(sections):
            for k in range(pairs):
                mixed = 2.0 * own_refs[e][0, k] - mirrored_refs[e][k]
                high = mixed.astype(jnp.bfloat16)
                low = (mixed - high.astype(jnp.float32)).astype(jnp.bfloat16)
                split_ref[k, pl.ds(e * rows, rows)] = high
                split_ref[k, pl.ds(tall + e * rows, rows)] = low

    total = None
    for k in range(pairs):
        both = jnp.dot(split_ref[k], masked_ref[0, k], preferred_element_type=jnp.float32)
        both = both[:tall] + both[tall:]
        total = both if total is None else total + both
    for e in range(sections):
        part = total[e * rows : (e + 1) * rows]
        if len(out_refs) == 1:
            out_refs[0][place_ref[0] ^ e, 0] = part
        else:
            out_refs[e][0] = part


def product(place, own, mirrored, masked, start, after, stacked):
    sections = len(mirrored)
    pairs, rows, virtuals = mirrored[0].shape
    slots = masked.shape[0]
    deep = virtuals // sections
    wide = min(virtuals, 512)
    if stacked:
        blocks = [pl.BlockSpec((sections, 1, rows, wide), lambda s, n, at: (0, s, 0, n))]
        shapes = [jax.ShapeDtypeStruct((sections, slots, rows, virtuals), jnp.float32)]
    else:
        blocks = [pl.BlockSpec((1, rows, wide), lambda s, n, at: (s, 0, n))] * sections
        shapes = [jax.ShapeDtypeStruct((slots, rows, virtuals), jnp.float32)] * sections
    return call(
        functools.partial(product_kernel, sections),
        "product",
        place,
        [own] * sections + list(mirrored) + [masked],
        [
            pl.BlockSpec(
                tuple(pl.Element(size) for size in (1, pairs, rows, virtuals)),
                lambda s, n, at, e=e: (0, 0, pl.multiple_of((at[0] ^ e) * deep + start, 8), 0),
            )
            for e in range(sections)
        ]
        + [whole(mirrored[0].shape)] * sections
        + [pl.BlockSpec((1, pairs, virtuals, wide), lambda s, n, at: (s, 0, 0, n))],
        blocks,
        shapes,
        (slots, virtuals // wide),
        scratch=[pltpu.VMEM((pairs, 2 * sections * rows, virtuals), jnp.bfloat16)],
        flops=4 * sections * rows * pairs * virtuals * virtuals * slots,
        after=after,
    )


def add_kernel(place_ref, *refs):
    refs[-1][...] = sum((part[...] for part in refs[1:-1]), refs[0][...])


def add(place, parts, after):
    slots, rows, virtuals = parts[0].shape
    block = pl.BlockSpec((1, rows, virtuals), lambda s, at: (s, 0, 0))
    return call(
        add_kernel,
        "add",
        place,
        parts,
        [block] * len(parts),
        block,
        jax.ShapeDtypeStruct(parts[0].shape, jnp.float32),
        (slots,),
        after=after,
    )


def cut_kernel(chunks, place_ref, *refs):
    total_refs, cut_refs = refs[:chunks], refs[chunks:]
    parts, _, _, wide = cut_refs[0].shape
    for e, cut_ref in enumerate(cut_refs):
        columns = pl.ds(pl.multiple_of((place_ref[0] ^ e) * wide, wide), wide)
        at = 0
        for total_ref in total_refs:
            short = total_ref.shape[1] // parts
            for part in range(parts):
                cut_ref[part, :, at : at + short] = total_ref[
                    :, part * short : (part + 1) * short, columns
                ]
            at += short


def cut(place, totals, sections, parts):
    slots, _, virtuals = totals[0].shape
    rows = sum(total.shape[1] for total in totals)
    shape = (parts, slots, rows // parts, virtuals // sections)
    return call(
        functools.partial(cut_kernel, len(totals)),
        "cut",
        place,
        totals,
        [whole(total.shape) for total in totals],
        [whole(shape)] * sections,
        [jax.ShapeDtypeStruct(shape, jnp.float32)] * sections,
        (1,),
    )


def hold_kernel(index_ref, out_ref):
    for at in range(out_ref.shape[0]):
        out_ref[at] = index_ref[at]


def hold(index, after):
    return call(
        hold_kernel,
        "hold",
        index,
        [],
        [],
        pl.BlockSpec(memory_space=pltpu.SMEM),
        jax.ShapeDtypeStruct(index.shape, index.dtype),
        (1,),
        after=after,
    )


def finish_kernel(spans, groups, place_ref, *refs):
    chunks = len(spans)
    own_refs, delivered_refs = refs[:chunks], refs[chunks : chunks + len(groups)]
    out_ref, columns_ref = refs[chunks + len(groups) :]
    wide = out_ref.shape[2]
    sections = columns_ref.shape[0] // wide
    for group, delivered_ref in zip(groups, delivered_refs):
        parts = delivered_ref.shape[0] // sections
        for e in range(sections):
            base = (place_ref[0] ^ e) * wide
            for part in range(parts):
                at = 0
                for chunk in group:
                    start, rows = spans[chunk]
                    short = rows // parts
                    spot = pl.multiple_of(base + start + part * short, 8)
                    columns_ref[pl.ds(spot, short)] = delivered_ref[
                        e * parts + part, 0, at : at + short
                    ]
                    at += short
    turned = columns_ref[...].T
    for (start, rows), own_ref in zip(spans, own_refs):
        out_ref[0, 0, start : start + rows] = own_ref[0] + turned[start : start + rows]


def finish(place, spans, groups, own, delivered):
    slots, _, virtuals = own[0].shape
    wide = delivered[0].shape[-1]
    return call(
        functools.partial(finish_kernel, spans, groups),
        "finish",
        place,
        list(own) + list(delivered),
        [pl.BlockSpec((1, *x.shape[1:]), lambda s, at: (s, 0, 0)) for x in own]
        + [
            pl.BlockSpec((x.shape[0], 1, *x.shape[2:]), lambda s, at: (0, s, 0, 0))
            for x in delivered
        ],
        pl.BlockSpec((1, 1, wide, virtuals), lambda s, at: (0, s, 0, 0)),
        jax.ShapeDtypeStruct((1, slots, wide, virtuals), jnp.float32),
        (slots,),
        scratch=[pltpu.VMEM((virtuals, wide), jnp.float32)],
    )


def swap(array, axis):
    return lax.all_to_all(array, axis, split_axis=0, concat_axis=0, tiled=True)


def spread(pieces):
    count = len(pieces)
    return [pieces[0]] + [
        lax.ppermute(pieces[e], "ka", [(q, q ^ e) for q in range(count)]) for e in range(1, count)
    ]


def body(sections, amplitudes, integrals, tile_mask, pair_list):
    _, pairs, virtuals, _ = amplitudes.shape
    occupied, slots = pair_list.shape
    wide = virtuals // sections
    sizes = [wide * part // sum(CHUNKS) for part in CHUNKS]
    spans = [(sum(sizes[:at]), size) for at, size in enumerate(sizes)]
    place = lax.axis_index("ka").astype(jnp.int32).reshape(1)

    owners = jnp.arange(occupied, dtype=jnp.int32)
    partner_slot = jnp.where(pair_list[pair_list, 0] == owners[:, None], 0, 1).astype(jnp.int32)
    source_row = (pair_list * slots + partner_slot).reshape(-1)

    def fetch(chunks, after):
        start, rows = spans[chunks[0]][0], sum(sizes[at] for at in chunks)
        pieces = [flip(place, amplitudes, sections, e, start, rows, after) for e in range(sections)]
        pieces = spread(pieces)
        return [
            functools.partial(part, place, pieces, spans[at][0] - start, sizes[at]) for at in chunks
        ]

    def hop(at):
        crossed = swap(across[at].reshape(occupied, sizes[at], virtuals), "ia")
        return crossed.reshape(sections, pairs, sizes[at], virtuals)

    def turn(at, crossed, after):
        pieces = scatter(place, crossed, after)
        return pieces[0], spread(pieces)

    def multiply(at, mirrored, after):
        stacked = at in SCATTERED
        parts = product(place, amplitudes, mirrored, masked, spans[at][0], after, stacked)
        if stacked:
            return parts[0], lax.psum_scatter(parts[0], "ka", scatter_dimension=0, tiled=False)
        return parts[0], add(place, spread(parts), [])

    def send(group):
        return spread(cut(place, [own[at] for at in group], sections, pairs))

    def meet(columns):
        return swap(columns.reshape(occupied, slots, *columns.shape[-2:]), "ia")

    def deliver(met, after):
        piece = met.shape[-2:]
        rows = hold(source_row, after)
        routed = jnp.take(met.reshape(occupied * slots, *piece), rows, axis=0)
        return swap(routed.reshape(occupied, slots, *piece), "ia")

    first = first_flip(place, amplitudes, sections, sizes[0])
    masked = mask_blocks(integrals, tile_mask, [first])
    across = [swap(first, "ka")]
    (second,) = fetch(SETS[1], [first])
    across.append(second([masked]))
    waiting = fetch(SETS[2], [across[1]])
    own = [None] * len(spans)
    turned, mirrored = turn(0, hop(0), [across[1]])
    begun, own[0] = multiply(0, mirrored, [])
    across.append(waiting[0]([begun]))
    turned, mirrored = turn(1, hop(1), [across[2]])
    turned, later = turn(2, hop(2), [turned])
    across.append(waiting[1]([turned, own[0]]))
    begun, own[1] = multiply(1, mirrored, [])
    crossed = hop(3)
    leading = gather(place, send(GROUPS[0]), [crossed, begun])
    turned, mirrored = turn(3, crossed, [leading])
    begun, own[2] = multiply(2, later, [turned])
    delivered = [deliver(meet(leading), [begun])]
    begun, own[3] = multiply(3, mirrored, delivered)
    after = [begun]
    for group in GROUPS[1:]:
        met = meet(gather(place, send(group), [delivered[-1], *after]))
        delivered.append(deliver(met, []))
        after = []
    return finish(place, spans, GROUPS, own, delivered)


def solution(mesh):
    placed = (
        P("ia", "ka", None, None),
        P("ia", None, "ka", None, None),
        P("ia", None, "ka", None, None),
        P(),
    )
    return jax.shard_map(
        functools.partial(body, mesh.shape["ka"]),
        mesh=mesh,
        in_specs=placed,
        out_specs=P("ia", None, "ka", None),
        check_vma=False,
    )
```

```python
import functools

import jax
import jax.numpy as jnp
from jax import lax
from jax.experimental import pallas as pl
from jax.experimental.pallas import tpu as pltpu
from jax.sharding import PartitionSpec as P

CHUNKS = (2, 3, 2, 1)
SETS = ((0,), (1,), (2, 3))
GROUPS = ((0,), (1,), (2, 3))
LANES = 128
VMEM_BYTES = 48 * 1024 * 1024


def call(
    kernel, name, scalars, operands, in_specs, out_specs, out_shape, grid, scratch=(), flops=0, after=()
):
    moved = sum(x.size * x.dtype.itemsize for x in jax.tree.leaves(out_shape)) * 2
    reads = 1 + len(operands)

    def trimmed(*refs):
        kernel(*refs[:reads], *refs[reads + len(after) :])

    return pl.pallas_call(
        trimmed,
        grid_spec=pltpu.PrefetchScalarGridSpec(
            num_scalar_prefetch=1,
            grid=grid,
            in_specs=list(in_specs) + [pl.BlockSpec(memory_space=pl.ANY)] * len(after),
            out_specs=out_specs,
            scratch_shapes=list(scratch),
        ),
        out_shape=out_shape,
        compiler_params=pltpu.CompilerParams(vmem_limit_bytes=VMEM_BYTES),
        cost_estimate=pl.CostEstimate(flops=flops, bytes_accessed=moved, transcendentals=0),
        name=name,
    )(scalars, *operands, *after)


def whole(shape):
    return pl.BlockSpec(shape, lambda *_: (0,) * len(shape))


def first_flip_kernel(place_ref, blocks_ref, piece_ref):
    piece_ref[0, 0] = blocks_ref[0, 0].T[: piece_ref.shape[2]]


def first_flip(place, amplitudes, sections, rows):
    pairs, virtuals = amplitudes.shape[1], amplitudes.shape[3]
    steps = virtuals // sections // LANES
    return call(
        first_flip_kernel,
        "first_flip",
        place,
        [amplitudes],
        [pl.BlockSpec((1, 1, virtuals, LANES), lambda d, q, at: (0, d, 0, q * steps))],
        pl.BlockSpec((1, 1, rows, virtuals), lambda d, q, at: (q, d, 0, 0)),
        jax.ShapeDtypeStruct((sections, pairs, rows, virtuals), jnp.float32),
        (pairs, sections),
    )


def flip_kernel(start, place_ref, blocks_ref, piece_ref):
    piece_ref[0] = blocks_ref[0, 0].T[start : start + piece_ref.shape[1]]


def flip(place, amplitudes, sections, e, start, rows, after):
    pairs, virtuals = amplitudes.shape[1], amplitudes.shape[3]
    wide = virtuals // sections
    return call(
        functools.partial(flip_kernel, start),
        "flip",
        place,
        [amplitudes],
        [pl.BlockSpec((1, 1, virtuals, wide), lambda d, at: (0, d, 0, at[0] ^ e))],
        pl.BlockSpec((1, rows, virtuals), lambda d, at: (d, 0, 0)),
        jax.ShapeDtypeStruct((pairs, rows, virtuals), jnp.float32),
        (pairs,),
        after=after,
    )


def part_kernel(start, place_ref, *refs):
    pieces, out_ref = refs[:-1], refs[-1]
    for e, piece in enumerate(pieces):
        out_ref[place_ref[0] ^ e, 0] = piece[0, start : start + out_ref.shape[2]]


def part(place, pieces, start, size, after):
    count, (pairs, rows, virtuals) = len(pieces), pieces[0].shape
    return call(
        functools.partial(part_kernel, start),
        "part",
        place,
        pieces,
        [pl.BlockSpec((1, rows, virtuals), lambda d, at: (d, 0, 0))] * count,
        pl.BlockSpec((count, 1, size, virtuals), lambda d, at: (0, d, 0, 0)),
        jax.ShapeDtypeStruct((count, pairs, size, virtuals), jnp.float32),
        (pairs,),
        after=after,
    )


def gather_kernel(place_ref, *refs):
    pieces, out_ref = refs[:-1], refs[-1]
    for e, piece in enumerate(pieces):
        out_ref[e] = piece[...]


def gather(place, pieces, after):
    shape = (len(pieces), *pieces[0].shape)
    return call(
        gather_kernel,
        "gather",
        place,
        pieces,
        [whole(pieces[0].shape)] * len(pieces),
        whole(shape),
        jax.ShapeDtypeStruct(shape, jnp.float32),
        (1,),
        after=after,
    )


def scatter_kernel(place_ref, stacked_ref, *pieces):
    for e, piece in enumerate(pieces):
        piece[...] = stacked_ref[place_ref[0] ^ e]


def scatter(place, stacked, after):
    count, shape = stacked.shape[0], stacked.shape[1:]
    return call(
        scatter_kernel,
        "scatter",
        place,
        [stacked],
        [whole(stacked.shape)],
        [whole(shape)] * count,
        [jax.ShapeDtypeStruct(shape, jnp.float32)] * count,
        (1,),
        after=after,
    )


def mask_kernel(tiles, mask_ref, integrals_ref, masked_ref):
    side = integrals_ref.shape[-1] // tiles
    slot, pair = pl.program_id(0), pl.program_id(1)
    for r in range(tiles):
        for c in range(tiles):
            keep = mask_ref[slot, pair, r, c] != 0
            spot = (pl.ds(r * side, side), pl.ds(c * side, side))
            tile = integrals_ref[0, 0, 0, spot[0], spot[1]]
            masked_ref[0, 0, spot[0], spot[1]] = jnp.where(keep, tile, jnp.zeros_like(tile))


def mask_blocks(integrals, tile_mask, after):
    _, slots, pairs, virtuals, _ = integrals.shape
    out_shape = jax.ShapeDtypeStruct((slots, pairs, virtuals, virtuals), jnp.bfloat16)
    return call(
        functools.partial(mask_kernel, tile_mask.shape[-1]),
        "mask",
        tile_mask[0],
        [integrals],
        [pl.BlockSpec((1, 1, 1, virtuals, virtuals), lambda s, k, mask: (0, s, k, 0, 0))],
        pl.BlockSpec((1, 1, virtuals, virtuals), lambda s, k, mask: (s, k, 0, 0)),
        out_shape,
        (slots, pairs),
        after=after,
    )


def product_kernel(sections, place_ref, *refs):
    own_refs, mirrored_refs, refs = refs[:sections], refs[sections : 2 * sections], refs[2 * sections :]
    masked_ref, out_ref, split_ref = refs
    pairs, rows, _ = mirrored_refs[0].shape
    tall = sections * rows

    @pl.when((pl.program_id(0) == 0) & (pl.program_id(1) == 0))
    def _():
        for e in range(sections):
            for k in range(pairs):
                mixed = 2.0 * own_refs[e][0, k] - mirrored_refs[e][k]
                high = mixed.astype(jnp.bfloat16)
                low = (mixed - high.astype(jnp.float32)).astype(jnp.bfloat16)
                split_ref[k, pl.ds(e * rows, rows)] = high
                split_ref[k, pl.ds(tall + e * rows, rows)] = low

    total = None
    for k in range(pairs):
        both = jnp.dot(split_ref[k], masked_ref[0, k], preferred_element_type=jnp.float32)
        both = both[:tall] + both[tall:]
        total = both if total is None else total + both
    for e in range(sections):
        out_ref[place_ref[0] ^ e, 0] = total[e * rows : (e + 1) * rows]


def product(place, own, mirrored, masked, start, after):
    sections = len(mirrored)
    pairs, rows, virtuals = mirrored[0].shape
    slots = masked.shape[0]
    deep = virtuals // sections
    wide = min(virtuals, 512)
    return call(
        functools.partial(product_kernel, sections),
        "product",
        place,
        [own] * sections + list(mirrored) + [masked],
        [
            pl.BlockSpec(
                tuple(pl.Element(size) for size in (1, pairs, rows, virtuals)),
                lambda s, n, at, e=e: (0, 0, pl.multiple_of((at[0] ^ e) * deep + start, 8), 0),
            )
            for e in range(sections)
        ]
        + [whole(mirrored[0].shape)] * sections
        + [pl.BlockSpec((1, pairs, virtuals, wide), lambda s, n, at: (s, 0, 0, n))],
        pl.BlockSpec((sections, 1, rows, wide), lambda s, n, at: (0, s, 0, n)),
        jax.ShapeDtypeStruct((sections, slots, rows, virtuals), jnp.float32),
        (slots, virtuals // wide),
        scratch=[pltpu.VMEM((pairs, 2 * sections * rows, virtuals), jnp.bfloat16)],
        flops=4 * sections * rows * pairs * virtuals * virtuals * slots,
        after=after,
    )


def cut_kernel(chunks, place_ref, *refs):
    total_refs, cut_refs = refs[:chunks], refs[chunks:]
    parts, _, _, wide = cut_refs[0].shape
    for e, cut_ref in enumerate(cut_refs):
        columns = pl.ds(pl.multiple_of((place_ref[0] ^ e) * wide, wide), wide)
        at = 0
        for total_ref in total_refs:
            short = total_ref.shape[1] // parts
            for part in range(parts):
                cut_ref[part, :, at : at + short] = total_ref[
                    :, part * short : (part + 1) * short, columns
                ]
            at += short


def cut(place, totals, sections, parts):
    slots, _, virtuals = totals[0].shape
    rows = sum(total.shape[1] for total in totals)
    shape = (parts, slots, rows // parts, virtuals // sections)
    return call(
        functools.partial(cut_kernel, len(totals)),
        "cut",
        place,
        totals,
        [whole(total.shape) for total in totals],
        [whole(shape)] * sections,
        [jax.ShapeDtypeStruct(shape, jnp.float32)] * sections,
        (1,),
    )


def finish_kernel(spans, groups, place_ref, *refs):
    chunks = len(spans)
    own_refs, delivered_refs = refs[:chunks], refs[chunks : chunks + len(groups)]
    out_ref, columns_ref = refs[chunks + len(groups) :]
    wide = out_ref.shape[2]
    sections = columns_ref.shape[0] // wide
    for group, delivered_ref in zip(groups, delivered_refs):
        parts = delivered_ref.shape[0] // sections
        for e in range(sections):
            base = (place_ref[0] ^ e) * wide
            for part in range(parts):
                at = 0
                for chunk in group:
                    start, rows = spans[chunk]
                    short = rows // parts
                    spot = pl.multiple_of(base + start + part * short, 8)
                    columns_ref[pl.ds(spot, short)] = delivered_ref[
                        e * parts + part, 0, at : at + short
                    ]
                    at += short
    turned = columns_ref[...].T
    for (start, rows), own_ref in zip(spans, own_refs):
        out_ref[0, 0, start : start + rows] = own_ref[0] + turned[start : start + rows]


def finish(place, spans, groups, own, delivered):
    slots, _, virtuals = own[0].shape
    wide = delivered[0].shape[-1]
    return call(
        functools.partial(finish_kernel, spans, groups),
        "finish",
        place,
        list(own) + list(delivered),
        [pl.BlockSpec((1, *x.shape[1:]), lambda s, at: (s, 0, 0)) for x in own]
        + [
            pl.BlockSpec((x.shape[0], 1, *x.shape[2:]), lambda s, at: (0, s, 0, 0))
            for x in delivered
        ],
        pl.BlockSpec((1, 1, wide, virtuals), lambda s, at: (0, s, 0, 0)),
        jax.ShapeDtypeStruct((1, slots, wide, virtuals), jnp.float32),
        (slots,),
        scratch=[pltpu.VMEM((virtuals, wide), jnp.float32)],
    )


def swap(array, axis):
    return lax.all_to_all(array, axis, split_axis=0, concat_axis=0, tiled=True)


def spread(pieces):
    count = len(pieces)
    return [pieces[0]] + [
        lax.ppermute(pieces[e], "ka", [(q, q ^ e) for q in range(count)]) for e in range(1, count)
    ]


def body(sections, amplitudes, integrals, tile_mask, pair_list):
    _, pairs, virtuals, _ = amplitudes.shape
    occupied, slots = pair_list.shape
    wide = virtuals // sections
    sizes = [wide * part // sum(CHUNKS) for part in CHUNKS]
    spans = [(sum(sizes[:at]), size) for at, size in enumerate(sizes)]
    place = lax.axis_index("ka").astype(jnp.int32).reshape(1)

    owners = jnp.arange(occupied, dtype=jnp.int32)
    partner_slot = jnp.where(pair_list[pair_list, 0] == owners[:, None], 0, 1).astype(jnp.int32)
    source_row = (pair_list * slots + partner_slot).reshape(-1)

    def fetch(chunks, after):
        start, rows = spans[chunks[0]][0], sum(sizes[at] for at in chunks)
        sent = [flip(place, amplitudes, sections, e, start, rows, after) for e in range(sections)]
        met = spread(sent)
        return sent, [
            functools.partial(part, place, met, spans[at][0] - start, sizes[at]) for at in chunks
        ]

    def hop(at):
        crossed = swap(across[at].reshape(occupied, sizes[at], virtuals), "ia")
        return crossed.reshape(sections, pairs, sizes[at], virtuals)

    def turn(at, crossed, after):
        pieces = scatter(place, crossed, after)
        return pieces[0], spread(pieces)

    def multiply(at, mirrored, after):
        parts = product(place, amplitudes, mirrored, masked, spans[at][0], after)
        return parts, lax.psum_scatter(parts, "ka", scatter_dimension=0, tiled=False)

    def send(group):
        return spread(cut(place, [own[at] for at in group], sections, pairs))

    def meet(columns):
        return swap(columns.reshape(occupied, slots, *columns.shape[-2:]), "ia")

    def deliver(met):
        piece = met.shape[-2:]
        routed = jnp.take(met.reshape(occupied * slots, *piece), source_row, axis=0)
        return swap(routed.reshape(occupied, slots, *piece), "ia")

    first = first_flip(place, amplitudes, sections, sizes[0])
    masked = mask_blocks(integrals, tile_mask, [first])
    across = [swap(first, "ka")]
    _, (second,) = fetch(SETS[1], [first])
    across.append(second([masked]))
    sent, (third, fourth) = fetch(SETS[2], [masked])
    own = [None] * len(spans)
    turned, mirrored = turn(0, hop(0), [across[1], *sent])
    across.append(third([]))
    begun, own[0] = multiply(0, mirrored, [across[2]])
    turned, mirrored = turn(1, hop(1), [begun])
    turned, later = turn(2, hop(2), [turned])
    leading = send(GROUPS[0])
    across.append(fourth([turned, *leading]))
    begun, own[1] = multiply(1, mirrored, [turned])
    crossed = hop(3)
    leading = gather(place, leading, [crossed, begun])
    turned, mirrored = turn(3, crossed, [leading])
    met = meet(leading)
    begun, own[2] = multiply(2, later, [turned, met])
    delivered = [deliver(met)]
    begun, own[3] = multiply(3, mirrored, [begun, *delivered])

    for group in GROUPS[1:]:
        met = meet(gather(place, send(group), [delivered[-1]]))
        delivered.append(deliver(met))
    return finish(place, spans, GROUPS, own, delivered)


def solution(mesh):
    placed = (
        P("ia", "ka", None, None),
        P("ia", None, "ka", None, None),
        P("ia", None, "ka", None, None),
        P(),
    )
    return jax.shard_map(
        functools.partial(body, mesh.shape["ka"]),
        mesh=mesh,
        in_specs=placed,
        out_specs=P("ia", None, "ka", None),
        check_vma=False,
    )
```

```python
import functools

import jax
import jax.numpy as jnp
from jax import lax
from jax.experimental import pallas as pl
from jax.experimental.pallas import tpu as pltpu
from jax.sharding import PartitionSpec as P

CHUNKS = (3, 3, 2)
GROUPS = ((0,), (1,), (2,))
LANES = 128
VMEM_BYTES = 48 * 1024 * 1024


def call(
    kernel, name, scalars, operands, in_specs, out_specs, out_shape, grid, scratch=(), flops=0, after=()
):
    moved = sum(x.size * x.dtype.itemsize for x in jax.tree.leaves(out_shape)) * 2
    reads = 1 + len(operands)

    def trimmed(*refs):
        kernel(*refs[:reads], *refs[reads + len(after) :])

    return pl.pallas_call(
        trimmed,
        grid_spec=pltpu.PrefetchScalarGridSpec(
            num_scalar_prefetch=1,
            grid=grid,
            in_specs=list(in_specs) + [pl.BlockSpec(memory_space=pl.ANY)] * len(after),
            out_specs=out_specs,
            scratch_shapes=list(scratch),
        ),
        out_shape=out_shape,
        compiler_params=pltpu.CompilerParams(vmem_limit_bytes=VMEM_BYTES),
        cost_estimate=pl.CostEstimate(flops=flops, bytes_accessed=moved, transcendentals=0),
        name=name,
    )(scalars, *operands, *after)


def whole(shape):
    return pl.BlockSpec(shape, lambda *_: (0,) * len(shape))


def first_flip_kernel(place_ref, blocks_ref, piece_ref):
    piece_ref[0, 0] = blocks_ref[0, 0].T[: piece_ref.shape[2]]


def first_flip(place, amplitudes, sections, rows):
    pairs, virtuals = amplitudes.shape[1], amplitudes.shape[3]
    steps = virtuals // sections // LANES
    return call(
        first_flip_kernel,
        "first_flip",
        place,
        [amplitudes],
        [pl.BlockSpec((1, 1, virtuals, LANES), lambda d, q, at: (0, d, 0, q * steps))],
        pl.BlockSpec((1, 1, rows, virtuals), lambda d, q, at: (q, d, 0, 0)),
        jax.ShapeDtypeStruct((sections, pairs, rows, virtuals), jnp.float32),
        (pairs, sections),
    )


def flip_kernel(start, place_ref, blocks_ref, piece_ref):
    piece_ref[0] = blocks_ref[0, 0].T[start : start + piece_ref.shape[1]]


def flip(place, amplitudes, sections, e, start, rows, after):
    pairs, virtuals = amplitudes.shape[1], amplitudes.shape[3]
    wide = virtuals // sections
    return call(
        functools.partial(flip_kernel, start),
        "flip",
        place,
        [amplitudes],
        [pl.BlockSpec((1, 1, virtuals, wide), lambda d, at: (0, d, 0, at[0] ^ e))],
        pl.BlockSpec((1, rows, virtuals), lambda d, at: (d, 0, 0)),
        jax.ShapeDtypeStruct((pairs, rows, virtuals), jnp.float32),
        (pairs,),
        after=after,
    )


def part_kernel(start, place_ref, *refs):
    pieces, out_ref = refs[:-1], refs[-1]
    for e, piece in enumerate(pieces):
        out_ref[place_ref[0] ^ e, 0] = piece[0, start : start + out_ref.shape[2]]


def part(place, pieces, start, size, after):
    count, (pairs, rows, virtuals) = len(pieces), pieces[0].shape
    return call(
        functools.partial(part_kernel, start),
        "part",
        place,
        pieces,
        [pl.BlockSpec((1, rows, virtuals), lambda d, at: (d, 0, 0))] * count,
        pl.BlockSpec((count, 1, size, virtuals), lambda d, at: (0, d, 0, 0)),
        jax.ShapeDtypeStruct((count, pairs, size, virtuals), jnp.float32),
        (pairs,),
        after=after,
    )


def gather_kernel(place_ref, *refs):
    pieces, out_ref = refs[:-1], refs[-1]
    for e, piece in enumerate(pieces):
        out_ref[e] = piece[...]


def gather(place, pieces, after):
    shape = (len(pieces), *pieces[0].shape)
    return call(
        gather_kernel,
        "gather",
        place,
        pieces,
        [whole(pieces[0].shape)] * len(pieces),
        whole(shape),
        jax.ShapeDtypeStruct(shape, jnp.float32),
        (1,),
        after=after,
    )


def scatter_kernel(place_ref, stacked_ref, *pieces):
    for e, piece in enumerate(pieces):
        piece[...] = stacked_ref[place_ref[0] ^ e]


def scatter(place, stacked, after):
    count, shape = stacked.shape[0], stacked.shape[1:]
    return call(
        scatter_kernel,
        "scatter",
        place,
        [stacked],
        [whole(stacked.shape)],
        [whole(shape)] * count,
        [jax.ShapeDtypeStruct(shape, jnp.float32)] * count,
        (1,),
        after=after,
    )


def mask_kernel(tiles, mask_ref, integrals_ref, masked_ref):
    side = integrals_ref.shape[-1] // tiles
    slot, pair = pl.program_id(0), pl.program_id(1)
    for r in range(tiles):
        for c in range(tiles):
            keep = mask_ref[slot, pair, r, c] != 0
            spot = (pl.ds(r * side, side), pl.ds(c * side, side))
            tile = integrals_ref[0, 0, 0, spot[0], spot[1]]
            masked_ref[0, 0, spot[0], spot[1]] = jnp.where(keep, tile, jnp.zeros_like(tile))


def mask_blocks(integrals, tile_mask, after):
    _, slots, pairs, virtuals, _ = integrals.shape
    out_shape = jax.ShapeDtypeStruct((slots, pairs, virtuals, virtuals), jnp.bfloat16)
    return call(
        functools.partial(mask_kernel, tile_mask.shape[-1]),
        "mask",
        tile_mask[0],
        [integrals],
        [pl.BlockSpec((1, 1, 1, virtuals, virtuals), lambda s, k, mask: (0, s, k, 0, 0))],
        pl.BlockSpec((1, 1, virtuals, virtuals), lambda s, k, mask: (s, k, 0, 0)),
        out_shape,
        (slots, pairs),
        after=after,
    )


def product_kernel(sections, place_ref, *refs):
    own_refs, mirrored_refs, refs = refs[:sections], refs[sections : 2 * sections], refs[2 * sections :]
    masked_ref, out_ref, split_ref = refs
    pairs, rows, _ = mirrored_refs[0].shape
    tall = sections * rows

    @pl.when((pl.program_id(0) == 0) & (pl.program_id(1) == 0))
    def _():
        for e in range(sections):
            for k in range(pairs):
                mixed = 2.0 * own_refs[e][0, k] - mirrored_refs[e][k]
                high = mixed.astype(jnp.bfloat16)
                low = (mixed - high.astype(jnp.float32)).astype(jnp.bfloat16)
                split_ref[k, pl.ds(e * rows, rows)] = high
                split_ref[k, pl.ds(tall + e * rows, rows)] = low

    total = None
    for k in range(pairs):
        both = jnp.dot(split_ref[k], masked_ref[0, k], preferred_element_type=jnp.float32)
        both = both[:tall] + both[tall:]
        total = both if total is None else total + both
    for e in range(sections):
        out_ref[place_ref[0] ^ e, 0] = total[e * rows : (e + 1) * rows]


def product(place, own, mirrored, masked, start, after):
    sections = len(mirrored)
    pairs, rows, virtuals = mirrored[0].shape
    slots = masked.shape[0]
    deep = virtuals // sections
    wide = min(virtuals, 512)
    return call(
        functools.partial(product_kernel, sections),
        "product",
        place,
        [own] * sections + list(mirrored) + [masked],
        [
            pl.BlockSpec(
                tuple(pl.Element(size) for size in (1, pairs, rows, virtuals)),
                lambda s, n, at, e=e: (0, 0, pl.multiple_of((at[0] ^ e) * deep + start, 8), 0),
            )
            for e in range(sections)
        ]
        + [whole(mirrored[0].shape)] * sections
        + [pl.BlockSpec((1, pairs, virtuals, wide), lambda s, n, at: (s, 0, 0, n))],
        pl.BlockSpec((sections, 1, rows, wide), lambda s, n, at: (0, s, 0, n)),
        jax.ShapeDtypeStruct((sections, slots, rows, virtuals), jnp.float32),
        (slots, virtuals // wide),
        scratch=[pltpu.VMEM((pairs, 2 * sections * rows, virtuals), jnp.bfloat16)],
        flops=4 * sections * rows * pairs * virtuals * virtuals * slots,
        after=after,
    )


def cut_kernel(chunks, place_ref, *refs):
    total_refs, cut_refs = refs[:chunks], refs[chunks:]
    parts, _, _, wide = cut_refs[0].shape
    for e, cut_ref in enumerate(cut_refs):
        columns = pl.ds(pl.multiple_of((place_ref[0] ^ e) * wide, wide), wide)
        at = 0
        for total_ref in total_refs:
            short = total_ref.shape[1] // parts
            for part in range(parts):
                cut_ref[part, :, at : at + short] = total_ref[
                    :, part * short : (part + 1) * short, columns
                ]
            at += short


def cut(place, totals, sections, parts):
    slots, _, virtuals = totals[0].shape
    rows = sum(total.shape[1] for total in totals)
    shape = (parts, slots, rows // parts, virtuals // sections)
    return call(
        functools.partial(cut_kernel, len(totals)),
        "cut",
        place,
        totals,
        [whole(total.shape) for total in totals],
        [whole(shape)] * sections,
        [jax.ShapeDtypeStruct(shape, jnp.float32)] * sections,
        (1,),
    )


def finish_kernel(spans, groups, place_ref, *refs):
    chunks = len(spans)
    own_refs, delivered_refs = refs[:chunks], refs[chunks : chunks + len(groups)]
    out_ref, columns_ref = refs[chunks + len(groups) :]
    wide = out_ref.shape[2]
    sections = columns_ref.shape[0] // wide
    for group, delivered_ref in zip(groups, delivered_refs):
        parts = delivered_ref.shape[0] // sections
        for e in range(sections):
            base = (place_ref[0] ^ e) * wide
            for part in range(parts):
                at = 0
                for chunk in group:
                    start, rows = spans[chunk]
                    short = rows // parts
                    spot = pl.multiple_of(base + start + part * short, 8)
                    columns_ref[pl.ds(spot, short)] = delivered_ref[
                        e * parts + part, 0, at : at + short
                    ]
                    at += short
    turned = columns_ref[...].T
    for (start, rows), own_ref in zip(spans, own_refs):
        out_ref[0, 0, start : start + rows] = own_ref[0] + turned[start : start + rows]


def finish(place, spans, groups, own, delivered):
    slots, _, virtuals = own[0].shape
    wide = delivered[0].shape[-1]
    return call(
        functools.partial(finish_kernel, spans, groups),
        "finish",
        place,
        list(own) + list(delivered),
        [pl.BlockSpec((1, *x.shape[1:]), lambda s, at: (s, 0, 0)) for x in own]
        + [
            pl.BlockSpec((x.shape[0], 1, *x.shape[2:]), lambda s, at: (0, s, 0, 0))
            for x in delivered
        ],
        pl.BlockSpec((1, 1, wide, virtuals), lambda s, at: (0, s, 0, 0)),
        jax.ShapeDtypeStruct((1, slots, wide, virtuals), jnp.float32),
        (slots,),
        scratch=[pltpu.VMEM((virtuals, wide), jnp.float32)],
    )


def swap(array, axis):
    return lax.all_to_all(array, axis, split_axis=0, concat_axis=0, tiled=True)


def spread(pieces):
    count = len(pieces)
    return [pieces[0]] + [
        lax.ppermute(pieces[e], "ka", [(q, q ^ e) for q in range(count)]) for e in range(1, count)
    ]


def body(sections, amplitudes, integrals, tile_mask, pair_list):
    _, pairs, virtuals, _ = amplitudes.shape
    occupied, slots = pair_list.shape
    wide = virtuals // sections
    sizes = [wide * part // sum(CHUNKS) for part in CHUNKS]
    spans = [(sum(sizes[:at]), size) for at, size in enumerate(sizes)]
    place = lax.axis_index("ka").astype(jnp.int32).reshape(1)

    owners = jnp.arange(occupied, dtype=jnp.int32)
    partner_slot = jnp.where(pair_list[pair_list, 0] == owners[:, None], 0, 1).astype(jnp.int32)
    source_row = (pair_list * slots + partner_slot).reshape(-1)

    def fetch(chunks, after):
        start, rows = spans[chunks[0]][0], sum(sizes[at] for at in chunks)
        met = spread(
            [flip(place, amplitudes, sections, e, start, rows, after) for e in range(sections)]
        )
        return [
            functools.partial(part, place, met, spans[at][0] - start, sizes[at]) for at in chunks
        ]

    def hop(at):
        crossed = swap(across[at].reshape(occupied, sizes[at], virtuals), "ia")
        return crossed.reshape(sections, pairs, sizes[at], virtuals)

    def turn(at, crossed, after):
        pieces = scatter(place, crossed, after)
        return pieces[0], spread(pieces)

    def multiply(at, mirrored, after):
        parts = product(place, amplitudes, mirrored, masked, spans[at][0], after)
        return parts, lax.psum_scatter(parts, "ka", scatter_dimension=0, tiled=False)

    def send(group):
        return spread(cut(place, [own[at] for at in group], sections, pairs))

    def meet(columns):
        return swap(columns.reshape(occupied, slots, *columns.shape[-2:]), "ia")

    def deliver(met):
        piece = met.shape[-2:]
        routed = jnp.take(met.reshape(occupied * slots, *piece), source_row, axis=0)
        return swap(routed.reshape(occupied, slots, *piece), "ia")

    first = first_flip(place, amplitudes, sections, sizes[0])
    masked = mask_blocks(integrals, tile_mask, [first])
    across = [swap(first, "ka")]
    second, third = fetch((1, 2), [first])
    own = [None] * len(spans)
    across += [second([masked]), third([masked])]
    turned, early = turn(0, hop(0), across[1:2])
    turned, middle = turn(1, hop(1), [turned])
    _, own[0] = multiply(0, early, [turned])
    crossed = hop(2)
    turned, late = turn(2, crossed, [turned])
    begun, own[1] = multiply(1, middle, [turned])
    met = meet(gather(place, send(GROUPS[0]), [crossed]))
    _, own[2] = multiply(2, late, [begun, met])
    delivered = [deliver(met)]
    for group in GROUPS[1:]:
        met = meet(gather(place, send(group), [delivered[-1]]))
        delivered.append(deliver(met))
    return finish(place, spans, GROUPS, own, delivered)


def solution(mesh):
    placed = (
        P("ia", "ka", None, None),
        P("ia", None, "ka", None, None),
        P("ia", None, "ka", None, None),
        P(),
    )
    return jax.shard_map(
        functools.partial(body, mesh.shape["ka"]),
        mesh=mesh,
        in_specs=placed,
        out_specs=P("ia", None, "ka", None),
        check_vma=False,
    )
```

```python
import functools

import jax
import jax.numpy as jnp
from jax import lax
from jax.experimental import pallas as pl
from jax.experimental.pallas import tpu as pltpu
from jax.sharding import PartitionSpec as P

CHUNKS = (3, 3, 2)
GROUPS = ((0,), (1,), (2,))
LANES = 128
VMEM_BYTES = 48 * 1024 * 1024


def call(
    kernel, name, scalars, operands, in_specs, out_specs, out_shape, grid, scratch=(), flops=0, after=()
):
    moved = sum(x.size * x.dtype.itemsize for x in jax.tree.leaves(out_shape)) * 2
    reads = 1 + len(operands)

    def trimmed(*refs):
        kernel(*refs[:reads], *refs[reads + len(after) :])

    return pl.pallas_call(
        trimmed,
        grid_spec=pltpu.PrefetchScalarGridSpec(
            num_scalar_prefetch=1,
            grid=grid,
            in_specs=list(in_specs) + [pl.BlockSpec(memory_space=pl.ANY)] * len(after),
            out_specs=out_specs,
            scratch_shapes=list(scratch),
        ),
        out_shape=out_shape,
        compiler_params=pltpu.CompilerParams(vmem_limit_bytes=VMEM_BYTES),
        cost_estimate=pl.CostEstimate(flops=flops, bytes_accessed=moved, transcendentals=0),
        name=name,
    )(scalars, *operands, *after)


def whole(shape):
    return pl.BlockSpec(shape, lambda *_: (0,) * len(shape))


def first_flip_kernel(place_ref, blocks_ref, piece_ref):
    piece_ref[0, 0] = blocks_ref[0, 0].T[: piece_ref.shape[2]]


def first_flip(place, amplitudes, sections, rows):
    pairs, virtuals = amplitudes.shape[1], amplitudes.shape[3]
    steps = virtuals // sections // LANES
    return call(
        first_flip_kernel,
        "first_flip",
        place,
        [amplitudes],
        [pl.BlockSpec((1, 1, virtuals, LANES), lambda d, q, at: (0, d, 0, q * steps))],
        pl.BlockSpec((1, 1, rows, virtuals), lambda d, q, at: (q, d, 0, 0)),
        jax.ShapeDtypeStruct((sections, pairs, rows, virtuals), jnp.float32),
        (pairs, sections),
    )


def flip_kernel(start, place_ref, blocks_ref, piece_ref):
    piece_ref[0] = blocks_ref[0, 0].T[start : start + piece_ref.shape[1]]


def flip(place, amplitudes, sections, e, start, rows, after):
    pairs, virtuals = amplitudes.shape[1], amplitudes.shape[3]
    wide = virtuals // sections
    return call(
        functools.partial(flip_kernel, start),
        "flip",
        place,
        [amplitudes],
        [pl.BlockSpec((1, 1, virtuals, wide), lambda d, at: (0, d, 0, at[0] ^ e))],
        pl.BlockSpec((1, rows, virtuals), lambda d, at: (d, 0, 0)),
        jax.ShapeDtypeStruct((pairs, rows, virtuals), jnp.float32),
        (pairs,),
        after=after,
    )


def part_kernel(start, place_ref, *refs):
    pieces, out_ref = refs[:-1], refs[-1]
    for e, piece in enumerate(pieces):
        out_ref[place_ref[0] ^ e, 0] = piece[0, start : start + out_ref.shape[2]]


def part(place, pieces, start, size, after):
    count, (pairs, rows, virtuals) = len(pieces), pieces[0].shape
    return call(
        functools.partial(part_kernel, start),
        "part",
        place,
        pieces,
        [pl.BlockSpec((1, rows, virtuals), lambda d, at: (d, 0, 0))] * count,
        pl.BlockSpec((count, 1, size, virtuals), lambda d, at: (0, d, 0, 0)),
        jax.ShapeDtypeStruct((count, pairs, size, virtuals), jnp.float32),
        (pairs,),
        after=after,
    )


def gather_kernel(place_ref, *refs):
    pieces, out_ref = refs[:-1], refs[-1]
    for e, piece in enumerate(pieces):
        out_ref[e] = piece[...]


def gather(place, pieces, after):
    shape = (len(pieces), *pieces[0].shape)
    return call(
        gather_kernel,
        "gather",
        place,
        pieces,
        [whole(pieces[0].shape)] * len(pieces),
        whole(shape),
        jax.ShapeDtypeStruct(shape, jnp.float32),
        (1,),
        after=after,
    )


def scatter_kernel(place_ref, stacked_ref, *pieces):
    for e, piece in enumerate(pieces):
        piece[...] = stacked_ref[place_ref[0] ^ e]


def scatter(place, stacked, after):
    count, shape = stacked.shape[0], stacked.shape[1:]
    return call(
        scatter_kernel,
        "scatter",
        place,
        [stacked],
        [whole(stacked.shape)],
        [whole(shape)] * count,
        [jax.ShapeDtypeStruct(shape, jnp.float32)] * count,
        (1,),
        after=after,
    )


def mask_kernel(tiles, mask_ref, integrals_ref, masked_ref):
    side = integrals_ref.shape[-1] // tiles
    slot, pair = pl.program_id(0), pl.program_id(1)
    for r in range(tiles):
        for c in range(tiles):
            keep = mask_ref[slot, pair, r, c] != 0
            spot = (pl.ds(r * side, side), pl.ds(c * side, side))
            tile = integrals_ref[0, 0, 0, spot[0], spot[1]]
            masked_ref[0, 0, spot[0], spot[1]] = jnp.where(keep, tile, jnp.zeros_like(tile))


def mask_blocks(integrals, tile_mask, after):
    _, slots, pairs, virtuals, _ = integrals.shape
    out_shape = jax.ShapeDtypeStruct((slots, pairs, virtuals, virtuals), jnp.bfloat16)
    return call(
        functools.partial(mask_kernel, tile_mask.shape[-1]),
        "mask",
        tile_mask[0],
        [integrals],
        [pl.BlockSpec((1, 1, 1, virtuals, virtuals), lambda s, k, mask: (0, s, k, 0, 0))],
        pl.BlockSpec((1, 1, virtuals, virtuals), lambda s, k, mask: (s, k, 0, 0)),
        out_shape,
        (slots, pairs),
        after=after,
    )


def product_kernel(sections, place_ref, *refs):
    own_refs, mirrored_refs, refs = refs[:sections], refs[sections : 2 * sections], refs[2 * sections :]
    masked_ref, out_ref, split_ref = refs
    pairs, rows, _ = mirrored_refs[0].shape
    tall = sections * rows

    @pl.when((pl.program_id(0) == 0) & (pl.program_id(1) == 0))
    def _():
        for e in range(sections):
            for k in range(pairs):
                mixed = 2.0 * own_refs[e][0, k] - mirrored_refs[e][k]
                high = mixed.astype(jnp.bfloat16)
                low = (mixed - high.astype(jnp.float32)).astype(jnp.bfloat16)
                split_ref[k, pl.ds(e * rows, rows)] = high
                split_ref[k, pl.ds(tall + e * rows, rows)] = low

    total = None
    for k in range(pairs):
        both = jnp.dot(split_ref[k], masked_ref[0, k], preferred_element_type=jnp.float32)
        both = both[:tall] + both[tall:]
        total = both if total is None else total + both
    for e in range(sections):
        out_ref[place_ref[0] ^ e, 0] = total[e * rows : (e + 1) * rows]


def product(place, own, mirrored, masked, start, after):
    sections = len(mirrored)
    pairs, rows, virtuals = mirrored[0].shape
    slots = masked.shape[0]
    deep = virtuals // sections
    wide = min(virtuals, 512)
    return call(
        functools.partial(product_kernel, sections),
        "product",
        place,
        [own] * sections + list(mirrored) + [masked],
        [
            pl.BlockSpec(
                tuple(pl.Element(size) for size in (1, pairs, rows, virtuals)),
                lambda s, n, at, e=e: (0, 0, pl.multiple_of((at[0] ^ e) * deep + start, 8), 0),
            )
            for e in range(sections)
        ]
        + [whole(mirrored[0].shape)] * sections
        + [pl.BlockSpec((1, pairs, virtuals, wide), lambda s, n, at: (s, 0, 0, n))],
        pl.BlockSpec((sections, 1, rows, wide), lambda s, n, at: (0, s, 0, n)),
        jax.ShapeDtypeStruct((sections, slots, rows, virtuals), jnp.float32),
        (slots, virtuals // wide),
        scratch=[pltpu.VMEM((pairs, 2 * sections * rows, virtuals), jnp.bfloat16)],
        flops=4 * sections * rows * pairs * virtuals * virtuals * slots,
        after=after,
    )


def cut_kernel(chunks, place_ref, *refs):
    total_refs, cut_refs = refs[:chunks], refs[chunks:]
    parts, _, _, wide = cut_refs[0].shape
    for e, cut_ref in enumerate(cut_refs):
        columns = pl.ds(pl.multiple_of((place_ref[0] ^ e) * wide, wide), wide)
        at = 0
        for total_ref in total_refs:
            short = total_ref.shape[1] // parts
            for part in range(parts):
                cut_ref[part, :, at : at + short] = total_ref[
                    :, part * short : (part + 1) * short, columns
                ]
            at += short


def cut(place, totals, sections, parts):
    slots, _, virtuals = totals[0].shape
    rows = sum(total.shape[1] for total in totals)
    shape = (parts, slots, rows // parts, virtuals // sections)
    return call(
        functools.partial(cut_kernel, len(totals)),
        "cut",
        place,
        totals,
        [whole(total.shape) for total in totals],
        [whole(shape)] * sections,
        [jax.ShapeDtypeStruct(shape, jnp.float32)] * sections,
        (1,),
    )


def finish_kernel(spans, groups, place_ref, *refs):
    chunks = len(spans)
    own_refs, delivered_refs = refs[:chunks], refs[chunks : chunks + len(groups)]
    out_ref, columns_ref = refs[chunks + len(groups) :]
    wide = out_ref.shape[2]
    sections = columns_ref.shape[0] // wide
    for group, delivered_ref in zip(groups, delivered_refs):
        parts = delivered_ref.shape[0] // sections
        for e in range(sections):
            base = (place_ref[0] ^ e) * wide
            for part in range(parts):
                at = 0
                for chunk in group:
                    start, rows = spans[chunk]
                    short = rows // parts
                    spot = pl.multiple_of(base + start + part * short, 8)
                    columns_ref[pl.ds(spot, short)] = delivered_ref[
                        e * parts + part, 0, at : at + short
                    ]
                    at += short
    turned = columns_ref[...].T
    for (start, rows), own_ref in zip(spans, own_refs):
        out_ref[0, 0, start : start + rows] = own_ref[0] + turned[start : start + rows]


def finish(place, spans, groups, own, delivered):
    slots, _, virtuals = own[0].shape
    wide = delivered[0].shape[-1]
    return call(
        functools.partial(finish_kernel, spans, groups),
        "finish",
        place,
        list(own) + list(delivered),
        [pl.BlockSpec((1, *x.shape[1:]), lambda s, at: (s, 0, 0)) for x in own]
        + [
            pl.BlockSpec((x.shape[0], 1, *x.shape[2:]), lambda s, at: (0, s, 0, 0))
            for x in delivered
        ],
        pl.BlockSpec((1, 1, wide, virtuals), lambda s, at: (0, s, 0, 0)),
        jax.ShapeDtypeStruct((1, slots, wide, virtuals), jnp.float32),
        (slots,),
        scratch=[pltpu.VMEM((virtuals, wide), jnp.float32)],
    )


def swap(array, axis):
    return lax.all_to_all(array, axis, split_axis=0, concat_axis=0, tiled=True)


def spread(pieces):
    count = len(pieces)
    return [pieces[0]] + [
        lax.ppermute(pieces[e], "ka", [(q, q ^ e) for q in range(count)]) for e in range(1, count)
    ]


def body(sections, amplitudes, integrals, tile_mask, pair_list):
    _, pairs, virtuals, _ = amplitudes.shape
    occupied, slots = pair_list.shape
    wide = virtuals // sections
    sizes = [wide * part // sum(CHUNKS) for part in CHUNKS]
    spans = [(sum(sizes[:at]), size) for at, size in enumerate(sizes)]
    place = lax.axis_index("ka").astype(jnp.int32).reshape(1)

    owners = jnp.arange(occupied, dtype=jnp.int32)
    partner_slot = jnp.where(pair_list[pair_list, 0] == owners[:, None], 0, 1).astype(jnp.int32)
    source_row = (pair_list * slots + partner_slot).reshape(-1)

    def fetch(chunks, after):
        start, rows = spans[chunks[0]][0], sum(sizes[at] for at in chunks)
        met = spread(
            [flip(place, amplitudes, sections, e, start, rows, after) for e in range(sections)]
        )
        return [
            functools.partial(part, place, met, spans[at][0] - start, sizes[at]) for at in chunks
        ]

    def hop(at):
        crossed = swap(across[at].reshape(occupied, sizes[at], virtuals), "ia")
        return crossed.reshape(sections, pairs, sizes[at], virtuals)

    def turn(at, crossed, after):
        pieces = scatter(place, crossed, after)
        return pieces[0], spread(pieces)

    def multiply(at, mirrored, after):
        parts = product(place, amplitudes, mirrored, masked, spans[at][0], after)
        return parts, lax.psum_scatter(parts, "ka", scatter_dimension=0, tiled=False)

    def send(group):
        return spread(cut(place, [own[at] for at in group], sections, pairs))

    def meet(columns):
        return swap(columns.reshape(occupied, slots, *columns.shape[-2:]), "ia")

    def deliver(met):
        piece = met.shape[-2:]
        routed = jnp.take(met.reshape(occupied * slots, *piece), source_row, axis=0)
        return swap(routed.reshape(occupied, slots, *piece), "ia")

    first = first_flip(place, amplitudes, sections, sizes[0])
    masked = mask_blocks(integrals, tile_mask, [first])
    across = [swap(first, "ka")]
    second, third = fetch((1, 2), [first])
    own = [None] * len(spans)
    across += [second([masked]), third([masked])]
    turned, early = turn(0, hop(0), across[1:])
    begun, own[0] = multiply(0, early, [])
    turned, middle = turn(1, hop(1), [begun])
    leading = send(GROUPS[0])
    crossed = hop(2)
    turned, late = turn(2, crossed, [turned, *leading])
    begun, own[1] = multiply(1, middle, [turned])
    met = meet(gather(place, leading, [crossed]))
    _, own[2] = multiply(2, late, [begun, met])
    delivered = [deliver(met)]
    for group in GROUPS[1:]:
        met = meet(gather(place, send(group), [delivered[-1]]))
        delivered.append(deliver(met))
    return finish(place, spans, GROUPS, own, delivered)


def solution(mesh):
    placed = (
        P("ia", "ka", None, None),
        P("ia", None, "ka", None, None),
        P("ia", None, "ka", None, None),
        P(),
    )
    return jax.shard_map(
        functools.partial(body, mesh.shape["ka"]),
        mesh=mesh,
        in_specs=placed,
        out_specs=P("ia", None, "ka", None),
        check_vma=False,
    )
```

```python
import functools

import jax
import jax.numpy as jnp
from jax import lax
from jax.experimental import pallas as pl
from jax.experimental.pallas import tpu as pltpu
from jax.sharding import PartitionSpec as P

CHUNKS = (3, 3, 2)
GROUPS = ((0,), (1,), (2,))
LANES = 128
VMEM_BYTES = 48 * 1024 * 1024


def call(
    kernel, name, scalars, operands, in_specs, out_specs, out_shape, grid, scratch=(), flops=0, after=()
):
    moved = sum(x.size * x.dtype.itemsize for x in jax.tree.leaves(out_shape)) * 2
    reads = 1 + len(operands)

    def trimmed(*refs):
        kernel(*refs[:reads], *refs[reads + len(after) :])

    return pl.pallas_call(
        trimmed,
        grid_spec=pltpu.PrefetchScalarGridSpec(
            num_scalar_prefetch=1,
            grid=grid,
            in_specs=list(in_specs) + [pl.BlockSpec(memory_space=pl.ANY)] * len(after),
            out_specs=out_specs,
            scratch_shapes=list(scratch),
        ),
        out_shape=out_shape,
        compiler_params=pltpu.CompilerParams(vmem_limit_bytes=VMEM_BYTES),
        cost_estimate=pl.CostEstimate(flops=flops, bytes_accessed=moved, transcendentals=0),
        name=name,
    )(scalars, *operands, *after)


def whole(shape):
    return pl.BlockSpec(shape, lambda *_: (0,) * len(shape))


def first_flip_kernel(place_ref, blocks_ref, piece_ref):
    piece_ref[0, 0] = blocks_ref[0, 0].T[: piece_ref.shape[2]]


def first_flip(place, amplitudes, sections, rows):
    pairs, virtuals = amplitudes.shape[1], amplitudes.shape[3]
    steps = virtuals // sections // LANES
    return call(
        first_flip_kernel,
        "first_flip",
        place,
        [amplitudes],
        [pl.BlockSpec((1, 1, virtuals, LANES), lambda d, q, at: (0, d, 0, q * steps))],
        pl.BlockSpec((1, 1, rows, virtuals), lambda d, q, at: (q, d, 0, 0)),
        jax.ShapeDtypeStruct((sections, pairs, rows, virtuals), jnp.float32),
        (pairs, sections),
    )


def flip_kernel(start, place_ref, blocks_ref, piece_ref):
    piece_ref[0] = blocks_ref[0, 0].T[start : start + piece_ref.shape[1]]


def flip(place, amplitudes, sections, e, start, rows, after):
    pairs, virtuals = amplitudes.shape[1], amplitudes.shape[3]
    wide = virtuals // sections
    return call(
        functools.partial(flip_kernel, start),
        "flip",
        place,
        [amplitudes],
        [pl.BlockSpec((1, 1, virtuals, wide), lambda d, at: (0, d, 0, at[0] ^ e))],
        pl.BlockSpec((1, rows, virtuals), lambda d, at: (d, 0, 0)),
        jax.ShapeDtypeStruct((pairs, rows, virtuals), jnp.float32),
        (pairs,),
        after=after,
    )


def part_kernel(start, place_ref, *refs):
    pieces, out_ref = refs[:-1], refs[-1]
    for e, piece in enumerate(pieces):
        out_ref[place_ref[0] ^ e, 0] = piece[0, start : start + out_ref.shape[2]]


def part(place, pieces, start, size, after):
    count, (pairs, rows, virtuals) = len(pieces), pieces[0].shape
    return call(
        functools.partial(part_kernel, start),
        "part",
        place,
        pieces,
        [pl.BlockSpec((1, rows, virtuals), lambda d, at: (d, 0, 0))] * count,
        pl.BlockSpec((count, 1, size, virtuals), lambda d, at: (0, d, 0, 0)),
        jax.ShapeDtypeStruct((count, pairs, size, virtuals), jnp.float32),
        (pairs,),
        after=after,
    )


def gather_kernel(place_ref, *refs):
    pieces, out_ref = refs[:-1], refs[-1]
    for e, piece in enumerate(pieces):
        out_ref[e] = piece[...]


def gather(place, pieces, after):
    shape = (len(pieces), *pieces[0].shape)
    return call(
        gather_kernel,
        "gather",
        place,
        pieces,
        [whole(pieces[0].shape)] * len(pieces),
        whole(shape),
        jax.ShapeDtypeStruct(shape, jnp.float32),
        (1,),
        after=after,
    )


def scatter_kernel(place_ref, stacked_ref, *pieces):
    for e, piece in enumerate(pieces):
        piece[...] = stacked_ref[place_ref[0] ^ e]


def scatter(place, stacked, after):
    count, shape = stacked.shape[0], stacked.shape[1:]
    return call(
        scatter_kernel,
        "scatter",
        place,
        [stacked],
        [whole(stacked.shape)],
        [whole(shape)] * count,
        [jax.ShapeDtypeStruct(shape, jnp.float32)] * count,
        (1,),
        after=after,
    )


def mask_kernel(tiles, mask_ref, integrals_ref, masked_ref):
    side = integrals_ref.shape[-1] // tiles
    slot, pair = pl.program_id(0), pl.program_id(1)
    for r in range(tiles):
        for c in range(tiles):
            keep = mask_ref[slot, pair, r, c] != 0
            spot = (pl.ds(r * side, side), pl.ds(c * side, side))
            tile = integrals_ref[0, 0, 0, spot[0], spot[1]]
            masked_ref[0, 0, spot[0], spot[1]] = jnp.where(keep, tile, jnp.zeros_like(tile))


def mask_blocks(integrals, tile_mask, after):
    _, slots, pairs, virtuals, _ = integrals.shape
    out_shape = jax.ShapeDtypeStruct((slots, pairs, virtuals, virtuals), jnp.bfloat16)
    return call(
        functools.partial(mask_kernel, tile_mask.shape[-1]),
        "mask",
        tile_mask[0],
        [integrals],
        [pl.BlockSpec((1, 1, 1, virtuals, virtuals), lambda s, k, mask: (0, s, k, 0, 0))],
        pl.BlockSpec((1, 1, virtuals, virtuals), lambda s, k, mask: (s, k, 0, 0)),
        out_shape,
        (slots, pairs),
        after=after,
    )


def product_kernel(sections, place_ref, *refs):
    own_refs, mirrored_refs, refs = refs[:sections], refs[sections : 2 * sections], refs[2 * sections :]
    masked_ref, out_ref, split_ref = refs
    pairs, rows, _ = mirrored_refs[0].shape
    tall = sections * rows

    @pl.when((pl.program_id(0) == 0) & (pl.program_id(1) == 0))
    def _():
        for e in range(sections):
            for k in range(pairs):
                mixed = 2.0 * own_refs[e][0, k] - mirrored_refs[e][k]
                high = mixed.astype(jnp.bfloat16)
                low = (mixed - high.astype(jnp.float32)).astype(jnp.bfloat16)
                split_ref[k, pl.ds(e * rows, rows)] = high
                split_ref[k, pl.ds(tall + e * rows, rows)] = low

    total = None
    for k in range(pairs):
        both = jnp.dot(split_ref[k], masked_ref[0, k], preferred_element_type=jnp.float32)
        both = both[:tall] + both[tall:]
        total = both if total is None else total + both
    for e in range(sections):
        out_ref[place_ref[0] ^ e, 0] = total[e * rows : (e + 1) * rows]


def product(place, own, mirrored, masked, start, after):
    sections = len(mirrored)
    pairs, rows, virtuals = mirrored[0].shape
    slots = masked.shape[0]
    deep = virtuals // sections
    wide = min(virtuals, 512)
    return call(
        functools.partial(product_kernel, sections),
        "product",
        place,
        [own] * sections + list(mirrored) + [masked],
        [
            pl.BlockSpec(
                tuple(pl.Element(size) for size in (1, pairs, rows, virtuals)),
                lambda s, n, at, e=e: (0, 0, pl.multiple_of((at[0] ^ e) * deep + start, 8), 0),
            )
            for e in range(sections)
        ]
        + [whole(mirrored[0].shape)] * sections
        + [pl.BlockSpec((1, pairs, virtuals, wide), lambda s, n, at: (s, 0, 0, n))],
        pl.BlockSpec((sections, 1, rows, wide), lambda s, n, at: (0, s, 0, n)),
        jax.ShapeDtypeStruct((sections, slots, rows, virtuals), jnp.float32),
        (slots, virtuals // wide),
        scratch=[pltpu.VMEM((pairs, 2 * sections * rows, virtuals), jnp.bfloat16)],
        flops=4 * sections * rows * pairs * virtuals * virtuals * slots,
        after=after,
    )


def cut_kernel(chunks, place_ref, *refs):
    total_refs, cut_refs = refs[:chunks], refs[chunks:]
    parts, _, _, wide = cut_refs[0].shape
    for e, cut_ref in enumerate(cut_refs):
        columns = pl.ds(pl.multiple_of((place_ref[0] ^ e) * wide, wide), wide)
        at = 0
        for total_ref in total_refs:
            short = total_ref.shape[1] // parts
            for part in range(parts):
                cut_ref[part, :, at : at + short] = total_ref[
                    :, part * short : (part + 1) * short, columns
                ]
            at += short


def cut(place, totals, sections, parts):
    slots, _, virtuals = totals[0].shape
    rows = sum(total.shape[1] for total in totals)
    shape = (parts, slots, rows // parts, virtuals // sections)
    return call(
        functools.partial(cut_kernel, len(totals)),
        "cut",
        place,
        totals,
        [whole(total.shape) for total in totals],
        [whole(shape)] * sections,
        [jax.ShapeDtypeStruct(shape, jnp.float32)] * sections,
        (1,),
    )


def finish_kernel(spans, groups, place_ref, *refs):
    chunks = len(spans)
    own_refs, delivered_refs = refs[:chunks], refs[chunks : chunks + len(groups)]
    out_ref, columns_ref = refs[chunks + len(groups) :]
    wide = out_ref.shape[2]
    sections = columns_ref.shape[0] // wide
    for group, delivered_ref in zip(groups, delivered_refs):
        parts = delivered_ref.shape[0] // sections
        for e in range(sections):
            base = (place_ref[0] ^ e) * wide
            for part in range(parts):
                at = 0
                for chunk in group:
                    start, rows = spans[chunk]
                    short = rows // parts
                    spot = pl.multiple_of(base + start + part * short, 8)
                    columns_ref[pl.ds(spot, short)] = delivered_ref[
                        e * parts + part, 0, at : at + short
                    ]
                    at += short
    turned = columns_ref[...].T
    for (start, rows), own_ref in zip(spans, own_refs):
        out_ref[0, 0, start : start + rows] = own_ref[0] + turned[start : start + rows]


def finish(place, spans, groups, own, delivered):
    slots, _, virtuals = own[0].shape
    wide = delivered[0].shape[-1]
    return call(
        functools.partial(finish_kernel, spans, groups),
        "finish",
        place,
        list(own) + list(delivered),
        [pl.BlockSpec((1, *x.shape[1:]), lambda s, at: (s, 0, 0)) for x in own]
        + [
            pl.BlockSpec((x.shape[0], 1, *x.shape[2:]), lambda s, at: (0, s, 0, 0))
            for x in delivered
        ],
        pl.BlockSpec((1, 1, wide, virtuals), lambda s, at: (0, s, 0, 0)),
        jax.ShapeDtypeStruct((1, slots, wide, virtuals), jnp.float32),
        (slots,),
        scratch=[pltpu.VMEM((virtuals, wide), jnp.float32)],
    )


def swap(array, axis):
    return lax.all_to_all(array, axis, split_axis=0, concat_axis=0, tiled=True)


def spread(pieces):
    count = len(pieces)
    return [pieces[0]] + [
        lax.ppermute(pieces[e], "ka", [(q, q ^ e) for q in range(count)]) for e in range(1, count)
    ]


def body(sections, amplitudes, integrals, tile_mask, pair_list):
    _, pairs, virtuals, _ = amplitudes.shape
    occupied, slots = pair_list.shape
    wide = virtuals // sections
    sizes = [wide * part // sum(CHUNKS) for part in CHUNKS]
    spans = [(sum(sizes[:at]), size) for at, size in enumerate(sizes)]
    place = lax.axis_index("ka").astype(jnp.int32).reshape(1)

    owners = jnp.arange(occupied, dtype=jnp.int32)
    partner_slot = jnp.where(pair_list[pair_list, 0] == owners[:, None], 0, 1).astype(jnp.int32)
    source_row = (pair_list * slots + partner_slot).reshape(-1)

    def fetch(chunks, after):
        start, rows = spans[chunks[0]][0], sum(sizes[at] for at in chunks)
        met = spread(
            [flip(place, amplitudes, sections, e, start, rows, after) for e in range(sections)]
        )
        return [
            functools.partial(part, place, met, spans[at][0] - start, sizes[at]) for at in chunks
        ]

    def hop(at):
        crossed = swap(across[at].reshape(occupied, sizes[at], virtuals), "ia")
        return crossed.reshape(sections, pairs, sizes[at], virtuals)

    def turn(at, crossed, after):
        pieces = scatter(place, crossed, after)
        return pieces[0], spread(pieces)

    def multiply(at, mirrored, after):
        parts = product(place, amplitudes, mirrored, masked, spans[at][0], after)
        return parts, lax.psum_scatter(parts, "ka", scatter_dimension=0, tiled=False)

    def send(group):
        return spread(cut(place, [own[at] for at in group], sections, pairs))

    def meet(columns):
        return swap(columns.reshape(occupied, slots, *columns.shape[-2:]), "ia")

    def deliver(met):
        piece = met.shape[-2:]
        routed = jnp.take(met.reshape(occupied * slots, *piece), source_row, axis=0)
        return swap(routed.reshape(occupied, slots, *piece), "ia")

    first = first_flip(place, amplitudes, sections, sizes[0])
    masked = mask_blocks(integrals, tile_mask, [first])
    across = [swap(first, "ka")]
    second, third = fetch((1, 2), [first])
    own = [None] * len(spans)
    across += [second([masked]), third([masked])]
    turned, early = turn(0, hop(0), across[1:])
    begun, own[0] = multiply(0, early, [])
    turned, middle = turn(1, hop(1), [begun])
    leading = send(GROUPS[0])
    begun, own[1] = multiply(1, middle, leading)
    crossed = hop(2)
    turned, late = turn(2, crossed, [begun])
    met = meet(gather(place, leading, [crossed]))
    _, own[2] = multiply(2, late, [begun, met])
    delivered = [deliver(met)]
    for group in GROUPS[1:]:
        met = meet(gather(place, send(group), [delivered[-1]]))
        delivered.append(deliver(met))
    return finish(place, spans, GROUPS, own, delivered)


def solution(mesh):
    placed = (
        P("ia", "ka", None, None),
        P("ia", None, "ka", None, None),
        P("ia", None, "ka", None, None),
        P(),
    )
    return jax.shard_map(
        functools.partial(body, mesh.shape["ka"]),
        mesh=mesh,
        in_specs=placed,
        out_specs=P("ia", None, "ka", None),
        check_vma=False,
    )
```

```python
import functools

import jax
import jax.numpy as jnp
from jax import lax
from jax.experimental import pallas as pl
from jax.experimental.pallas import tpu as pltpu
from jax.sharding import PartitionSpec as P

CHUNKS = (3, 3, 2)
GROUPS = ((0,), (1,), (2,))
LANES = 128
VMEM_BYTES = 48 * 1024 * 1024


def call(
    kernel, name, scalars, operands, in_specs, out_specs, out_shape, grid, scratch=(), flops=0, after=()
):
    moved = sum(x.size * x.dtype.itemsize for x in jax.tree.leaves(out_shape)) * 2
    reads = 1 + len(operands)

    def trimmed(*refs):
        kernel(*refs[:reads], *refs[reads + len(after) :])

    return pl.pallas_call(
        trimmed,
        grid_spec=pltpu.PrefetchScalarGridSpec(
            num_scalar_prefetch=1,
            grid=grid,
            in_specs=list(in_specs) + [pl.BlockSpec(memory_space=pl.ANY)] * len(after),
            out_specs=out_specs,
            scratch_shapes=list(scratch),
        ),
        out_shape=out_shape,
        compiler_params=pltpu.CompilerParams(vmem_limit_bytes=VMEM_BYTES),
        cost_estimate=pl.CostEstimate(flops=flops, bytes_accessed=moved, transcendentals=0),
        name=name,
    )(scalars, *operands, *after)


def whole(shape):
    return pl.BlockSpec(shape, lambda *_: (0,) * len(shape))


def first_flip_kernel(place_ref, blocks_ref, piece_ref):
    piece_ref[0, 0] = blocks_ref[0, 0].T[: piece_ref.shape[2]]


def first_flip(place, amplitudes, sections, rows):
    pairs, virtuals = amplitudes.shape[1], amplitudes.shape[3]
    steps = virtuals // sections // LANES
    return call(
        first_flip_kernel,
        "first_flip",
        place,
        [amplitudes],
        [pl.BlockSpec((1, 1, virtuals, LANES), lambda d, q, at: (0, d, 0, q * steps))],
        pl.BlockSpec((1, 1, rows, virtuals), lambda d, q, at: (q, d, 0, 0)),
        jax.ShapeDtypeStruct((sections, pairs, rows, virtuals), jnp.float32),
        (pairs, sections),
    )


def flip_kernel(start, place_ref, blocks_ref, piece_ref):
    piece_ref[0] = blocks_ref[0, 0].T[start : start + piece_ref.shape[1]]


def flip(place, amplitudes, sections, e, start, rows, after):
    pairs, virtuals = amplitudes.shape[1], amplitudes.shape[3]
    wide = virtuals // sections
    return call(
        functools.partial(flip_kernel, start),
        "flip",
        place,
        [amplitudes],
        [pl.BlockSpec((1, 1, virtuals, wide), lambda d, at: (0, d, 0, at[0] ^ e))],
        pl.BlockSpec((1, rows, virtuals), lambda d, at: (d, 0, 0)),
        jax.ShapeDtypeStruct((pairs, rows, virtuals), jnp.float32),
        (pairs,),
        after=after,
    )


def part_kernel(start, place_ref, *refs):
    pieces, out_ref = refs[:-1], refs[-1]
    for e, piece in enumerate(pieces):
        out_ref[place_ref[0] ^ e, 0] = piece[0, start : start + out_ref.shape[2]]


def part(place, pieces, start, size, after):
    count, (pairs, rows, virtuals) = len(pieces), pieces[0].shape
    return call(
        functools.partial(part_kernel, start),
        "part",
        place,
        pieces,
        [pl.BlockSpec((1, rows, virtuals), lambda d, at: (d, 0, 0))] * count,
        pl.BlockSpec((count, 1, size, virtuals), lambda d, at: (0, d, 0, 0)),
        jax.ShapeDtypeStruct((count, pairs, size, virtuals), jnp.float32),
        (pairs,),
        after=after,
    )


def gather_kernel(place_ref, *refs):
    pieces, out_ref = refs[:-1], refs[-1]
    for e, piece in enumerate(pieces):
        out_ref[e] = piece[...]


def gather(place, pieces, after):
    shape = (len(pieces), *pieces[0].shape)
    return call(
        gather_kernel,
        "gather",
        place,
        pieces,
        [whole(pieces[0].shape)] * len(pieces),
        whole(shape),
        jax.ShapeDtypeStruct(shape, jnp.float32),
        (1,),
        after=after,
    )


def scatter_kernel(place_ref, stacked_ref, *pieces):
    for e, piece in enumerate(pieces):
        piece[...] = stacked_ref[place_ref[0] ^ e]


def scatter(place, stacked, after):
    count, shape = stacked.shape[0], stacked.shape[1:]
    return call(
        scatter_kernel,
        "scatter",
        place,
        [stacked],
        [whole(stacked.shape)],
        [whole(shape)] * count,
        [jax.ShapeDtypeStruct(shape, jnp.float32)] * count,
        (1,),
        after=after,
    )


def mask_kernel(tiles, mask_ref, integrals_ref, masked_ref):
    side = integrals_ref.shape[-1] // tiles
    slot, pair = pl.program_id(0), pl.program_id(1)
    for r in range(tiles):
        for c in range(tiles):
            keep = mask_ref[slot, pair, r, c] != 0
            spot = (pl.ds(r * side, side), pl.ds(c * side, side))
            tile = integrals_ref[0, 0, 0, spot[0], spot[1]]
            masked_ref[0, 0, spot[0], spot[1]] = jnp.where(keep, tile, jnp.zeros_like(tile))


def mask_blocks(integrals, tile_mask, after):
    _, slots, pairs, virtuals, _ = integrals.shape
    out_shape = jax.ShapeDtypeStruct((slots, pairs, virtuals, virtuals), jnp.bfloat16)
    return call(
        functools.partial(mask_kernel, tile_mask.shape[-1]),
        "mask",
        tile_mask[0],
        [integrals],
        [pl.BlockSpec((1, 1, 1, virtuals, virtuals), lambda s, k, mask: (0, s, k, 0, 0))],
        pl.BlockSpec((1, 1, virtuals, virtuals), lambda s, k, mask: (s, k, 0, 0)),
        out_shape,
        (slots, pairs),
        after=after,
    )


def product_kernel(sections, place_ref, *refs):
    own_refs, mirrored_refs, refs = refs[:sections], refs[sections : 2 * sections], refs[2 * sections :]
    masked_ref, out_ref, split_ref = refs
    pairs, rows, _ = mirrored_refs[0].shape
    tall = sections * rows

    @pl.when((pl.program_id(0) == 0) & (pl.program_id(1) == 0))
    def _():
        for e in range(sections):
            for k in range(pairs):
                mixed = 2.0 * own_refs[e][0, k] - mirrored_refs[e][k]
                high = mixed.astype(jnp.bfloat16)
                low = (mixed - high.astype(jnp.float32)).astype(jnp.bfloat16)
                split_ref[k, pl.ds(e * rows, rows)] = high
                split_ref[k, pl.ds(tall + e * rows, rows)] = low

    total = None
    for k in range(pairs):
        both = jnp.dot(split_ref[k], masked_ref[0, k], preferred_element_type=jnp.float32)
        both = both[:tall] + both[tall:]
        total = both if total is None else total + both
    for e in range(sections):
        out_ref[place_ref[0] ^ e, 0] = total[e * rows : (e + 1) * rows]


def product(place, own, mirrored, masked, start, after):
    sections = len(mirrored)
    pairs, rows, virtuals = mirrored[0].shape
    slots = masked.shape[0]
    deep = virtuals // sections
    wide = min(virtuals, 512)
    return call(
        functools.partial(product_kernel, sections),
        "product",
        place,
        [own] * sections + list(mirrored) + [masked],
        [
            pl.BlockSpec(
                tuple(pl.Element(size) for size in (1, pairs, rows, virtuals)),
                lambda s, n, at, e=e: (0, 0, pl.multiple_of((at[0] ^ e) * deep + start, 8), 0),
            )
            for e in range(sections)
        ]
        + [whole(mirrored[0].shape)] * sections
        + [pl.BlockSpec((1, pairs, virtuals, wide), lambda s, n, at: (s, 0, 0, n))],
        pl.BlockSpec((sections, 1, rows, wide), lambda s, n, at: (0, s, 0, n)),
        jax.ShapeDtypeStruct((sections, slots, rows, virtuals), jnp.float32),
        (slots, virtuals // wide),
        scratch=[pltpu.VMEM((pairs, 2 * sections * rows, virtuals), jnp.bfloat16)],
        flops=4 * sections * rows * pairs * virtuals * virtuals * slots,
        after=after,
    )


def cut_kernel(chunks, place_ref, *refs):
    total_refs, cut_refs = refs[:chunks], refs[chunks:]
    parts, _, _, wide = cut_refs[0].shape
    for e, cut_ref in enumerate(cut_refs):
        columns = pl.ds(pl.multiple_of((place_ref[0] ^ e) * wide, wide), wide)
        at = 0
        for total_ref in total_refs:
            short = total_ref.shape[1] // parts
            for part in range(parts):
                cut_ref[part, :, at : at + short] = total_ref[
                    :, part * short : (part + 1) * short, columns
                ]
            at += short


def cut(place, totals, sections, parts):
    slots, _, virtuals = totals[0].shape
    rows = sum(total.shape[1] for total in totals)
    shape = (parts, slots, rows // parts, virtuals // sections)
    return call(
        functools.partial(cut_kernel, len(totals)),
        "cut",
        place,
        totals,
        [whole(total.shape) for total in totals],
        [whole(shape)] * sections,
        [jax.ShapeDtypeStruct(shape, jnp.float32)] * sections,
        (1,),
    )


def finish_kernel(spans, groups, place_ref, *refs):
    chunks = len(spans)
    own_refs, delivered_refs = refs[:chunks], refs[chunks : chunks + len(groups)]
    out_ref, columns_ref = refs[chunks + len(groups) :]
    wide = out_ref.shape[2]
    sections = columns_ref.shape[0] // wide
    for group, delivered_ref in zip(groups, delivered_refs):
        parts = delivered_ref.shape[0] // sections
        for e in range(sections):
            base = (place_ref[0] ^ e) * wide
            for part in range(parts):
                at = 0
                for chunk in group:
                    start, rows = spans[chunk]
                    short = rows // parts
                    spot = pl.multiple_of(base + start + part * short, 8)
                    columns_ref[pl.ds(spot, short)] = delivered_ref[
                        e * parts + part, 0, at : at + short
                    ]
                    at += short
    turned = columns_ref[...].T
    for (start, rows), own_ref in zip(spans, own_refs):
        out_ref[0, 0, start : start + rows] = own_ref[0] + turned[start : start + rows]


def finish(place, spans, groups, own, delivered):
    slots, _, virtuals = own[0].shape
    wide = delivered[0].shape[-1]
    return call(
        functools.partial(finish_kernel, spans, groups),
        "finish",
        place,
        list(own) + list(delivered),
        [pl.BlockSpec((1, *x.shape[1:]), lambda s, at: (s, 0, 0)) for x in own]
        + [
            pl.BlockSpec((x.shape[0], 1, *x.shape[2:]), lambda s, at: (0, s, 0, 0))
            for x in delivered
        ],
        pl.BlockSpec((1, 1, wide, virtuals), lambda s, at: (0, s, 0, 0)),
        jax.ShapeDtypeStruct((1, slots, wide, virtuals), jnp.float32),
        (slots,),
        scratch=[pltpu.VMEM((virtuals, wide), jnp.float32)],
    )


def swap(array, axis):
    return lax.all_to_all(array, axis, split_axis=0, concat_axis=0, tiled=True)


def spread(pieces):
    count = len(pieces)
    return [pieces[0]] + [
        lax.ppermute(pieces[e], "ka", [(q, q ^ e) for q in range(count)]) for e in range(1, count)
    ]


def body(sections, amplitudes, integrals, tile_mask, pair_list):
    _, pairs, virtuals, _ = amplitudes.shape
    occupied, slots = pair_list.shape
    wide = virtuals // sections
    sizes = [wide * part // sum(CHUNKS) for part in CHUNKS]
    spans = [(sum(sizes[:at]), size) for at, size in enumerate(sizes)]
    place = lax.axis_index("ka").astype(jnp.int32).reshape(1)

    owners = jnp.arange(occupied, dtype=jnp.int32)
    partner_slot = jnp.where(pair_list[pair_list, 0] == owners[:, None], 0, 1).astype(jnp.int32)
    source_row = (pair_list * slots + partner_slot).reshape(-1)

    def fetch(chunks, after):
        start, rows = spans[chunks[0]][0], sum(sizes[at] for at in chunks)
        met = spread(
            [flip(place, amplitudes, sections, e, start, rows, after) for e in range(sections)]
        )
        return [
            functools.partial(part, place, met, spans[at][0] - start, sizes[at]) for at in chunks
        ]

    def hop(at):
        crossed = swap(across[at].reshape(occupied, sizes[at], virtuals), "ia")
        return crossed.reshape(sections, pairs, sizes[at], virtuals)

    def turn(at, crossed, after):
        pieces = scatter(place, crossed, after)
        return pieces[0], spread(pieces)

    def multiply(at, mirrored, after):
        parts = product(place, amplitudes, mirrored, masked, spans[at][0], after)
        return parts, lax.psum_scatter(parts, "ka", scatter_dimension=0, tiled=False)

    def columns_of(group):
        return cut(place, [own[at] for at in group], sections, pairs)

    def meet(columns):
        return swap(columns.reshape(occupied, slots, *columns.shape[-2:]), "ia")

    def deliver(met):
        piece = met.shape[-2:]
        routed = jnp.take(met.reshape(occupied * slots, *piece), source_row, axis=0)
        return swap(routed.reshape(occupied, slots, *piece), "ia")

    first = first_flip(place, amplitudes, sections, sizes[0])
    masked = mask_blocks(integrals, tile_mask, [first])
    across = [swap(first, "ka")]
    second, third = fetch((1, 2), [first])
    own = [None] * len(spans)
    across += [second([masked]), third([masked])]
    turned, early = turn(0, hop(0), across[1:])
    begun, own[0] = multiply(0, early, [])
    turned, middle = turn(1, hop(1), [begun])
    leading = columns_of(GROUPS[0])
    crossed = hop(2)
    turned, late = turn(2, crossed, [turned, leading[0]])
    begun, own[1] = multiply(1, middle, [turned])
    met = meet(gather(place, spread(leading), [crossed]))
    _, own[2] = multiply(2, late, [begun, met])
    delivered = [deliver(met)]
    for group in GROUPS[1:]:
        met = meet(gather(place, spread(columns_of(group)), [delivered[-1]]))
        delivered.append(deliver(met))
    return finish(place, spans, GROUPS, own, delivered)


def solution(mesh):
    placed = (
        P("ia", "ka", None, None),
        P("ia", None, "ka", None, None),
        P("ia", None, "ka", None, None),
        P(),
    )
    return jax.shard_map(
        functools.partial(body, mesh.shape["ka"]),
        mesh=mesh,
        in_specs=placed,
        out_specs=P("ia", None, "ka", None),
        check_vma=False,
    )
```

```python
import functools

import jax
import jax.numpy as jnp
from jax import lax
from jax.experimental import pallas as pl
from jax.experimental.pallas import tpu as pltpu
from jax.sharding import PartitionSpec as P

CHUNKS = (3, 3, 2)
GROUPS = ((0,), (1,), (2,))
LANES = 128
VMEM_BYTES = 48 * 1024 * 1024


def call(
    kernel, name, scalars, operands, in_specs, out_specs, out_shape, grid, scratch=(), flops=0, after=()
):
    moved = sum(x.size * x.dtype.itemsize for x in jax.tree.leaves(out_shape)) * 2
    reads = 1 + len(operands)

    def trimmed(*refs):
        kernel(*refs[:reads], *refs[reads + len(after) :])

    return pl.pallas_call(
        trimmed,
        grid_spec=pltpu.PrefetchScalarGridSpec(
            num_scalar_prefetch=1,
            grid=grid,
            in_specs=list(in_specs) + [pl.BlockSpec(memory_space=pl.ANY)] * len(after),
            out_specs=out_specs,
            scratch_shapes=list(scratch),
        ),
        out_shape=out_shape,
        compiler_params=pltpu.CompilerParams(vmem_limit_bytes=VMEM_BYTES),
        cost_estimate=pl.CostEstimate(flops=flops, bytes_accessed=moved, transcendentals=0),
        name=name,
    )(scalars, *operands, *after)


def whole(shape):
    return pl.BlockSpec(shape, lambda *_: (0,) * len(shape))


def first_flip_kernel(place_ref, blocks_ref, piece_ref):
    piece_ref[0, 0] = blocks_ref[0, 0].T[: piece_ref.shape[2]]


def first_flip(place, amplitudes, sections, rows):
    pairs, virtuals = amplitudes.shape[1], amplitudes.shape[3]
    steps = virtuals // sections // LANES
    return call(
        first_flip_kernel,
        "first_flip",
        place,
        [amplitudes],
        [pl.BlockSpec((1, 1, virtuals, LANES), lambda d, q, at: (0, d, 0, q * steps))],
        pl.BlockSpec((1, 1, rows, virtuals), lambda d, q, at: (q, d, 0, 0)),
        jax.ShapeDtypeStruct((sections, pairs, rows, virtuals), jnp.float32),
        (pairs, sections),
    )


def flip_kernel(start, place_ref, blocks_ref, piece_ref):
    piece_ref[0] = blocks_ref[0, 0].T[start : start + piece_ref.shape[1]]


def flip(place, amplitudes, sections, e, start, rows, after):
    pairs, virtuals = amplitudes.shape[1], amplitudes.shape[3]
    wide = virtuals // sections
    return call(
        functools.partial(flip_kernel, start),
        "flip",
        place,
        [amplitudes],
        [pl.BlockSpec((1, 1, virtuals, wide), lambda d, at: (0, d, 0, at[0] ^ e))],
        pl.BlockSpec((1, rows, virtuals), lambda d, at: (d, 0, 0)),
        jax.ShapeDtypeStruct((pairs, rows, virtuals), jnp.float32),
        (pairs,),
        after=after,
    )


def part_kernel(start, place_ref, *refs):
    pieces, out_ref = refs[:-1], refs[-1]
    for e, piece in enumerate(pieces):
        out_ref[place_ref[0] ^ e, 0] = piece[0, start : start + out_ref.shape[2]]


def part(place, pieces, start, size, after):
    count, (pairs, rows, virtuals) = len(pieces), pieces[0].shape
    return call(
        functools.partial(part_kernel, start),
        "part",
        place,
        pieces,
        [pl.BlockSpec((1, rows, virtuals), lambda d, at: (d, 0, 0))] * count,
        pl.BlockSpec((count, 1, size, virtuals), lambda d, at: (0, d, 0, 0)),
        jax.ShapeDtypeStruct((count, pairs, size, virtuals), jnp.float32),
        (pairs,),
        after=after,
    )


def gather_kernel(place_ref, *refs):
    pieces, out_ref = refs[:-1], refs[-1]
    for e, piece in enumerate(pieces):
        out_ref[e] = piece[...]


def gather(place, pieces, after):
    shape = (len(pieces), *pieces[0].shape)
    return call(
        gather_kernel,
        "gather",
        place,
        pieces,
        [whole(pieces[0].shape)] * len(pieces),
        whole(shape),
        jax.ShapeDtypeStruct(shape, jnp.float32),
        (1,),
        after=after,
    )


def scatter_kernel(place_ref, stacked_ref, *pieces):
    for e, piece in enumerate(pieces):
        piece[...] = stacked_ref[place_ref[0] ^ e]


def scatter(place, stacked, after):
    count, shape = stacked.shape[0], stacked.shape[1:]
    return call(
        scatter_kernel,
        "scatter",
        place,
        [stacked],
        [whole(stacked.shape)],
        [whole(shape)] * count,
        [jax.ShapeDtypeStruct(shape, jnp.float32)] * count,
        (1,),
        after=after,
    )


def mask_kernel(tiles, mask_ref, integrals_ref, masked_ref):
    side = integrals_ref.shape[-1] // tiles
    slot, pair = pl.program_id(0), pl.program_id(1)
    for r in range(tiles):
        for c in range(tiles):
            keep = mask_ref[slot, pair, r, c] != 0
            spot = (pl.ds(r * side, side), pl.ds(c * side, side))
            tile = integrals_ref[0, 0, 0, spot[0], spot[1]]
            masked_ref[0, 0, spot[0], spot[1]] = jnp.where(keep, tile, jnp.zeros_like(tile))


def mask_blocks(integrals, tile_mask, after):
    _, slots, pairs, virtuals, _ = integrals.shape
    out_shape = jax.ShapeDtypeStruct((slots, pairs, virtuals, virtuals), jnp.bfloat16)
    return call(
        functools.partial(mask_kernel, tile_mask.shape[-1]),
        "mask",
        tile_mask[0],
        [integrals],
        [pl.BlockSpec((1, 1, 1, virtuals, virtuals), lambda s, k, mask: (0, s, k, 0, 0))],
        pl.BlockSpec((1, 1, virtuals, virtuals), lambda s, k, mask: (s, k, 0, 0)),
        out_shape,
        (slots, pairs),
        after=after,
    )


def product_kernel(sections, place_ref, *refs):
    own_refs, mirrored_refs, refs = refs[:sections], refs[sections : 2 * sections], refs[2 * sections :]
    masked_ref, out_ref, split_ref = refs
    pairs, rows, _ = mirrored_refs[0].shape
    tall = sections * rows

    @pl.when((pl.program_id(0) == 0) & (pl.program_id(1) == 0))
    def _():
        for e in range(sections):
            for k in range(pairs):
                mixed = 2.0 * own_refs[e][0, k] - mirrored_refs[e][k]
                high = mixed.astype(jnp.bfloat16)
                low = (mixed - high.astype(jnp.float32)).astype(jnp.bfloat16)
                split_ref[k, pl.ds(e * rows, rows)] = high
                split_ref[k, pl.ds(tall + e * rows, rows)] = low

    total = None
    for k in range(pairs):
        both = jnp.dot(split_ref[k], masked_ref[0, k], preferred_element_type=jnp.float32)
        both = both[:tall] + both[tall:]
        total = both if total is None else total + both
    for e in range(sections):
        out_ref[place_ref[0] ^ e, 0] = total[e * rows : (e + 1) * rows]


def product(place, own, mirrored, masked, start, after):
    sections = len(mirrored)
    pairs, rows, virtuals = mirrored[0].shape
    slots = masked.shape[0]
    deep = virtuals // sections
    wide = min(virtuals, 512)
    return call(
        functools.partial(product_kernel, sections),
        "product",
        place,
        [own] * sections + list(mirrored) + [masked],
        [
            pl.BlockSpec(
                tuple(pl.Element(size) for size in (1, pairs, rows, virtuals)),
                lambda s, n, at, e=e: (0, 0, pl.multiple_of((at[0] ^ e) * deep + start, 8), 0),
            )
            for e in range(sections)
        ]
        + [whole(mirrored[0].shape)] * sections
        + [pl.BlockSpec((1, pairs, virtuals, wide), lambda s, n, at: (s, 0, 0, n))],
        pl.BlockSpec((sections, 1, rows, wide), lambda s, n, at: (0, s, 0, n)),
        jax.ShapeDtypeStruct((sections, slots, rows, virtuals), jnp.float32),
        (slots, virtuals // wide),
        scratch=[pltpu.VMEM((pairs, 2 * sections * rows, virtuals), jnp.bfloat16)],
        flops=4 * sections * rows * pairs * virtuals * virtuals * slots,
        after=after,
    )


def cut_kernel(chunks, place_ref, *refs):
    total_refs, cut_refs = refs[:chunks], refs[chunks:]
    parts, _, _, wide = cut_refs[0].shape
    for e, cut_ref in enumerate(cut_refs):
        columns = pl.ds(pl.multiple_of((place_ref[0] ^ e) * wide, wide), wide)
        at = 0
        for total_ref in total_refs:
            short = total_ref.shape[1] // parts
            for part in range(parts):
                cut_ref[part, :, at : at + short] = total_ref[
                    :, part * short : (part + 1) * short, columns
                ]
            at += short


def cut(place, totals, sections, parts):
    slots, _, virtuals = totals[0].shape
    rows = sum(total.shape[1] for total in totals)
    shape = (parts, slots, rows // parts, virtuals // sections)
    return call(
        functools.partial(cut_kernel, len(totals)),
        "cut",
        place,
        totals,
        [whole(total.shape) for total in totals],
        [whole(shape)] * sections,
        [jax.ShapeDtypeStruct(shape, jnp.float32)] * sections,
        (1,),
    )


def finish_kernel(spans, groups, place_ref, *refs):
    chunks = len(spans)
    own_refs, delivered_refs = refs[:chunks], refs[chunks : chunks + len(groups)]
    out_ref, columns_ref = refs[chunks + len(groups) :]
    wide = out_ref.shape[2]
    sections = columns_ref.shape[0] // wide
    for group, delivered_ref in zip(groups, delivered_refs):
        parts = delivered_ref.shape[0] // sections
        for e in range(sections):
            base = (place_ref[0] ^ e) * wide
            for part in range(parts):
                at = 0
                for chunk in group:
                    start, rows = spans[chunk]
                    short = rows // parts
                    spot = pl.multiple_of(base + start + part * short, 8)
                    columns_ref[pl.ds(spot, short)] = delivered_ref[
                        e * parts + part, 0, at : at + short
                    ]
                    at += short
    turned = columns_ref[...].T
    for (start, rows), own_ref in zip(spans, own_refs):
        out_ref[0, 0, start : start + rows] = own_ref[0] + turned[start : start + rows]


def finish(place, spans, groups, own, delivered):
    slots, _, virtuals = own[0].shape
    wide = delivered[0].shape[-1]
    return call(
        functools.partial(finish_kernel, spans, groups),
        "finish",
        place,
        list(own) + list(delivered),
        [pl.BlockSpec((1, *x.shape[1:]), lambda s, at: (s, 0, 0)) for x in own]
        + [
            pl.BlockSpec((x.shape[0], 1, *x.shape[2:]), lambda s, at: (0, s, 0, 0))
            for x in delivered
        ],
        pl.BlockSpec((1, 1, wide, virtuals), lambda s, at: (0, s, 0, 0)),
        jax.ShapeDtypeStruct((1, slots, wide, virtuals), jnp.float32),
        (slots,),
        scratch=[pltpu.VMEM((virtuals, wide), jnp.float32)],
    )


def swap(array, axis):
    return lax.all_to_all(array, axis, split_axis=0, concat_axis=0, tiled=True)


def spread(pieces):
    count = len(pieces)
    return [pieces[0]] + [
        lax.ppermute(pieces[e], "ka", [(q, q ^ e) for q in range(count)]) for e in range(1, count)
    ]


def body(sections, amplitudes, integrals, tile_mask, pair_list):
    _, pairs, virtuals, _ = amplitudes.shape
    occupied, slots = pair_list.shape
    wide = virtuals // sections
    sizes = [wide * part // sum(CHUNKS) for part in CHUNKS]
    spans = [(sum(sizes[:at]), size) for at, size in enumerate(sizes)]
    place = lax.axis_index("ka").astype(jnp.int32).reshape(1)

    owners = jnp.arange(occupied, dtype=jnp.int32)
    partner_slot = jnp.where(pair_list[pair_list, 0] == owners[:, None], 0, 1).astype(jnp.int32)
    source_row = (pair_list * slots + partner_slot).reshape(-1)

    def fetch(chunks, after):
        start, rows = spans[chunks[0]][0], sum(sizes[at] for at in chunks)
        met = spread(
            [flip(place, amplitudes, sections, e, start, rows, after) for e in range(sections)]
        )
        return [
            functools.partial(part, place, met, spans[at][0] - start, sizes[at]) for at in chunks
        ]

    def hop(at):
        crossed = swap(across[at].reshape(occupied, sizes[at], virtuals), "ia")
        return crossed.reshape(sections, pairs, sizes[at], virtuals)

    def turn(at, crossed, after):
        pieces = scatter(place, crossed, after)
        return pieces[0], spread(pieces)

    def multiply(at, mirrored, after):
        parts = product(place, amplitudes, mirrored, masked, spans[at][0], after)
        return parts, lax.psum_scatter(parts, "ka", scatter_dimension=0, tiled=False)

    def columns_of(group):
        return cut(place, [own[at] for at in group], sections, pairs)

    def meet(columns):
        return swap(columns.reshape(occupied, slots, *columns.shape[-2:]), "ia")

    def deliver(met):
        piece = met.shape[-2:]
        routed = jnp.take(met.reshape(occupied * slots, *piece), source_row, axis=0)
        return swap(routed.reshape(occupied, slots, *piece), "ia")

    first = first_flip(place, amplitudes, sections, sizes[0])
    masked = mask_blocks(integrals, tile_mask, [first])
    across = [swap(first, "ka")]
    second, third = fetch((1, 2), [first])
    own = [None] * len(spans)
    across += [second([masked]), third([masked])]
    turned, early = turn(0, hop(0), across[1:])
    begun, own[0] = multiply(0, early, [])
    turned, middle = turn(1, hop(1), [begun])
    leading = columns_of(GROUPS[0])
    crossed = hop(2)
    turned, late = turn(2, crossed, [turned, leading[0]])
    begun, own[1] = multiply(1, middle, [turned])
    met = meet(gather(place, spread(leading), [crossed]))
    _, own[2] = multiply(2, late, [begun])
    delivered = [deliver(met)]
    for group in GROUPS[1:]:
        met = meet(gather(place, spread(columns_of(group)), [delivered[-1]]))
        delivered.append(deliver(met))
    return finish(place, spans, GROUPS, own, delivered)


def solution(mesh):
    placed = (
        P("ia", "ka", None, None),
        P("ia", None, "ka", None, None),
        P("ia", None, "ka", None, None),
        P(),
    )
    return jax.shard_map(
        functools.partial(body, mesh.shape["ka"]),
        mesh=mesh,
        in_specs=placed,
        out_specs=P("ia", None, "ka", None),
        check_vma=False,
    )
```
